128 devices in a mesh: dp: 16 (over z, x), row: 2 (over y_hi), col: 4 (over y_lo, core).
Axes of the slice: x: 4, y: 4 (y_hi: 2, y_lo: 2; y = y_hi * 2 + y_lo), z: 4, core: 2. Of those that a mesh axis runs over, the one named last changes fastest.
Arguments:
- hidden: bfloat16 [16384, 1408], P('dp', ('col', 'row')), may hold values from -6 to 6
- skipped: bfloat16 [16384, 1408], P('dp', ('col', 'row')), may hold values from -6 to 6
- text: bfloat16 [16, 333, 1024], P('dp', None, ('row', 'col')), may hold values from -6 to 6
- teacher: bfloat16 [16384, 1408], P('dp', ('row', 'col')), may hold values from -6 to 6
- valid: int32 [16384], P('dp'), may hold values from 0 to 1, as said below
- steps: int32 [16], P('dp'), may hold values from 0 to 999
- positions: int32 [2, 16384], P(None, 'dp'), may hold values from 0 to 63, as said below
- w_skip: bfloat16 [2, 1408, 1408], P(None, 'col', 'row'), may hold values from -0.109375 to 0.109375
- g_skip: float32 [2, 1408], P(None, ('col', 'row')), may hold values from 0.5 to 1.5
- b_skip: float32 [2, 1408], P(None, ('col', 'row')), may hold values from -2 to 2
- w_mod: bfloat16 [256, 1408], P('col', 'row'), may hold values from -0.5 to 0.5
- g_one: float32 [1408], P(('row', 'col')), may hold values from 0.5 to 1.5
- b_one: float32 [1408], P(('row', 'col')), may hold values from -2 to 2
- w_qkv: bfloat16 [1408, 4224], P('row', 'col'), may hold values from -0.15625 to 0.15625
- g_query: float32 [88], replicated, may hold values from 0.25 to 1.75
- g_key: float32 [88], replicated, may hold values from 0.25 to 1.75
- w_out: bfloat16 [1408, 1408], P('col', 'row'), may hold values from -1.25 to 1.25
- g_three: float32 [1408], P(('row', 'col')), may hold values from 0.5 to 1.5
- b_three: float32 [1408], P(('row', 'col')), may hold values from -2 to 2
- w_cquery: bfloat16 [1408, 1408], P('row', 'col'), may hold values from -0.15625 to 0.15625
- w_ckv: bfloat16 [1024, 2816], P('row', 'col'), may hold values from -0.1875 to 0.1875
- g_cquery: float32 [88], replicated, may hold values from 0.25 to 1.75
- g_ckey: float32 [88], replicated, may hold values from 0.25 to 1.75
- w_cout: bfloat16 [1408, 1408], P('col', 'row'), may hold values from -1.25 to 1.25
- g_two: float32 [1408], P(('row', 'col')), may hold values from 0.5 to 1.5
- b_two: float32 [1408], P(('row', 'col')), may hold values from -2 to 2
- w_up: bfloat16 [1408, 6144], P('row', 'col'), may hold values from -0.15625 to 0.15625
- w_down: bfloat16 [6144, 1408], P('col', 'row'), may hold values from -0.078125 to 0.078125
Outputs:
- output: float32 [16384, 1408], P('dp', ('row', 'col'))
- d_hidden: float32 [16384, 1408], P('dp', ('col', 'row'))
- d_skipped: float32 [16384, 1408], P('dp', ('col', 'row'))
- d_w_skip: float32 [2, 1408, 1408], P(None, 'col', 'row')
- d_g_skip: float32 [2, 1408], P(None, ('col', 'row'))
- d_b_skip: float32 [2, 1408], P(None, ('col', 'row'))
- d_w_mod: float32 [256, 1408], P('col', 'row')
- d_g_one: float32 [1408], P(('row', 'col'))
- d_b_one: float32 [1408], P(('row', 'col'))
- d_w_qkv: float32 [1408, 4224], P('row', 'col')
- d_g_query: float32 [88], replicated
- d_g_key: float32 [88], replicated
- d_w_out: float32 [1408, 1408], P('col', 'row')
- d_g_three: float32 [1408], P(('row', 'col'))
- d_b_three: float32 [1408], P(('row', 'col'))
- d_w_cquery: float32 [1408, 1408], P('row', 'col')
- d_w_ckv: float32 [1024, 2816], P('row', 'col')
- d_g_cquery: float32 [88], replicated
- d_g_ckey: float32 [88], replicated
- d_w_cout: float32 [1408, 1408], P('col', 'row')
- d_g_two: float32 [1408], P(('row', 'col'))
- d_b_two: float32 [1408], P(('row', 'col'))
- d_w_up: float32 [1408, 6144], P('row', 'col')
- d_w_down: float32 [6144, 1408], P('col', 'row')
- loss: float32 [], replicated
The draws below stay inside these ranges and needn't reach their ends.
Inputs may be any that keep to these rules, and one draw needn't show every extreme that they name: Token 0 of every latent is valid. The 1024 tokens of each latent lie in row-major order on a grid of h rows and 1024/h columns, h one of 16, 32 and 64; positions[0] is the row, positions[1] the column.
All inputs are finite; a program needn't handle non-finite values.
Results may differ from the reference program's by a relative error of at most 0.019.
Values may be sent and summed in bfloat16 or wider, within the bound.
No kernel may reach another device: no remote copies, remote signals or barrier semaphores. Data moves between devices by JAX's collectives and lax.ppermute only.
A program may use at most 192 MiB of HBM per device.

```python
import math
import jax
import jax.numpy as jnp
from jax import lax

D = 1408
HEADS = 16
HD = 88
FF = 6144
TD = 1024
FREQ = 256
TXT = 333
SIDE = 32
SEQ = 1024
LATENTS = 16
TOKENS = 16384


def draw_valid(key, part):
    key = jax.random.fold_in(key, 11)
    place = jnp.arange(LATENTS * SEQ, dtype=jnp.int32)
    latent = place // SEQ
    cutoff = 300 + 650 * latent // (LATENTS - 1)
    ticket = jax.random.randint(key, (LATENTS * SEQ,), 0, 1000)
    first = place % SEQ == 0
    return jnp.where(first | (ticket < cutoff), 1, 0).astype(jnp.int32)


def draw_positions(key, part):
    key = jax.random.fold_in(key, 23)
    pick = jax.random.randint(key, (LATENTS, 1), 0, 3)
    height = jnp.where(pick == 0, SIDE // 2, jnp.where(pick == 1, SIDE, 2 * SIDE)).astype(jnp.int32)
    across = (SEQ // height).astype(jnp.int32)
    place = jnp.arange(SEQ, dtype=jnp.int32)[None, :]
    rows_at = place // across
    cols_at = place % across
    return jnp.stack([rows_at.reshape(-1), cols_at.reshape(-1)]).astype(jnp.int32)


def touch_ends(values, own_key, low, high):
    index_at = [jax.random.randint(jax.random.fold_in(own_key, axis), (), 0, length) for axis, length in enumerate(values.shape)]
    main_axis = values.shape.index(max(values.shape))
    next_to = index_at[:main_axis] + [(index_at[main_axis] + 1) % values.shape[main_axis]] + index_at[main_axis + 1:]
    return values.at[tuple(index_at)].set(low).at[tuple(next_to)].set(high)


def block_levels(rng, extent, cuts, smallest, high):
    def one(axis_at, blocks):
        draws = jax.random.uniform(jax.random.fold_in(jax.random.fold_in(rng, 6), axis_at), (blocks,), jnp.float32, smallest / len(cuts), high / len(cuts))
        return jnp.repeat(jnp.exp(draws), extent[axis_at] // blocks).reshape((-1,) + (1,) * (len(extent) - axis_at - 1))

    level = one(*cuts[0])
    for cut in cuts[1:]:
        level = level * one(*cut)
    return level


def scatter_about(key, shape, scale, reach, cuts=(), kind=jnp.bfloat16):
    level = block_levels(key, shape, cuts, -0.22, 0.18) if cuts else 1.0
    drawn = jax.random.normal(key, shape, jnp.float32) * scale * level
    return jnp.minimum(jnp.maximum(drawn, -reach), reach).astype(kind)


def setup_inputs(seed: int = 0) -> dict:
    splits = jax.random.split(jax.random.key(seed), 29)
    return {
        "hidden": scatter_about(splits[0], (TOKENS, D), 1.0, 6.0, ((0, 16), (1, 8))),
        "skipped": scatter_about(splits[1], (TOKENS, D), 1.0, 6.0, ((0, 16), (1, 8))),
        "text": scatter_about(splits[2], (LATENTS, TXT, TD), 1.0, 6.0, ((0, 16), (2, 8))),
        "teacher": scatter_about(splits[3], (TOKENS, D), 1.0, 6.0, ((0, 16), (1, 8))),
        "valid": draw_valid(jax.random.fold_in(splits[28], 71), 0),
        "steps": touch_ends(jax.random.randint(splits[5], (LATENTS,), 0, 1000), jax.random.fold_in(splits[5], 1), 0, 999).astype(jnp.int32),
        "positions": draw_positions(jax.random.fold_in(splits[28], 71), 0),
        "w_skip": scatter_about(splits[7], (2, D, D), (2 * D) ** -0.5, 0.109375, ((1, 4), (2, 2))),
        "g_skip": jnp.clip(1.0 + 0.1 * jax.random.normal(splits[8], (2, D), jnp.float32), 0.5, 1.5),
        "b_skip": scatter_about(splits[9], (2, D), 0.3, 2.0, ((1, 8),), jnp.float32),
        "w_mod": scatter_about(splits[10], (FREQ, D), (FREQ // 2) ** -0.5, 0.5, ((0, 4), (1, 2))),
        "g_one": jnp.clip(1.0 + 0.1 * jax.random.normal(splits[11], (D,), jnp.float32), 0.5, 1.5),
        "b_one": scatter_about(splits[12], (D,), 0.3, 2.0, ((0, 8),), jnp.float32),
        "w_qkv": scatter_about(splits[13], (D, 3 * D), D ** -0.5, 0.15625, ((0, 2), (1, 4))),
        "g_query": jnp.clip(1.0 + 0.15 * jax.random.normal(splits[14], (HD,), jnp.float32), 0.25, 1.75),
        "g_key": jnp.clip(1.0 + 0.15 * jax.random.normal(splits[15], (HD,), jnp.float32), 0.25, 1.75),
        "w_out": scatter_about(splits[16], (D, D), (HD // 4) ** -0.5, 1.25, ((0, 4), (1, 2))),
        "g_three": jnp.clip(1.0 + 0.1 * jax.random.normal(splits[17], (D,), jnp.float32), 0.5, 1.5),
        "b_three": scatter_about(splits[18], (D,), 0.3, 2.0, ((0, 8),), jnp.float32),
        "w_cquery": scatter_about(splits[19], (D, D), D ** -0.5, 0.15625, ((0, 2), (1, 4))),
        "w_ckv": scatter_about(splits[20], (TD, 2 * D), TD ** -0.5, 0.1875, ((0, 2), (1, 4))),
        "g_cquery": jnp.clip(1.0 + 0.15 * jax.random.normal(splits[21], (HD,), jnp.float32), 0.25, 1.75),
        "g_ckey": jnp.clip(1.0 + 0.15 * jax.random.normal(splits[22], (HD,), jnp.float32), 0.25, 1.75),
        "w_cout": scatter_about(splits[23], (D, D), (HD // 4) ** -0.5, 1.25, ((0, 4), (1, 2))),
        "g_two": jnp.clip(1.0 + 0.1 * jax.random.normal(splits[24], (D,), jnp.float32), 0.5, 1.5),
        "b_two": scatter_about(splits[25], (D,), 0.3, 2.0, ((0, 8),), jnp.float32),
        "w_up": scatter_about(splits[26], (D, FF), D ** -0.5, 0.15625, ((0, 2), (1, 4))),
        "w_down": scatter_about(splits[27], (FF, D), FF ** -0.5, 0.078125, ((0, 4), (1, 2))),
    }


@jax.custom_vjp
def low(v):
    return lax.optimization_barrier(v.astype(jnp.bfloat16)).astype(jnp.float32)

@jax.custom_vjp
def low_back(v):
    return v

def low_keep(v):
    return (low(v), None)

def low_pass(kept, grad):
    return (grad,)

def back_keep(v):
    return (v, None)

def back_low(kept, grad):
    return (low(grad),)
low.defvjp(low_keep, low_pass)
low_back.defvjp(back_keep, back_low)
precise = lax.Precision.HIGHEST
epsilon = 1e-06

def matmul(left, right):
    return jnp.dot(left, right, precision=precise)

def layer_norm(values, gain, offset):
    mean = lax.optimization_barrier(jnp.mean(values, axis=-1, keepdims=True))
    spread = lax.optimization_barrier(jnp.mean(values * values, axis=-1, keepdims=True)) - mean * mean
    return (values - mean) * lax.rsqrt(spread + epsilon) * gain + offset

def head_norm(values, gain):
    mean = lax.optimization_barrier(jnp.mean(values, axis=-1, keepdims=True))
    spread = lax.optimization_barrier(jnp.mean(values * values, axis=-1, keepdims=True)) - mean * mean
    return (values - mean) * lax.rsqrt(spread + epsilon) * gain

def rotate(values):
    quarter = values.shape[-1] // 4
    return jnp.concatenate([-values[..., quarter:2 * quarter], values[..., :quarter], -values[..., 3 * quarter:], values[..., 2 * quarter:3 * quarter]], axis=-1)

def qk_prep(raw, gain, cosine, sine):
    normal = head_norm(raw, gain)
    return normal * cosine + rotate(normal) * sine

def rope_tables(positions):
    quarter = HD // 4
    freqs = jnp.exp(-math.log(10000.0) * jnp.arange(quarter, dtype=jnp.float32) / quarter)
    rows_angle = positions[0].astype(jnp.float32)[:, None] * freqs[None, :]
    cols_angle = positions[1].astype(jnp.float32)[:, None] * freqs[None, :]
    cosine = jnp.concatenate([jnp.cos(rows_angle), jnp.cos(rows_angle), jnp.cos(cols_angle), jnp.cos(cols_angle)], axis=1)
    sine = jnp.concatenate([jnp.sin(rows_angle), jnp.sin(rows_angle), jnp.sin(cols_angle), jnp.sin(cols_angle)], axis=1)
    return (cosine, sine)

def time_embed(steps):
    half = FREQ // 2
    freqs = jnp.exp(-math.log(10000.0) * jnp.arange(half, dtype=jnp.float32) / half)
    angles = steps.astype(jnp.float32)[:, None] * freqs[None, :]
    return jnp.concatenate([jnp.cos(angles), jnp.sin(angles)], axis=1)

def softmax_rows(scores):
    top = lax.optimization_barrier(jnp.max(scores, axis=-1, keepdims=True))
    expo = jnp.exp(scores - top)
    return expo / lax.optimization_barrier(jnp.sum(expo, axis=-1, keepdims=True))

def attend(query, keys, values):
    scale = HD ** (-0.5)
    block = min(512, query.shape[0])

    def one_block(piece):
        scores = low_back(scale * jnp.einsum('qhd,khd->hqk', piece, keys, precision=precise))
        weights = low(softmax_rows(scores))
        return jnp.einsum('hqk,khd->qhd', weights, values, precision=precise)
    pieces = query.reshape(query.shape[0] // block, block, query.shape[1], query.shape[2])
    return lax.map(jax.checkpoint(one_block), pieces).reshape(query.shape)

def attend_triple(triple):
    return attend(triple[0], triple[1], triple[2])

def layer(params, hidden, skipped, text, emb, cosine, sine):
    w_skip, g_skip, b_skip, w_mod, g_one, b_one, w_qkv, g_query, g_key, w_out, g_three, b_three, w_cquery, w_ckv, g_cquery, g_ckey, w_cout, g_two, b_two, w_up, w_down = params
    rows = hidden.shape[0]
    groups = rows // SEQ
    joined = jnp.concatenate([hidden, skipped], axis=1)
    normed = low(layer_norm(joined, g_skip.reshape(2 * D), b_skip.reshape(2 * D)))
    stream = low_back(matmul(normed, w_skip.reshape(2 * D, D)))
    shift = low_back(matmul(low(emb), w_mod))
    inputs_one = low(layer_norm(stream, g_one, b_one) + jnp.repeat(shift, SEQ, axis=0))
    packed = low_back(matmul(inputs_one, w_qkv)).reshape(rows, HEADS, 3, HD)
    cos_three = cosine[:, None, :]
    sin_three = sine[:, None, :]
    query = low(qk_prep(packed[:, :, 0], g_query, cos_three, sin_three))
    keys = low(qk_prep(packed[:, :, 1], g_key, cos_three, sin_three))
    values = low(packed[:, :, 2])
    shape_four = (groups, SEQ, HEADS, HD)
    mixed = lax.map(attend_triple, (query.reshape(shape_four), keys.reshape(shape_four), values.reshape(shape_four)))
    mixed = low(low_back(mixed.reshape(rows, D)))
    stream = stream + low_back(matmul(mixed, w_out))
    inputs_three = low(layer_norm(stream, g_three, b_three))
    craw = low_back(matmul(inputs_three, w_cquery)).reshape(rows, HEADS, HD)
    cquery = low(qk_prep(craw, g_cquery, cos_three, sin_three))
    ckv = low_back(matmul(text.reshape(groups * TXT, TD), w_ckv)).reshape(groups, TXT, HEADS, 2, HD)
    ckeys = low(head_norm(ckv[:, :, :, 0], g_ckey))
    cvalues = low(ckv[:, :, :, 1])
    cmixed = lax.map(attend_triple, (cquery.reshape(shape_four), ckeys, cvalues))
    cmixed = low(low_back(cmixed.reshape(rows, D)))
    stream = stream + low_back(matmul(cmixed, w_cout))
    inputs_two = low(layer_norm(stream, g_two, b_two))
    upper = low_back(matmul(inputs_two, w_up))
    active = low(jax.nn.gelu(upper, approximate=True))
    return stream + low_back(matmul(active, w_down))

def reference(hidden, skipped, text, teacher, valid, steps, positions, w_skip, g_skip, b_skip, w_mod, g_one, b_one, w_qkv, g_query, g_key, w_out, g_three, b_three, w_cquery, w_ckv, g_cquery, g_ckey, w_cout, g_two, b_two, w_up, w_down):
    params = (w_skip.astype(jnp.float32), g_skip.astype(jnp.float32), b_skip.astype(jnp.float32), w_mod.astype(jnp.float32), g_one.astype(jnp.float32), b_one.astype(jnp.float32), w_qkv.astype(jnp.float32), g_query.astype(jnp.float32), g_key.astype(jnp.float32), w_out.astype(jnp.float32), g_three.astype(jnp.float32), b_three.astype(jnp.float32), w_cquery.astype(jnp.float32), w_ckv.astype(jnp.float32), g_cquery.astype(jnp.float32), g_ckey.astype(jnp.float32), w_cout.astype(jnp.float32), g_two.astype(jnp.float32), b_two.astype(jnp.float32), w_up.astype(jnp.float32), w_down.astype(jnp.float32))
    emb = time_embed(steps)
    cosine, sine = rope_tables(positions)
    group = math.gcd(LATENTS, 4)
    rounds = LATENTS // group
    size = group * SEQ
    mask = valid.astype(jnp.float32)
    count = jnp.sum(mask)
    target = teacher.astype(jnp.float32)
    texts = text.astype(jnp.float32).reshape(rounds, group, TXT, TD)

    def total(params, hidden_f, skipped_f):

        def step(carry, pieces):
            part_hidden, part_skip, part_text, part_emb, part_cos, part_sin, part_target, part_mask = pieces
            result = jax.checkpoint(layer)(params, part_hidden, part_skip, part_text, part_emb, part_cos, part_sin)
            error = jnp.sum(part_mask[:, None] * (result - part_target) ** 2)
            return (carry + error, result)
        sse, results = lax.scan(step, jnp.zeros((), jnp.float32), (hidden_f.reshape(rounds, size, D), skipped_f.reshape(rounds, size, D), texts, emb.reshape(rounds, group, FREQ), cosine.reshape(rounds, size, HD), sine.reshape(rounds, size, HD), target.reshape(rounds, size, D), mask.reshape(rounds, size)))
        scaled = sse * (16.0 * LATENTS) / count
        return (scaled, (results.reshape(TOKENS, D), sse))
    scaled, back_fn, extra = jax.vjp(total, params, hidden.astype(jnp.float32), skipped.astype(jnp.float32), has_aux=True)
    output, sse = extra
    grads, d_hidden, d_skipped = back_fn(jnp.ones((), jnp.float32))
    d_w_skip, d_g_skip, d_b_skip, d_w_mod, d_g_one, d_b_one, d_w_qkv, d_g_query, d_g_key, d_w_out, d_g_three, d_b_three, d_w_cquery, d_w_ckv, d_g_cquery, d_g_ckey, d_w_cout, d_g_two, d_b_two, d_w_up, d_w_down = grads
    loss = sse / (count * D)
    return (output, d_hidden, d_skipped, d_w_skip, d_g_skip, d_b_skip, d_w_mod, d_g_one, d_b_one, d_w_qkv, d_g_query, d_g_key, d_w_out, d_g_three, d_b_three, d_w_cquery, d_w_ckv, d_g_cquery, d_g_ckey, d_w_cout, d_g_two, d_b_two, d_w_up, d_w_down, loss)
```

```python
from functools import partial
import math

import jax
import jax.numpy as jnp
from jax import lax
from jax.sharding import Mesh
from jax.sharding import PartitionSpec as P

D = 1408
HEADS = 16
HD = 88
FREQ = 256
TXT = 333
SEQ = 1024
LINE = ("row", "col_0")
CORE = "col_1"
COL = ("col_0", "col_1")
ROW_COL = ("row", "col_0", "col_1")
DP = ("dp_0", "dp_1")
ALL = ("dp_0", "dp_1", "row", "col_0", "col_1")
COL_ROW = ("col_0", "col_1", "row")
CHIPS = 4
HALF = SEQ // 2
PIECE = HALF // CHIPS
BF = jnp.bfloat16
F32 = jnp.float32


epsilon = 1e-06


def mult(left, right):
    return jnp.dot(left, right, preferred_element_type=jnp.float32)


def mult_left(left, right):
    return lax.dot_general(
        left, right, (((0,), (0,)), ((), ())), preferred_element_type=jnp.float32
    )


def mult_right(left, right):
    return lax.dot_general(
        left, right, (((1,), (1,)), ((), ())), preferred_element_type=jnp.float32
    )


def from_chip(value, ahead):
    return lax.ppermute(value, LINE, [(i, (i - ahead) % CHIPS) for i in range(CHIPS)])


def other_core(value):
    return lax.ppermute(value, CORE, [(0, 1), (1, 0)])


def other_row(value):
    return lax.ppermute(value, "row", [(0, 1), (1, 0)])


def gather_tokens(piece):
    return jnp.concatenate([piece] + [from_chip(piece, j) for j in range(1, CHIPS)], axis=0)


SENT = (BF,) * 7


def scatter_tokens(partial_sums, which=0):
    total = partial_sums[:PIECE]
    for j in range(1, CHIPS):
        sent = partial_sums[j * PIECE : (j + 1) * PIECE].astype(SENT[which])
        total = total + from_chip(sent, CHIPS - j).astype(F32)
    return total


def sum_over_chips(value):
    total = value
    for j in range(1, CHIPS):
        total = total + jnp.roll(from_chip(value, j), j * PIECE, axis=1)
    return total


def turned(value, start):
    twice = jnp.concatenate([value, value], axis=0)
    return lax.dynamic_slice_in_dim(twice, start, value.shape[0], 0)


def norm_forward(values, gain, offset):
    mean = jnp.mean(values, axis=1, keepdims=True)
    spread = jnp.mean(values * values, axis=1, keepdims=True) - mean * mean
    rstd = lax.rsqrt(spread + epsilon)
    scaled = (values - mean) * rstd
    return (scaled * gain + offset, scaled, rstd)


def norm_backward(grad, scaled, rstd, gain):
    weighted = grad * gain
    first = jnp.mean(weighted, axis=1, keepdims=True)
    second = jnp.mean(weighted * scaled, axis=1, keepdims=True)
    back = rstd * (weighted - first - scaled * second)
    return (back, jnp.sum(grad * scaled, axis=0), jnp.sum(grad, axis=0))


def halves_swapped(weight, dim, row):
    kept = lax.dynamic_slice_in_dim(weight, row * (weight.shape[dim] // 2), weight.shape[dim] // 2, dim)
    sent = lax.dynamic_slice_in_dim(
        weight, (1 - row) * (weight.shape[dim] // 2), weight.shape[dim] // 2, dim
    )
    return (kept, other_row(sent))


def in_row_order(kept, received, dim, row):
    three = jnp.concatenate([received, kept, received], axis=dim)
    return lax.dynamic_slice_in_dim(
        three, (1 - row) * kept.shape[dim], 2 * kept.shape[dim], dim
    )


def full_columns(weight, row):
    kept, received = halves_swapped(weight, 1, row)
    own = in_row_order(kept, received, 0, row)
    return jnp.concatenate([own, other_core(own)], axis=1)


def full_rows(weight, row):
    kept, received = halves_swapped(weight, 0, row)
    own = in_row_order(kept, received, 1, row)
    return jnp.concatenate([own, other_core(own)], axis=0)


def core_summed(partial_sums):
    n = partial_sums.shape[1] // 2
    sent = other_core(partial_sums[:, n:].astype(BF))
    return (partial_sums[:, :n] + sent.astype(F32)).astype(BF)


def over_latents(grads, row):
    rows, n = grads.shape
    count = lax.axis_size(DP)
    if count == 1:
        kept, received = halves_swapped(grads, 0, row)
        return in_row_order(kept, received, 1, row)
    chunk = rows // count
    arrived = lax.all_to_all(grads.reshape(count, chunk, n), DP, 0, 0, tiled=True)
    part = jnp.sum(arrived.astype(F32), axis=0).astype(BF)
    half = count // 2
    pairs = []
    for i in range(count):
        for r in range(2):
            stays = i // half == r
            pairs.append((2 * i + r, 2 * i + r if stays else 2 * ((i + half) % count) + 1 - r))
    part = lax.ppermute(part, DP + ("row",), pairs)
    spread = lax.all_gather(part, DP, axis=0)
    spread = spread.reshape(2, half * chunk, n)
    return jnp.concatenate([spread[0], spread[1]], axis=1)


def head_norm(values, gain):
    mean = jnp.mean(values, axis=-1, keepdims=True)
    spread = jnp.mean(values * values, axis=-1, keepdims=True) - mean * mean
    return (values - mean) * lax.rsqrt(spread + epsilon) * gain


def rotate(values):
    quarter = values.shape[-1] // 4
    return jnp.concatenate(
        [
            -values[..., quarter : 2 * quarter],
            values[..., :quarter],
            -values[..., 3 * quarter :],
            values[..., 2 * quarter : 3 * quarter],
        ],
        axis=-1,
    )


def qk_prep(raw, gain, cosine, sine):
    normal = head_norm(raw, gain)
    return normal * cosine + rotate(normal) * sine


def gelu_tanh(values):
    return jax.nn.gelu(values, approximate=True)


def rope_tables(positions):
    quarter = HD // 4
    freqs = jnp.exp(-math.log(10000.0) * jnp.arange(quarter, dtype=jnp.float32) / quarter)
    rows_angle = positions[0].astype(jnp.float32)[:, None] * freqs[None, :]
    cols_angle = positions[1].astype(jnp.float32)[:, None] * freqs[None, :]
    cosine = jnp.concatenate(
        [jnp.cos(rows_angle), jnp.cos(rows_angle), jnp.cos(cols_angle), jnp.cos(cols_angle)], axis=1
    )
    sine = jnp.concatenate(
        [jnp.sin(rows_angle), jnp.sin(rows_angle), jnp.sin(cols_angle), jnp.sin(cols_angle)], axis=1
    )
    return (cosine, sine)


def time_embed(steps):
    half = FREQ // 2
    freqs = jnp.exp(-math.log(10000.0) * jnp.arange(half, dtype=jnp.float32) / half)
    angles = steps.astype(jnp.float32)[:, None] * freqs[None, :]
    return jnp.concatenate([jnp.cos(angles), jnp.sin(angles)], axis=1)


def attend_forward(query, keys, values):
    scale = HD ** (-0.5)
    length = query.shape[1]
    block = min(512, length)
    outputs = []
    totals = []
    for start in range(0, length, block):
        piece = query[:, start : start + block]
        scores = scale * jnp.einsum(
            "lqhd,lkhd->lhqk", piece, keys, preferred_element_type=jnp.float32
        )
        top = jnp.max(scores, axis=-1, keepdims=True)
        expo = jnp.exp(scores - top)
        summed = jnp.sum(expo, axis=-1, keepdims=True)
        weights = expo / summed
        totals.append(top[..., 0] + jnp.log(summed[..., 0]))
        outputs.append(
            jnp.einsum(
                "lhqk,lkhd->lqhd",
                weights.astype(jnp.bfloat16),
                values,
                preferred_element_type=jnp.float32,
            )
        )
    return (jnp.concatenate(outputs, axis=1), jnp.concatenate(totals, axis=2))


def attend_backward(query, keys, values, totals, grad_out):
    scale = HD ** (-0.5)
    length = query.shape[1]
    block = min(512, length)
    d_keys = jnp.zeros(keys.shape, jnp.float32)
    d_values = jnp.zeros(values.shape, jnp.float32)
    d_query = []
    for start in range(0, length, block):
        piece = query[:, start : start + block]
        grad_piece = grad_out[:, start : start + block]
        scores = scale * jnp.einsum(
            "lqhd,lkhd->lhqk", piece, keys, preferred_element_type=jnp.float32
        )
        weights = jnp.exp(scores - totals[:, :, start : start + block, None])
        d_weights = jnp.einsum(
            "lqhd,lkhd->lhqk", grad_piece, values, preferred_element_type=jnp.float32
        )
        d_scores = weights * (d_weights - jnp.sum(d_weights * weights, axis=-1, keepdims=True))
        d_scores_b = d_scores.astype(jnp.bfloat16)
        d_query.append(
            scale
            * jnp.einsum("lhqk,lkhd->lqhd", d_scores_b, keys, preferred_element_type=jnp.float32)
        )
        d_keys = d_keys + scale * jnp.einsum(
            "lhqk,lqhd->lkhd", d_scores_b, piece, preferred_element_type=jnp.float32
        )
        d_values = d_values + jnp.einsum(
            "lhqk,lqhd->lkhd",
            weights.astype(jnp.bfloat16),
            grad_piece,
            preferred_element_type=jnp.float32,
        )
    return (jnp.concatenate(d_query, axis=1), d_keys, d_values)


def local(
    hidden,
    skipped,
    text,
    teacher,
    valid,
    steps,
    positions,
    w_skip,
    g_skip,
    b_skip,
    w_mod,
    g_one,
    b_one,
    w_qkv,
    g_query,
    g_key,
    w_out,
    g_three,
    b_three,
    w_cquery,
    w_ckv,
    g_cquery,
    g_ckey,
    w_cout,
    g_two,
    b_two,
    w_up,
    w_down,
):
    row = lax.axis_index("row")
    chip = lax.axis_index(LINE)
    core = lax.axis_index(CORE)
    width = hidden.shape[1]
    turn = chip * PIECE
    heads_own = HEADS // (2 * CHIPS)
    heads = 2 * heads_own
    shape_four = (1, HALF, heads, HD)

    def own_tokens(values):
        return turned(lax.dynamic_slice_in_dim(values, core * HALF, HALF, 0), turn)

    def other_tokens(values):
        return turned(lax.dynamic_slice_in_dim(values, (1 - core) * HALF, HALF, 0), turn)

    skip_kept, skip_received = halves_swapped(w_skip, 1, row)
    skip_own = in_row_order(skip_kept, skip_received, 2, row)
    skip_all = jnp.stack([skip_own, other_core(skip_own)], axis=1).reshape(4 * width, D)
    qkv_all = full_columns(w_qkv, row)
    out_all = full_rows(w_out, row)
    cquery_all = full_columns(w_cquery, row)
    ckv_all = full_columns(w_ckv, row)
    cout_all = full_rows(w_cout, row)
    up_all = full_columns(w_up, row)
    down_all = full_rows(w_down, row)

    emb = time_embed(steps).astype(BF)
    freq_here = w_mod.shape[0]
    emb_here = lax.dynamic_slice_in_dim(emb, lax.axis_index(COL) * freq_here, freq_here, 1)
    shift_part = mult(emb_here, w_mod)
    vectors = jnp.concatenate(
        [jnp.stack([g_one, b_one, g_three, b_three, g_two, b_two]).reshape(-1), shift_part[0]]
    )
    gathered = lax.all_gather(vectors, ROW_COL, axis=0)
    gains = jnp.transpose(gathered[:, : 6 * width].reshape(8, 6, width), (1, 0, 2)).reshape(6, D)
    gain_one, offset_one, gain_three, offset_three, gain_two, offset_two = gains
    shift = jnp.sum(gathered[:, 6 * width :].reshape(2, 4, D // 2), axis=1).reshape(D)
    mask_all = valid.astype(F32)
    count = lax.psum(jnp.sum(mask_all), DP)
    mask = lax.dynamic_slice_in_dim(mask_all, core * HALF + turn, PIECE, 0)

    teacher_blocks = jnp.transpose(
        teacher.reshape(2, CHIPS, PIECE, width), (1, 0, 2, 3)
    ).reshape(2 * CHIPS, PIECE, width)
    teacher_here = jnp.transpose(
        lax.all_to_all(teacher_blocks, ROW_COL, 0, 0, tiled=True), (1, 0, 2)
    ).reshape(PIECE, D)

    wide_text = lax.all_gather(text[0], ROW_COL, axis=1, tiled=True)

    cosine, sine = rope_tables(own_tokens(positions.T).T)
    prep = partial(qk_prep, cosine=cosine[:, None, :], sine=sine[:, None, :])

    joined = jnp.concatenate([hidden, skipped], axis=1)
    mine = own_tokens(joined)
    theirs = other_core(other_tokens(joined))
    pairs = jnp.stack(
        [mine.reshape(HALF, 2, width), theirs.reshape(HALF, 2, width)], axis=2
    ).reshape(HALF, 4 * width).astype(F32)
    skip_vectors = jnp.stack([g_skip, b_skip])
    both_vectors = jnp.stack([skip_vectors, other_core(skip_vectors)], axis=2).reshape(2, 4 * width)
    skip_sums = sum_over_chips(jnp.stack([jnp.sum(pairs, axis=1), jnp.sum(pairs * pairs, axis=1)]))
    skip_mean = skip_sums[0] / (2 * D)
    skip_rstd = lax.rsqrt(skip_sums[1] / (2 * D) - skip_mean * skip_mean + epsilon)
    skip_scaled = (pairs - skip_mean[:, None]) * skip_rstd[:, None]
    normed = (skip_scaled * both_vectors[0] + both_vectors[1]).astype(BF)
    stream = scatter_tokens(mult(normed, skip_all), 0)

    normed_one, scaled_one, rstd_one = norm_forward(stream, gain_one, offset_one)
    wide_one = gather_tokens((normed_one + shift).astype(BF))
    packed = mult(wide_one, qkv_all).reshape(HALF, heads, 3, HD)
    query_raw = packed[:, :, 0]
    key_raw = packed[:, :, 1]
    query = prep(query_raw, g_query).astype(BF).reshape(shape_four)
    keys_here = prep(key_raw, g_key).astype(BF)
    values_here = packed[:, :, 2].astype(BF)

    def swapped_heads(values):
        return jnp.concatenate([values[:, heads_own:], values[:, :heads_own]], axis=1)

    key_values = other_core(swapped_heads(jnp.concatenate([keys_here, values_here], axis=2)))
    keys = jnp.concatenate([keys_here, key_values[..., :HD]], axis=0)[None]
    values = jnp.concatenate([values_here, key_values[..., HD:]], axis=0)[None]
    mixed, self_totals = attend_forward(query, keys, values)
    mixed_here = mixed.reshape(HALF, heads * HD).astype(BF)
    stream_two = stream + scatter_tokens(mult(mixed_here, out_all), 1)

    normed_three, scaled_three, rstd_three = norm_forward(stream_two, gain_three, offset_three)
    wide_three = gather_tokens(normed_three.astype(BF))
    cquery_raw = mult(wide_three, cquery_all).reshape(HALF, heads, HD)
    cquery = prep(cquery_raw, g_cquery).astype(BF).reshape(shape_four)
    ckv = mult(wide_text, ckv_all).reshape(1, TXT, heads, 2, HD)
    ckey_raw = ckv[:, :, :, 0]
    ckeys = head_norm(ckey_raw, g_ckey).astype(BF)
    cvalues = ckv[:, :, :, 1].astype(BF)
    cmixed, cross_totals = attend_forward(cquery, ckeys, cvalues)
    cmixed_here = cmixed.reshape(HALF, heads * HD).astype(BF)
    stream_three = stream_two + scatter_tokens(mult(cmixed_here, cout_all), 2)

    normed_two, scaled_two, rstd_two = norm_forward(stream_three, gain_two, offset_two)
    wide_two = gather_tokens(normed_two.astype(BF))
    upper = mult(wide_two, up_all)
    active, gelu_back = jax.vjp(gelu_tanh, upper)
    active_here = active.astype(BF)
    output_here = stream_three + scatter_tokens(mult(active_here, down_all), 3)

    diff = output_here - teacher_here.astype(F32)
    sse_local = jnp.sum(mask[:, None] * diff * diff)
    factor = 32.0 * lax.axis_size(DP) / count
    grad_out = factor * mask[:, None] * diff
    output_blocks = jnp.transpose(
        output_here.astype(BF).reshape(PIECE, 2 * CHIPS, width), (1, 0, 2)
    )
    output_back = lax.all_to_all(output_blocks, ROW_COL, 0, 0, tiled=True)
    output = jnp.transpose(
        output_back.reshape(CHIPS, 2, PIECE, width), (1, 0, 2, 3)
    ).reshape(SEQ, width).astype(F32)

    wide_grad = gather_tokens(grad_out.astype(BF))
    d_upper = gelu_back(mult_right(wide_grad, down_all))[0].astype(BF)
    d_normed_two = scatter_tokens(mult_right(d_upper, up_all), 4)
    d_down = core_summed(mult_left(wide_grad, active_here))
    d_up = core_summed(mult_left(wide_two, d_upper))
    back_two, d_g_two, d_b_two = norm_backward(d_normed_two, scaled_two, rstd_two, gain_two)
    grad_three = grad_out + back_two

    wide_three_grad = gather_tokens(grad_three.astype(BF))
    d_cmixed = mult_right(wide_three_grad, cout_all).astype(BF).reshape(shape_four)
    d_cquery, d_ckeys, d_cvalues = attend_backward(cquery, ckeys, cvalues, cross_totals, d_cmixed)
    unused, cquery_back = jax.vjp(prep, cquery_raw, g_cquery)
    d_cquery_raw, d_g_cquery = cquery_back(d_cquery.reshape(HALF, heads, HD))
    d_cquery_here = d_cquery_raw.reshape(HALF, heads * HD).astype(BF)
    d_normed_three = scatter_tokens(mult_right(d_cquery_here, cquery_all), 5)
    unused, ckey_back = jax.vjp(head_norm, ckey_raw, g_ckey)
    d_ckey_raw, d_g_ckey = ckey_back(d_ckeys)
    d_ckv = jnp.stack([d_ckey_raw, d_cvalues], axis=3).reshape(TXT, heads * 2 * HD).astype(BF)
    d_cout = core_summed(mult_left(wide_three_grad, cmixed_here))
    d_cquery_w = core_summed(mult_left(wide_three, d_cquery_here))
    d_ckv_w = core_summed(mult_left(wide_text, d_ckv))
    back_three, d_g_three, d_b_three = norm_backward(
        d_normed_three, scaled_three, rstd_three, gain_three
    )
    grad_two = grad_three + back_three

    wide_two_grad = gather_tokens(grad_two.astype(BF))
    d_mixed = mult_right(wide_two_grad, out_all).astype(BF).reshape(shape_four)
    d_out = core_summed(mult_left(wide_two_grad, mixed_here))
    d_query, d_keys, d_values = attend_backward(query, keys, values, self_totals, d_mixed)
    d_both = jnp.concatenate([d_keys[0], d_values[0]], axis=2)
    d_both = d_both[:HALF] + other_core(swapped_heads(d_both[HALF:]).astype(BF)).astype(F32)
    unused, query_back = jax.vjp(prep, query_raw, g_query)
    d_query_raw, d_g_query = query_back(d_query.reshape(HALF, heads, HD))
    unused, key_back = jax.vjp(prep, key_raw, g_key)
    d_key_raw, d_g_key = key_back(d_both[..., :HD])
    d_packed = (
        jnp.stack([d_query_raw, d_key_raw, d_both[..., HD:]], axis=2)
        .reshape(HALF, heads * 3 * HD)
        .astype(BF)
    )
    d_inputs = scatter_tokens(mult_right(d_packed, qkv_all), 6)
    d_qkv = core_summed(mult_left(wide_one, d_packed))
    d_shift_part = jnp.sum(d_inputs, axis=0)
    back_one, d_g_one, d_b_one = norm_backward(d_inputs, scaled_one, rstd_one, gain_one)
    grad_one = grad_two + back_one

    wide_one_grad = gather_tokens(grad_one.astype(BF))
    d_joined = mult_right(wide_one_grad, skip_all)
    d_skip_part = mult_left(wide_one_grad, normed).reshape(D, 2, 2, width)
    d_skip = core_summed(jnp.transpose(d_skip_part, (0, 2, 1, 3)).reshape(D, 4 * width))
    weighted = d_joined * both_vectors[0]
    back_sums = sum_over_chips(
        jnp.stack([jnp.sum(weighted, axis=1), jnp.sum(weighted * skip_scaled, axis=1)])
    ) / (2 * D)
    back_joined = skip_rstd[:, None] * (
        weighted - back_sums[0][:, None] - skip_scaled * back_sums[1][:, None]
    )
    back_joined = back_joined.reshape(HALF, 2, 2, width)
    back_mine = back_joined[:, :, 0].reshape(HALF, 2 * width)
    back_theirs = other_core(back_joined[:, :, 1].reshape(HALF, 2 * width))
    unturn = (CHIPS - chip) % CHIPS * PIECE
    back_mine = turned(back_mine, unturn)
    back_theirs = turned(back_theirs, unturn)
    back_tokens = lax.dynamic_slice_in_dim(
        jnp.concatenate([back_mine, back_theirs, back_mine], axis=0), core * HALF, SEQ, 0
    )
    d_hidden = back_tokens[:, :width]
    d_skipped = back_tokens[:, width:]
    skip_grads = jnp.stack([jnp.sum(d_joined * skip_scaled, axis=0), jnp.sum(d_joined, axis=0)])
    skip_grads = skip_grads.reshape(2, 2, 2, width)
    skip_grads = skip_grads[:, :, 0] + other_core(skip_grads[:, :, 1])

    norm_grads = jnp.stack([d_g_one, d_b_one, d_g_three, d_b_three, d_g_two, d_b_two])
    norm_grads = jnp.transpose(norm_grads.reshape(6, 8, width), (1, 0, 2)).reshape(8, 6 * width)
    shift_grads = jnp.repeat(d_shift_part.reshape(2, D // 2), 4, axis=0)
    shared = jnp.concatenate([d_g_query, d_g_key, d_g_cquery, d_g_ckey, sse_local[None]])
    small = jnp.concatenate(
        [norm_grads, shift_grads, jnp.broadcast_to(shared[None], (8, shared.shape[0]))], axis=1
    )
    small = jnp.sum(lax.all_to_all(small, ROW_COL, 0, 0, tiled=True), axis=0)
    small = jnp.concatenate([small, skip_grads.reshape(-1)])
    small = lax.all_gather(small, DP, axis=0)
    latent_shift = small[:, 6 * width : 6 * width + D // 2].astype(BF)
    all_emb = lax.all_gather(emb_here, DP, axis=0, tiled=True)
    d_w_mod = mult_left(all_emb, latent_shift)
    totals = jnp.sum(small, axis=0)
    d_g_one, d_b_one, d_g_three, d_b_three, d_g_two, d_b_two = totals[: 6 * width].reshape(6, width)
    shared = totals[6 * width + D // 2 :]
    d_g_query, d_g_key, d_g_cquery, d_g_ckey = shared[: 4 * HD].reshape(4, HD)
    loss = shared[4 * HD] / (count * D)
    d_g_skip, d_b_skip = shared[4 * HD + 1 :].reshape(2, 2, width)

    first = over_latents(jnp.concatenate([d_up, d_down], axis=1), row)
    second = over_latents(
        jnp.concatenate([d_cquery_w, d_cout, d_out], axis=1), row
    )
    d_w_ckv = over_latents(d_ckv_w, row).astype(F32)
    third = over_latents(d_qkv, row)
    fourth = over_latents(d_skip, row)

    def columns(summed, start, count):
        n = summed.shape[1] // 2
        return jnp.concatenate(
            [summed[:, start : start + count], summed[:, n + start : n + start + count]], axis=1
        ).astype(F32)

    n_up = d_up.shape[1]
    d_w_up = columns(first, 0, n_up)
    d_w_down = columns(first, n_up, n_up).T
    d_w_cquery = columns(second, 0, width)
    d_w_cout = columns(second, width, width).T
    d_w_out = columns(second, 2 * width, width).T
    d_w_qkv = third.astype(F32)
    d_w_skip = jnp.transpose(
        fourth.astype(F32).reshape(D // 2, 2, 2, width), (2, 1, 3, 0)
    ).reshape(2, 2 * width, D // 2)
    return (
        output,
        d_hidden,
        d_skipped,
        d_w_skip,
        d_g_skip,
        d_b_skip,
        d_w_mod,
        d_g_one,
        d_b_one,
        d_w_qkv,
        d_g_query,
        d_g_key,
        d_w_out,
        d_g_three,
        d_b_three,
        d_w_cquery,
        d_w_ckv,
        d_g_cquery,
        d_g_ckey,
        d_w_cout,
        d_g_two,
        d_b_two,
        d_w_up,
        d_w_down,
        loss,
    )


def solution(mesh):
    side = math.isqrt(mesh.shape["dp"])
    split = Mesh(
        mesh.devices.reshape(side, side, mesh.shape["row"], 2, 2),
        ("dp_0", "dp_1", "row", "col_0", "col_1"),
    )
    in_specs = (
        P(DP, COL_ROW),
        P(DP, COL_ROW),
        P(DP, None, ROW_COL),
        P(DP, ROW_COL),
        P(DP),
        P(DP),
        P(None, DP),
        P(None, COL, "row"),
        P(None, COL_ROW),
        P(None, COL_ROW),
        P(COL, "row"),
        P(ROW_COL),
        P(ROW_COL),
        P("row", COL),
        P(),
        P(),
        P(COL, "row"),
        P(ROW_COL),
        P(ROW_COL),
        P("row", COL),
        P("row", COL),
        P(),
        P(),
        P(COL, "row"),
        P(ROW_COL),
        P(ROW_COL),
        P("row", COL),
        P(COL, "row"),
    )
    out_specs = (
        P(DP, ROW_COL),
        P(DP, COL_ROW),
        P(DP, COL_ROW),
        P(None, COL, "row"),
        P(None, COL_ROW),
        P(None, COL_ROW),
        P(COL, "row"),
        P(ROW_COL),
        P(ROW_COL),
        P("row", COL),
        P(),
        P(),
        P(COL, "row"),
        P(ROW_COL),
        P(ROW_COL),
        P("row", COL),
        P("row", COL),
        P(),
        P(),
        P(COL, "row"),
        P(ROW_COL),
        P(ROW_COL),
        P("row", COL),
        P(COL, "row"),
        P(),
    )
    return jax.shard_map(local, mesh=split, in_specs=in_specs, out_specs=out_specs, check_vma=False)
```

```python
from functools import partial
import math

import jax
import jax.numpy as jnp
from jax import lax
from jax.sharding import Mesh
from jax.sharding import PartitionSpec as P

D = 1408
HEADS = 16
HD = 88
FREQ = 256
TXT = 333
SEQ = 1024
LINE = ("row", "col_0")
CORE = "col_1"
COL = ("col_0", "col_1")
ROW_COL = ("row", "col_0", "col_1")
DP = ("dp_0", "dp_1")
ALL = ("dp_0", "dp_1", "row", "col_0", "col_1")
COL_ROW = ("col_0", "col_1", "row")
CHIPS = 4
HALF = SEQ // 2
PIECE = HALF // CHIPS
BF = jnp.bfloat16
F32 = jnp.float32


epsilon = 1e-06


def mult(left, right):
    return jnp.dot(left, right, preferred_element_type=jnp.float32)


def mult_left(left, right):
    return lax.dot_general(
        left, right, (((0,), (0,)), ((), ())), preferred_element_type=jnp.float32
    )


def mult_right(left, right):
    return lax.dot_general(
        left, right, (((1,), (1,)), ((), ())), preferred_element_type=jnp.float32
    )


def from_chip(value, ahead):
    return lax.ppermute(value, LINE, [(i, (i - ahead) % CHIPS) for i in range(CHIPS)])


def other_core(value):
    return lax.ppermute(value, CORE, [(0, 1), (1, 0)])


def other_row(value):
    return lax.ppermute(value, "row", [(0, 1), (1, 0)])


def gather_tokens(piece):
    return jnp.concatenate([piece] + [from_chip(piece, j) for j in range(1, CHIPS)], axis=0)


def scatter_tokens(partial_sums):
    total = partial_sums[:PIECE]
    for j in range(1, CHIPS):
        sent = partial_sums[j * PIECE : (j + 1) * PIECE].astype(BF)
        total = total + from_chip(sent, CHIPS - j).astype(F32)
    return total


def sum_over_chips(value):
    total = value
    for j in range(1, CHIPS):
        total = total + jnp.roll(from_chip(value, j), j * PIECE, axis=1)
    return total


def turned(value, start):
    twice = jnp.concatenate([value, value], axis=0)
    return lax.dynamic_slice_in_dim(twice, start, value.shape[0], 0)


def norm_forward(values, gain, offset):
    mean = jnp.mean(values, axis=1, keepdims=True)
    spread = jnp.mean(values * values, axis=1, keepdims=True) - mean * mean
    rstd = lax.rsqrt(spread + epsilon)
    scaled = (values - mean) * rstd
    return (scaled * gain + offset, scaled, rstd)


def norm_backward(grad, scaled, rstd, gain):
    weighted = grad * gain
    first = jnp.mean(weighted, axis=1, keepdims=True)
    second = jnp.mean(weighted * scaled, axis=1, keepdims=True)
    back = rstd * (weighted - first - scaled * second)
    return (back, jnp.sum(grad * scaled, axis=0), jnp.sum(grad, axis=0))


def halves_swapped(weight, dim, row):
    kept = lax.dynamic_slice_in_dim(weight, row * (weight.shape[dim] // 2), weight.shape[dim] // 2, dim)
    sent = lax.dynamic_slice_in_dim(
        weight, (1 - row) * (weight.shape[dim] // 2), weight.shape[dim] // 2, dim
    )
    return (kept, other_row(sent))


def in_row_order(kept, received, dim, row):
    three = jnp.concatenate([received, kept, received], axis=dim)
    return lax.dynamic_slice_in_dim(
        three, (1 - row) * kept.shape[dim], 2 * kept.shape[dim], dim
    )


def settled(value):
    return jnp.minimum(jnp.abs(value.reshape(-1)[0].astype(F32)), 0.0)


def copied_to_each(value, axis):
    length = lax.axis_size(axis)
    return lax.all_to_all(
        jnp.broadcast_to(value[None], (length, *value.shape)), axis, 0, 0, tiled=True
    )


def with_other_core(own):
    return jnp.concatenate([own, other_core(own)], axis=1)


def whole_columns(weight, row):
    kept, received = halves_swapped(weight, 1, row)
    return in_row_order(kept, received, 0, row)


def whole_by_latents(blocks, row, after=None):
    place = lax.axis_index(DP)
    half = lax.axis_size(DP) // 2
    kept, sent = [], []
    for block in blocks:
        n = block.shape[1] // 2
        kept.append(lax.dynamic_slice_in_dim(block, row * n, n, 1))
        sent.append(lax.dynamic_slice_in_dim(block, (1 - row) * n, n, 1))
    kept = jnp.concatenate(kept, axis=1) if len(kept) > 1 else kept[0]
    sent = jnp.concatenate(sent, axis=1) if len(sent) > 1 else sent[0]
    mine = jnp.where(place // half == row, kept, other_row(sent))
    if after is not None:
        mine = mine + settled(after).astype(BF)
    return lax.all_gather(mine, DP, axis=0, tiled=True)


def block_of_rows(weight):
    half = lax.axis_size(DP) // 2
    rows = weight.shape[0] // half
    return lax.dynamic_slice_in_dim(weight, lax.axis_index(DP) % half * rows, rows, 0)


def block_of_columns(weight):
    half = lax.axis_size(DP) // 2
    columns = weight.shape[1] // half
    return lax.dynamic_slice_in_dim(weight, lax.axis_index(DP) % half * columns, columns, 1).T


def weight_grad(left, right):
    n = right.shape[1] // 2
    theirs = other_core(mult_left(left, right[:, n:]).astype(BF))
    return (mult_left(left, right[:, :n]) + theirs.astype(F32)).astype(BF)


def summed_over_latents(grads):
    count = lax.axis_size(DP)
    if count == 1:
        return grads
    rows, n = grads.shape
    arrived = lax.all_to_all(grads.reshape(count, rows // count, n), DP, 0, 0, tiled=True)
    part = jnp.sum(arrived.astype(F32), axis=0).astype(BF)
    half = count // 2
    pairs = []
    for i in range(count):
        for r in range(2):
            stays = i // half == r
            pairs.append((2 * i + r, 2 * i + r if stays else 2 * ((i + half) % count) + 1 - r))
    return lax.ppermute(part, DP + ("row",), pairs)


def spread_over_latents(part, row, gather=True):
    count = lax.axis_size(DP)
    if count == 1:
        kept, received = halves_swapped(part, 0, row)
        return in_row_order(kept, received, 1, row)
    rows, n = part.shape
    if gather:
        spread = lax.all_gather(part, DP, axis=0)
    else:
        spread = copied_to_each(part, DP)
    spread = spread.reshape(2, count // 2 * rows, n)
    return jnp.concatenate([spread[0], spread[1]], axis=1)


def head_norm(values, gain):
    mean = jnp.mean(values, axis=-1, keepdims=True)
    spread = jnp.mean(values * values, axis=-1, keepdims=True) - mean * mean
    return (values - mean) * lax.rsqrt(spread + epsilon) * gain


def rotate(values):
    quarter = values.shape[-1] // 4
    return jnp.concatenate(
        [
            -values[..., quarter : 2 * quarter],
            values[..., :quarter],
            -values[..., 3 * quarter :],
            values[..., 2 * quarter : 3 * quarter],
        ],
        axis=-1,
    )


def qk_prep(raw, gain, cosine, sine):
    normal = head_norm(raw, gain)
    return normal * cosine + rotate(normal) * sine


def gelu_tanh(values):
    return jax.nn.gelu(values, approximate=True)


def rope_tables(positions):
    quarter = HD // 4
    freqs = jnp.exp(-math.log(10000.0) * jnp.arange(quarter, dtype=jnp.float32) / quarter)
    rows_angle = positions[0].astype(jnp.float32)[:, None] * freqs[None, :]
    cols_angle = positions[1].astype(jnp.float32)[:, None] * freqs[None, :]
    cosine = jnp.concatenate(
        [jnp.cos(rows_angle), jnp.cos(rows_angle), jnp.cos(cols_angle), jnp.cos(cols_angle)], axis=1
    )
    sine = jnp.concatenate(
        [jnp.sin(rows_angle), jnp.sin(rows_angle), jnp.sin(cols_angle), jnp.sin(cols_angle)], axis=1
    )
    return (cosine, sine)


def time_embed(steps):
    half = FREQ // 2
    freqs = jnp.exp(-math.log(10000.0) * jnp.arange(half, dtype=jnp.float32) / half)
    angles = steps.astype(jnp.float32)[:, None] * freqs[None, :]
    return jnp.concatenate([jnp.cos(angles), jnp.sin(angles)], axis=1)


def attend_forward(query, keys, values):
    scale = HD ** (-0.5)
    length = query.shape[1]
    block = min(512, length)
    outputs = []
    totals = []
    for start in range(0, length, block):
        piece = query[:, start : start + block]
        scores = scale * jnp.einsum(
            "lqhd,lkhd->lhqk", piece, keys, preferred_element_type=jnp.float32
        )
        top = jnp.max(scores, axis=-1, keepdims=True)
        expo = jnp.exp(scores - top)
        summed = jnp.sum(expo, axis=-1, keepdims=True)
        weights = expo / summed
        totals.append(top[..., 0] + jnp.log(summed[..., 0]))
        outputs.append(
            jnp.einsum(
                "lhqk,lkhd->lqhd",
                weights.astype(jnp.bfloat16),
                values,
                preferred_element_type=jnp.float32,
            )
        )
    return (jnp.concatenate(outputs, axis=1), jnp.concatenate(totals, axis=2))


def attend_backward(query, keys, values, totals, grad_out):
    scale = HD ** (-0.5)
    length = query.shape[1]
    block = min(512, length)
    d_keys = jnp.zeros(keys.shape, jnp.float32)
    d_values = jnp.zeros(values.shape, jnp.float32)
    d_query = []
    for start in range(0, length, block):
        piece = query[:, start : start + block]
        grad_piece = grad_out[:, start : start + block]
        scores = scale * jnp.einsum(
            "lqhd,lkhd->lhqk", piece, keys, preferred_element_type=jnp.float32
        )
        weights = jnp.exp(scores - totals[:, :, start : start + block, None])
        d_weights = jnp.einsum(
            "lqhd,lkhd->lhqk", grad_piece, values, preferred_element_type=jnp.float32
        )
        d_scores = weights * (d_weights - jnp.sum(d_weights * weights, axis=-1, keepdims=True))
        d_scores_b = d_scores.astype(jnp.bfloat16)
        d_query.append(
            scale
            * jnp.einsum("lhqk,lkhd->lqhd", d_scores_b, keys, preferred_element_type=jnp.float32)
        )
        d_keys = d_keys + scale * jnp.einsum(
            "lhqk,lqhd->lkhd", d_scores_b, piece, preferred_element_type=jnp.float32
        )
        d_values = d_values + jnp.einsum(
            "lhqk,lqhd->lkhd",
            weights.astype(jnp.bfloat16),
            grad_piece,
            preferred_element_type=jnp.float32,
        )
    return (jnp.concatenate(d_query, axis=1), d_keys, d_values)


def local(
    hidden,
    skipped,
    text,
    teacher,
    valid,
    steps,
    positions,
    w_skip,
    g_skip,
    b_skip,
    w_mod,
    g_one,
    b_one,
    w_qkv,
    g_query,
    g_key,
    w_out,
    g_three,
    b_three,
    w_cquery,
    w_ckv,
    g_cquery,
    g_ckey,
    w_cout,
    g_two,
    b_two,
    w_up,
    w_down,
):
    row = lax.axis_index("row")
    chip = lax.axis_index(LINE)
    core = lax.axis_index(CORE)
    width = hidden.shape[1]
    turn = chip * PIECE
    heads_own = HEADS // (2 * CHIPS)
    heads = 2 * heads_own
    shape_four = (1, HALF, heads, HD)

    def own_tokens(values):
        return turned(lax.dynamic_slice_in_dim(values, core * HALF, HALF, 0), turn)

    def other_tokens(values):
        return turned(lax.dynamic_slice_in_dim(values, (1 - core) * HALF, HALF, 0), turn)

    skip_two = jnp.transpose(w_skip.reshape(2, 2, width, D // 2), (3, 1, 0, 2)).reshape(
        D // 2, 4 * width
    )
    skip_own = whole_columns(skip_two, row)
    skip_other = other_core(skip_own)
    skip_all = jnp.concatenate([skip_own, skip_other], axis=1)
    if lax.axis_size(DP) == 1:
        qkv_all = with_other_core(whole_columns(w_qkv, row))
        out_all = with_other_core(whole_columns(w_out.T, row))
        cquery_all = with_other_core(whole_columns(w_cquery, row))
        cout_all = with_other_core(whole_columns(w_cout.T, row))
        ckv_all = with_other_core(whole_columns(w_ckv, row))
        up_all = with_other_core(whole_columns(w_up, row))
        down_all = with_other_core(whole_columns(w_down.T, row))
    else:
        qkv_own = whole_by_latents([block_of_rows(w_qkv)], row)
        ckv_block = block_of_rows(w_ckv)
        ckv_rows = ckv_block.shape[0]
        ckv_block = jnp.pad(ckv_block, ((0, D // lax.axis_size(DP) - ckv_rows), (0, 0)))
        four_own = whole_by_latents(
            [
                block_of_columns(w_out),
                block_of_rows(w_cquery),
                block_of_columns(w_cout),
                ckv_block,
            ],
            row,
            qkv_own,
        )
        up_own = whole_by_latents([block_of_rows(w_up)], row, four_own)
        down_own = whole_by_latents([block_of_columns(w_down)], row, up_own)
        qkv_all = with_other_core(qkv_own)
        four_other = other_core(four_own)

        def both(start, count):
            return jnp.concatenate(
                [four_own[:, start : start + count], four_other[:, start : start + count]], axis=1
            )

        out_all = both(0, width)
        cquery_all = both(width, width)
        cout_all = both(2 * width, width)
        ckv_all = both(3 * width, 2 * width).reshape(lax.axis_size(DP), -1, 4 * width)
        ckv_all = ckv_all[:, :ckv_rows].reshape(-1, 4 * width)
        up_all = with_other_core(up_own)
        down_all = with_other_core(down_own)

    emb = time_embed(steps).astype(BF)
    freq_here = w_mod.shape[0]
    emb_here = lax.dynamic_slice_in_dim(emb, lax.axis_index(COL) * freq_here, freq_here, 1)
    shift_part = mult(emb_here, w_mod)
    vectors = jnp.concatenate(
        [jnp.stack([g_one, b_one, g_three, b_three, g_two, b_two]).reshape(-1), shift_part[0]]
    )
    gathered = copied_to_each(vectors, ROW_COL)
    gains = jnp.transpose(gathered[:, : 6 * width].reshape(8, 6, width), (1, 0, 2)).reshape(6, D)
    gain_one, offset_one, gain_three, offset_three, gain_two, offset_two = gains
    shift = jnp.sum(gathered[:, 6 * width :].reshape(2, 4, D // 2), axis=1).reshape(D)
    mask_all = valid.astype(F32)
    counts = copied_to_each(jnp.broadcast_to(jnp.sum(mask_all), (1, 128)), DP)
    count = jnp.sum(counts[:, 0, 0])
    mask = lax.dynamic_slice_in_dim(mask_all, core * HALF + turn, PIECE, 0)

    teacher_blocks = jnp.transpose(
        teacher.reshape(2, CHIPS, PIECE, width), (1, 0, 2, 3)
    ).reshape(2 * CHIPS, PIECE, width)
    teacher_here = jnp.transpose(
        lax.all_to_all(teacher_blocks, ROW_COL, 0, 0, tiled=True), (1, 0, 2)
    ).reshape(PIECE, D)

    wide_text = jnp.transpose(copied_to_each(text[0], ROW_COL), (1, 0, 2)).reshape(TXT, -1)

    cosine, sine = rope_tables(own_tokens(positions.T).T)
    prep = partial(qk_prep, cosine=cosine[:, None, :], sine=sine[:, None, :])

    joined = jnp.concatenate([hidden, skipped], axis=1)
    mine = own_tokens(joined)
    theirs = other_core(other_tokens(joined))
    pairs = jnp.concatenate([mine, theirs], axis=1).astype(F32)
    skip_vectors = jnp.stack([g_skip, b_skip]).reshape(2, 2 * width)
    both_vectors = jnp.concatenate([skip_vectors, other_core(skip_vectors)], axis=1)
    skip_sums = sum_over_chips(jnp.stack([jnp.sum(pairs, axis=1), jnp.sum(pairs * pairs, axis=1)]))
    skip_mean = skip_sums[0] / (2 * D)
    skip_rstd = lax.rsqrt(skip_sums[1] / (2 * D) - skip_mean * skip_mean + epsilon)
    skip_scaled = (pairs - skip_mean[:, None]) * skip_rstd[:, None]
    normed = (skip_scaled * both_vectors[0] + both_vectors[1]).astype(BF)
    stream = scatter_tokens(mult_right(normed, skip_all))

    normed_one, scaled_one, rstd_one = norm_forward(stream, gain_one, offset_one)
    wide_one = gather_tokens((normed_one + shift).astype(BF))
    packed = mult(wide_one, qkv_all).reshape(HALF, heads, 3, HD)
    query_raw = packed[:, :, 0]
    key_raw = packed[:, :, 1]
    query = prep(query_raw, g_query).astype(BF).reshape(shape_four)
    keys_here = prep(key_raw, g_key).astype(BF)
    values_here = packed[:, :, 2].astype(BF)

    def swapped_heads(values):
        return jnp.concatenate([values[:, heads_own:], values[:, :heads_own]], axis=1)

    key_values = other_core(swapped_heads(jnp.concatenate([keys_here, values_here], axis=2)))
    keys = jnp.concatenate([keys_here, key_values[..., :HD]], axis=0)[None]
    values = jnp.concatenate([values_here, key_values[..., HD:]], axis=0)[None]
    mixed, self_totals = attend_forward(query, keys, values)
    mixed_here = mixed.reshape(HALF, heads * HD).astype(BF)
    stream_two = stream + scatter_tokens(mult_right(mixed_here, out_all))

    normed_three, scaled_three, rstd_three = norm_forward(stream_two, gain_three, offset_three)
    wide_three = gather_tokens(normed_three.astype(BF))
    cquery_raw = mult(wide_three, cquery_all).reshape(HALF, heads, HD)
    cquery = prep(cquery_raw, g_cquery).astype(BF).reshape(shape_four)
    ckv = mult(wide_text, ckv_all).reshape(1, TXT, heads, 2, HD)
    ckey_raw = ckv[:, :, :, 0]
    ckeys = head_norm(ckey_raw, g_ckey).astype(BF)
    cvalues = ckv[:, :, :, 1].astype(BF)
    cmixed, cross_totals = attend_forward(cquery, ckeys, cvalues)
    cmixed_here = cmixed.reshape(HALF, heads * HD).astype(BF)
    stream_three = stream_two + scatter_tokens(mult_right(cmixed_here, cout_all))

    normed_two, scaled_two, rstd_two = norm_forward(stream_three, gain_two, offset_two)
    wide_two = gather_tokens(normed_two.astype(BF))
    upper = mult(wide_two, up_all)
    active, gelu_back = jax.vjp(gelu_tanh, upper)
    active_here = active.astype(BF)
    output_here = stream_three + scatter_tokens(mult_right(active_here, down_all))

    diff = output_here - teacher_here.astype(F32)
    sse_local = jnp.sum(mask[:, None] * diff * diff)
    factor = 32.0 * lax.axis_size(DP) / count
    grad_out = factor * mask[:, None] * diff
    output_blocks = jnp.transpose(
        output_here.astype(BF).reshape(PIECE, 2 * CHIPS, width), (1, 0, 2)
    )
    output_back = lax.all_to_all(output_blocks, ROW_COL, 0, 0, tiled=True)
    output = jnp.transpose(
        output_back.reshape(CHIPS, 2, PIECE, width), (1, 0, 2, 3)
    ).reshape(SEQ, width).astype(F32)

    wide_grad = gather_tokens(grad_out.astype(BF))
    d_upper = gelu_back(mult(wide_grad, down_all))[0].astype(BF)
    d_normed_two = scatter_tokens(mult_right(d_upper, up_all))
    d_down = weight_grad(wide_grad, active_here)
    d_up = weight_grad(wide_two, d_upper)
    down_part = summed_over_latents(d_down)
    up_part = summed_over_latents(d_up)
    back_two, d_g_two, d_b_two = norm_backward(d_normed_two, scaled_two, rstd_two, gain_two)
    grad_three = grad_out + back_two

    wide_three_grad = gather_tokens(grad_three.astype(BF))
    d_cmixed = mult(wide_three_grad, cout_all).astype(BF).reshape(shape_four)
    d_cquery, d_ckeys, d_cvalues = attend_backward(cquery, ckeys, cvalues, cross_totals, d_cmixed)
    unused, cquery_back = jax.vjp(prep, cquery_raw, g_cquery)
    d_cquery_raw, d_g_cquery = cquery_back(d_cquery.reshape(HALF, heads, HD))
    d_cquery_here = d_cquery_raw.reshape(HALF, heads * HD).astype(BF)
    d_normed_three = scatter_tokens(mult_right(d_cquery_here, cquery_all))
    unused, ckey_back = jax.vjp(head_norm, ckey_raw, g_ckey)
    d_ckey_raw, d_g_ckey = ckey_back(d_ckeys)
    d_ckv = jnp.stack([d_ckey_raw, d_cvalues], axis=3).reshape(TXT, heads * 2 * HD).astype(BF)
    d_cout = weight_grad(wide_three_grad, cmixed_here)
    d_cquery_w = weight_grad(wide_three, d_cquery_here)
    d_ckv_w = weight_grad(wide_text, d_ckv)
    back_three, d_g_three, d_b_three = norm_backward(
        d_normed_three, scaled_three, rstd_three, gain_three
    )
    grad_two = grad_three + back_three

    wide_two_grad = gather_tokens((grad_two + settled(down_part)).astype(BF))
    d_mixed = mult(wide_two_grad, out_all).astype(BF).reshape(shape_four)
    d_out = weight_grad(wide_two_grad, mixed_here)
    count_blocks = max(lax.axis_size(DP) // 2, 1)
    d_ckv_blocks = d_ckv_w.reshape(2 * count_blocks, -1, 2 * width)
    padding = D // (2 * count_blocks) - d_ckv_blocks.shape[1]
    d_ckv_w = jnp.pad(d_ckv_blocks, ((0, 0), (0, padding), (0, 0))).reshape(D, 2 * width)
    four_part = summed_over_latents(
        jnp.concatenate([d_out, d_cquery_w, d_cout, d_ckv_w], axis=1)
    )
    d_query, d_keys, d_values = attend_backward(query, keys, values, self_totals, d_mixed)
    d_both = jnp.concatenate([d_keys[0], d_values[0]], axis=2)
    d_both = d_both[:HALF] + other_core(swapped_heads(d_both[HALF:]).astype(BF)).astype(F32)
    unused, query_back = jax.vjp(prep, query_raw, g_query)
    d_query_raw, d_g_query = query_back(d_query.reshape(HALF, heads, HD))
    unused, key_back = jax.vjp(prep, key_raw, g_key)
    d_key_raw, d_g_key = key_back(d_both[..., :HD])
    d_packed = (
        jnp.stack([d_query_raw, d_key_raw, d_both[..., HD:]], axis=2)
        .reshape(HALF, heads * 3 * HD)
        .astype(BF)
    )
    d_inputs = scatter_tokens(mult_right(d_packed, qkv_all))
    d_qkv = weight_grad(wide_one, d_packed)
    qkv_part = summed_over_latents(d_qkv)
    d_shift_part = jnp.sum(d_inputs, axis=0)
    back_one, d_g_one, d_b_one = norm_backward(d_inputs, scaled_one, rstd_one, gain_one)
    grad_one = grad_two + back_one

    wide_one_grad = gather_tokens((grad_one + settled(up_part) + settled(four_part)).astype(BF))
    d_joined = mult(wide_one_grad, skip_all)
    d_skip = weight_grad(wide_one_grad, normed)
    weighted = d_joined * both_vectors[0]
    back_sums = sum_over_chips(
        jnp.stack([jnp.sum(weighted, axis=1), jnp.sum(weighted * skip_scaled, axis=1)])
    ) / (2 * D)
    back_joined = skip_rstd[:, None] * (
        weighted - back_sums[0][:, None] - skip_scaled * back_sums[1][:, None]
    )
    back_mine = back_joined[:, : 2 * width]
    back_theirs = other_core(back_joined[:, 2 * width :])
    unturn = (CHIPS - chip) % CHIPS * PIECE
    back_mine = turned(back_mine, unturn)
    back_theirs = turned(back_theirs, unturn)
    back_tokens = lax.dynamic_slice_in_dim(
        jnp.concatenate([back_mine, back_theirs, back_mine], axis=0), core * HALF, SEQ, 0
    )
    d_hidden = back_tokens[:, :width]
    d_skipped = back_tokens[:, width:]
    skip_grads = jnp.stack([jnp.sum(d_joined * skip_scaled, axis=0), jnp.sum(d_joined, axis=0)])
    skip_grads = skip_grads[:, : 2 * width] + other_core(skip_grads[:, 2 * width :])

    norm_grads = jnp.stack([d_g_one, d_b_one, d_g_three, d_b_three, d_g_two, d_b_two])
    norm_grads = jnp.transpose(norm_grads.reshape(6, 8, width), (1, 0, 2)).reshape(8, 6 * width)
    shift_grads = jnp.repeat(d_shift_part.reshape(2, D // 2), 4, axis=0)
    shared = jnp.concatenate([d_g_query, d_g_key, d_g_cquery, d_g_ckey, sse_local[None]])
    small = jnp.concatenate(
        [norm_grads, shift_grads, jnp.broadcast_to(shared[None], (8, shared.shape[0]))], axis=1
    )
    small = jnp.sum(lax.all_to_all(small, ROW_COL, 0, 0, tiled=True), axis=0)
    small = jnp.concatenate([small, skip_grads.reshape(-1)])
    small = copied_to_each(small, DP)
    latent_shift = small[:, 6 * width : 6 * width + D // 2].astype(BF)
    all_emb = copied_to_each(emb_here, DP).reshape(-1, freq_here)
    d_w_mod = mult_left(all_emb, latent_shift)
    totals = jnp.sum(small, axis=0)
    d_g_one, d_b_one, d_g_three, d_b_three, d_g_two, d_b_two = totals[: 6 * width].reshape(6, width)
    shared = totals[6 * width + D // 2 :]
    d_g_query, d_g_key, d_g_cquery, d_g_ckey = shared[: 4 * HD].reshape(4, HD)
    loss = shared[4 * HD] / (count * D)
    d_g_skip, d_b_skip = shared[4 * HD + 1 :].reshape(2, 2, width)

    w_up_grads = spread_over_latents(up_part, row)
    w_down_grads = spread_over_latents(down_part, row)
    four_grads = spread_over_latents(four_part, row)
    w_qkv_grads = spread_over_latents(qkv_part, row)
    w_skip_grads = spread_over_latents(summed_over_latents(d_skip), row, False)

    def columns(summed, start, count):
        n = summed.shape[1] // 2
        return jnp.concatenate(
            [summed[:, start : start + count], summed[:, n + start : n + start + count]], axis=1
        ).astype(F32)

    d_w_up = w_up_grads.astype(F32)
    d_w_down = w_down_grads.T.astype(F32)
    d_w_out = columns(four_grads, 0, width).T
    d_w_cquery = columns(four_grads, width, width)
    d_w_cout = columns(four_grads, 2 * width, width).T
    d_w_ckv = columns(four_grads, 3 * width, 2 * width)
    d_w_ckv = d_w_ckv.reshape(count_blocks, -1, 4 * width)[:, : w_ckv.shape[0] // count_blocks]
    d_w_ckv = d_w_ckv.reshape(-1, 4 * width)
    d_w_qkv = w_qkv_grads.astype(F32)
    d_w_skip = jnp.transpose(
        w_skip_grads.astype(F32).reshape(D // 2, 2, 2, width), (2, 1, 3, 0)
    ).reshape(2, 2 * width, D // 2)
    return (
        output,
        d_hidden,
        d_skipped,
        d_w_skip,
        d_g_skip,
        d_b_skip,
        d_w_mod,
        d_g_one,
        d_b_one,
        d_w_qkv,
        d_g_query,
        d_g_key,
        d_w_out,
        d_g_three,
        d_b_three,
        d_w_cquery,
        d_w_ckv,
        d_g_cquery,
        d_g_ckey,
        d_w_cout,
        d_g_two,
        d_b_two,
        d_w_up,
        d_w_down,
        loss,
    )


def solution(mesh):
    side = math.isqrt(mesh.shape["dp"])
    split = Mesh(
        mesh.devices.reshape(side, side, mesh.shape["row"], 2, 2),
        ("dp_0", "dp_1", "row", "col_0", "col_1"),
    )
    in_specs = (
        P(DP, COL_ROW),
        P(DP, COL_ROW),
        P(DP, None, ROW_COL),
        P(DP, ROW_COL),
        P(DP),
        P(DP),
        P(None, DP),
        P(None, COL, "row"),
        P(None, COL_ROW),
        P(None, COL_ROW),
        P(COL, "row"),
        P(ROW_COL),
        P(ROW_COL),
        P("row", COL),
        P(),
        P(),
        P(COL, "row"),
        P(ROW_COL),
        P(ROW_COL),
        P("row", COL),
        P("row", COL),
        P(),
        P(),
        P(COL, "row"),
        P(ROW_COL),
        P(ROW_COL),
        P("row", COL),
        P(COL, "row"),
    )
    out_specs = (
        P(DP, ROW_COL),
        P(DP, COL_ROW),
        P(DP, COL_ROW),
        P(None, COL, "row"),
        P(None, COL_ROW),
        P(None, COL_ROW),
        P(COL, "row"),
        P(ROW_COL),
        P(ROW_COL),
        P("row", COL),
        P(),
        P(),
        P(COL, "row"),
        P(ROW_COL),
        P(ROW_COL),
        P("row", COL),
        P("row", COL),
        P(),
        P(),
        P(COL, "row"),
        P(ROW_COL),
        P(ROW_COL),
        P("row", COL),
        P(COL, "row"),
        P(),
    )
    return jax.shard_map(local, mesh=split, in_specs=in_specs, out_specs=out_specs, check_vma=False)
```

```python
from functools import partial
import math

import jax
import jax.numpy as jnp
from jax import lax
from jax.sharding import Mesh
from jax.sharding import PartitionSpec as P

D = 1408
HEADS = 16
HD = 88
FREQ = 256
TXT = 333
SEQ = 1024
LINE = ("row", "col_0")
CORE = "col_1"
COL = ("col_0", "col_1")
ROW_COL = ("row", "col_0", "col_1")
DP = ("dp_0", "dp_1")
ALL = ("dp_0", "dp_1", "row", "col_0", "col_1")
COL_ROW = ("col_0", "col_1", "row")
CHIPS = 4
HALF = SEQ // 2
PIECE = HALF // CHIPS
BF = jnp.bfloat16
F32 = jnp.float32


epsilon = 1e-06


def mult(left, right):
    return jnp.dot(left, right, preferred_element_type=jnp.float32)


def mult_left(left, right):
    return lax.dot_general(
        left, right, (((0,), (0,)), ((), ())), preferred_element_type=jnp.float32
    )


def mult_right(left, right):
    return lax.dot_general(
        left, right, (((1,), (1,)), ((), ())), preferred_element_type=jnp.float32
    )


def from_chip(value, ahead):
    return lax.ppermute(value, LINE, [(i, (i - ahead) % CHIPS) for i in range(CHIPS)])


def other_core(value):
    return lax.ppermute(value, CORE, [(0, 1), (1, 0)])


def other_row(value):
    return lax.ppermute(value, "row", [(0, 1), (1, 0)])


def gather_tokens(piece):
    return jnp.concatenate([piece] + [from_chip(piece, j) for j in range(1, CHIPS)], axis=0)


def scatter_tokens(partial_sums):
    total = partial_sums[:PIECE]
    for j in range(1, CHIPS):
        sent = partial_sums[j * PIECE : (j + 1) * PIECE].astype(BF)
        total = total + from_chip(sent, CHIPS - j).astype(F32)
    return total


def sum_over_chips(value):
    total = value
    for j in range(1, CHIPS):
        total = total + jnp.roll(from_chip(value, j), j * PIECE, axis=1)
    return total


def turned(value, start):
    twice = jnp.concatenate([value, value], axis=0)
    return lax.dynamic_slice_in_dim(twice, start, value.shape[0], 0)


def norm_forward(values, gain, offset):
    mean = jnp.mean(values, axis=1, keepdims=True)
    spread = jnp.mean(values * values, axis=1, keepdims=True) - mean * mean
    rstd = lax.rsqrt(spread + epsilon)
    scaled = (values - mean) * rstd
    return (scaled * gain + offset, scaled, rstd)


def norm_backward(grad, scaled, rstd, gain):
    weighted = grad * gain
    first = jnp.mean(weighted, axis=1, keepdims=True)
    second = jnp.mean(weighted * scaled, axis=1, keepdims=True)
    back = rstd * (weighted - first - scaled * second)
    return (back, jnp.sum(grad * scaled, axis=0), jnp.sum(grad, axis=0))


def halves_swapped(weight, dim, row):
    kept = lax.dynamic_slice_in_dim(weight, row * (weight.shape[dim] // 2), weight.shape[dim] // 2, dim)
    sent = lax.dynamic_slice_in_dim(
        weight, (1 - row) * (weight.shape[dim] // 2), weight.shape[dim] // 2, dim
    )
    return (kept, other_row(sent))


def in_row_order(kept, received, dim, row):
    three = jnp.concatenate([received, kept, received], axis=dim)
    return lax.dynamic_slice_in_dim(
        three, (1 - row) * kept.shape[dim], 2 * kept.shape[dim], dim
    )


def settled(value):
    return jnp.minimum(jnp.abs(value[(0,) * value.ndim].astype(F32)), 0.0)


def copied_to_each(value, axis):
    length = lax.axis_size(axis)
    return lax.all_to_all(
        jnp.broadcast_to(value[None], (length, *value.shape)), axis, 0, 0, tiled=True
    )


def with_other_core(own):
    return jnp.concatenate([own, other_core(own)], axis=1)


def whole_columns(weight, row):
    kept, received = halves_swapped(weight, 1, row)
    return in_row_order(kept, received, 0, row)


def padded(value):
    return jnp.pad(value, ((0, 0), (0, -value.shape[1] % 128)))


def blocks_by_latents(blocks, row):
    half = lax.axis_size(DP) // 2
    kept, sent = [], []
    for block in blocks:
        n = block.shape[1] // 2
        kept.append(padded(lax.dynamic_slice_in_dim(block, row * n, n, 1)))
        sent.append(padded(lax.dynamic_slice_in_dim(block, (1 - row) * n, n, 1)))
    kept = jnp.concatenate(kept, axis=1) if len(kept) > 1 else kept[0]
    sent = jnp.concatenate(sent, axis=1) if len(sent) > 1 else sent[0]
    return jnp.where(lax.axis_index(DP) // half == row, kept, other_row(sent))


def block_of_rows(weight):
    half = lax.axis_size(DP) // 2
    rows = weight.shape[0] // half
    return lax.dynamic_slice_in_dim(weight, lax.axis_index(DP) % half * rows, rows, 0)


def block_of_columns(weight):
    half = lax.axis_size(DP) // 2
    columns = weight.shape[1] // half
    return lax.dynamic_slice_in_dim(weight, lax.axis_index(DP) % half * columns, columns, 1).T


def weight_grads(pairs):
    def products(part):
        outs = []
        for left, right in pairs:
            n = right.shape[1] // 2
            out = mult_left(left, right[:, part * n : (part + 1) * n])
            short = pairs[0][0].shape[1] - out.shape[0]
            if short:
                count = 2 * max(lax.axis_size(DP) // 2, 1)
                out = out.reshape(count, -1, n)
                out = jnp.pad(out, ((0, 0), (0, short // count), (0, 0))).reshape(-1, n)
            outs.append(out)
        return jnp.concatenate(outs, axis=1) if len(outs) > 1 else outs[0]

    theirs = other_core(products(1).astype(BF))
    return (products(0) + theirs.astype(F32)).astype(BF)


def summed_over_latents(grads):
    count = lax.axis_size(DP)
    if count == 1:
        return grads
    rows, n = grads.shape
    arrived = lax.all_to_all(grads.reshape(count, rows // count, n), DP, 0, 0, tiled=True)
    part = jnp.sum(arrived.astype(F32), axis=0).astype(BF)
    half = count // 2
    pairs = []
    for i in range(count):
        for r in range(2):
            stays = i // half == r
            pairs.append((2 * i + r, 2 * i + r if stays else 2 * ((i + half) % count) + 1 - r))
    return lax.ppermute(part, DP + ("row",), pairs)


def spread_over_latents(part, row, gather=True):
    count = lax.axis_size(DP)
    if count == 1:
        kept, received = halves_swapped(part, 0, row)
        return in_row_order(kept, received, 1, row)
    rows, n = part.shape
    if gather:
        spread = lax.all_gather(part, DP, axis=0)
    else:
        spread = copied_to_each(part, DP)
    spread = spread.reshape(2, count // 2 * rows, n)
    return jnp.concatenate([spread[0], spread[1]], axis=1)


def head_norm(values, gain):
    mean = jnp.mean(values, axis=-1, keepdims=True)
    spread = jnp.mean(values * values, axis=-1, keepdims=True) - mean * mean
    return (values - mean) * lax.rsqrt(spread + epsilon) * gain


def rotate(values):
    quarter = values.shape[-1] // 4
    return jnp.concatenate(
        [
            -values[..., quarter : 2 * quarter],
            values[..., :quarter],
            -values[..., 3 * quarter :],
            values[..., 2 * quarter : 3 * quarter],
        ],
        axis=-1,
    )


def qk_prep(raw, gain, cosine, sine):
    normal = head_norm(raw, gain)
    return normal * cosine + rotate(normal) * sine


def gelu_tanh(values):
    return jax.nn.gelu(values, approximate=True)


def rope_tables(positions):
    quarter = HD // 4
    freqs = jnp.exp(-math.log(10000.0) * jnp.arange(quarter, dtype=jnp.float32) / quarter)
    rows_angle = positions[0].astype(jnp.float32)[:, None] * freqs[None, :]
    cols_angle = positions[1].astype(jnp.float32)[:, None] * freqs[None, :]
    cosine = jnp.concatenate(
        [jnp.cos(rows_angle), jnp.cos(rows_angle), jnp.cos(cols_angle), jnp.cos(cols_angle)], axis=1
    )
    sine = jnp.concatenate(
        [jnp.sin(rows_angle), jnp.sin(rows_angle), jnp.sin(cols_angle), jnp.sin(cols_angle)], axis=1
    )
    return (cosine, sine)


def time_embed(steps):
    half = FREQ // 2
    freqs = jnp.exp(-math.log(10000.0) * jnp.arange(half, dtype=jnp.float32) / half)
    angles = steps.astype(jnp.float32)[:, None] * freqs[None, :]
    return jnp.concatenate([jnp.cos(angles), jnp.sin(angles)], axis=1)


def attend_forward(query, keys, values):
    scale = HD ** (-0.5)
    length = query.shape[1]
    block = min(512, length)
    outputs = []
    totals = []
    for start in range(0, length, block):
        piece = query[:, start : start + block]
        scores = scale * jnp.einsum(
            "lqhd,lkhd->lhqk", piece, keys, preferred_element_type=jnp.float32
        )
        top = jnp.max(scores, axis=-1, keepdims=True)
        expo = jnp.exp(scores - top)
        summed = jnp.sum(expo, axis=-1, keepdims=True)
        weights = expo / summed
        totals.append(top[..., 0] + jnp.log(summed[..., 0]))
        outputs.append(
            jnp.einsum(
                "lhqk,lkhd->lqhd",
                weights.astype(jnp.bfloat16),
                values,
                preferred_element_type=jnp.float32,
            )
        )
    return (jnp.concatenate(outputs, axis=1), jnp.concatenate(totals, axis=2))


def attend_backward(query, keys, values, totals, grad_out):
    scale = HD ** (-0.5)
    length = query.shape[1]
    block = min(512, length)
    d_keys = jnp.zeros(keys.shape, jnp.float32)
    d_values = jnp.zeros(values.shape, jnp.float32)
    d_query = []
    for start in range(0, length, block):
        piece = query[:, start : start + block]
        grad_piece = grad_out[:, start : start + block]
        scores = scale * jnp.einsum(
            "lqhd,lkhd->lhqk", piece, keys, preferred_element_type=jnp.float32
        )
        weights = jnp.exp(scores - totals[:, :, start : start + block, None])
        d_weights = jnp.einsum(
            "lqhd,lkhd->lhqk", grad_piece, values, preferred_element_type=jnp.float32
        )
        d_scores = weights * (d_weights - jnp.sum(d_weights * weights, axis=-1, keepdims=True))
        d_scores_b = d_scores.astype(jnp.bfloat16)
        d_query.append(
            scale
            * jnp.einsum("lhqk,lkhd->lqhd", d_scores_b, keys, preferred_element_type=jnp.float32)
        )
        d_keys = d_keys + scale * jnp.einsum(
            "lhqk,lqhd->lkhd", d_scores_b, piece, preferred_element_type=jnp.float32
        )
        d_values = d_values + jnp.einsum(
            "lhqk,lqhd->lkhd",
            weights.astype(jnp.bfloat16),
            grad_piece,
            preferred_element_type=jnp.float32,
        )
    return (jnp.concatenate(d_query, axis=1), d_keys, d_values)


def local(
    hidden,
    skipped,
    text,
    teacher,
    valid,
    steps,
    positions,
    w_skip,
    g_skip,
    b_skip,
    w_mod,
    g_one,
    b_one,
    w_qkv,
    g_query,
    g_key,
    w_out,
    g_three,
    b_three,
    w_cquery,
    w_ckv,
    g_cquery,
    g_ckey,
    w_cout,
    g_two,
    b_two,
    w_up,
    w_down,
):
    row = lax.axis_index("row")
    chip = lax.axis_index(LINE)
    core = lax.axis_index(CORE)
    width = hidden.shape[1]
    turn = chip * PIECE
    heads_own = HEADS // (2 * CHIPS)
    heads = 2 * heads_own
    shape_four = (1, HALF, heads, HD)

    def own_tokens(values):
        return turned(lax.dynamic_slice_in_dim(values, core * HALF, HALF, 0), turn)

    def other_tokens(values):
        return turned(lax.dynamic_slice_in_dim(values, (1 - core) * HALF, HALF, 0), turn)

    skip_two = jnp.transpose(w_skip.reshape(2, 2, width, D // 2), (3, 1, 0, 2)).reshape(
        D // 2, 4 * width
    )
    skip_own = whole_columns(skip_two, row)
    skip_other = other_core(skip_own)
    skip_all = jnp.concatenate([skip_own, skip_other], axis=1)
    if lax.axis_size(DP) == 1:
        qkv_all = with_other_core(whole_columns(w_qkv, row))
        out_all = with_other_core(whole_columns(w_out.T, row))
        cquery_all = with_other_core(whole_columns(w_cquery, row))
        cout_all = with_other_core(whole_columns(w_cout.T, row))
        ckv_all = with_other_core(whole_columns(w_ckv, row))
        up_all = with_other_core(whole_columns(w_up, row))
        down_all = with_other_core(whole_columns(w_down.T, row))
    else:
        qkv_block = blocks_by_latents([block_of_rows(w_qkv)], row)
        qkv_own = copied_to_each(qkv_block, DP).reshape(D, -1)[:, : 3 * width]
        ckv_block = block_of_rows(w_ckv)
        ckv_rows = ckv_block.shape[0]
        ckv_block = jnp.pad(ckv_block, ((0, D // lax.axis_size(DP) - ckv_rows), (0, 0)))
        four_block = blocks_by_latents(
            [
                block_of_columns(w_out),
                block_of_rows(w_cquery),
                block_of_columns(w_cout),
                ckv_block,
            ],
            row,
        )
        four_own = lax.all_gather(four_block, DP, axis=0, tiled=True)
        two_block = blocks_by_latents([block_of_rows(w_up), block_of_columns(w_down)], row)
        two_block = two_block + settled(four_own).astype(BF)
        two_own = lax.all_gather(two_block, DP, axis=0, tiled=True)
        qkv_all = with_other_core(qkv_own)
        four_other = other_core(four_own)

        def both(start, count):
            return jnp.concatenate(
                [four_own[:, start : start + count], four_other[:, start : start + count]], axis=1
            )

        step = width + (-width) % 128
        out_all = both(0, width)
        cquery_all = both(step, width)
        cout_all = both(2 * step, width)
        ckv_all = both(3 * step, 2 * width).reshape(lax.axis_size(DP), -1, 4 * width)
        ckv_all = ckv_all[:, :ckv_rows].reshape(-1, 4 * width)
        two_other = other_core(two_own)
        hidden_own = two_own.shape[1] // 2
        up_all = jnp.concatenate([two_own[:, :hidden_own], two_other[:, :hidden_own]], axis=1)
        down_all = jnp.concatenate([two_own[:, hidden_own:], two_other[:, hidden_own:]], axis=1)

    freq_here = w_mod.shape[0]
    mask_all = valid.astype(F32)
    tallies = jnp.stack([jnp.sum(mask_all), steps[0].astype(F32)])
    tallies = copied_to_each(jnp.pad(tallies[None], ((0, 0), (0, 126))), DP)[:, 0]
    count = jnp.sum(tallies[:, 0])
    all_emb = lax.dynamic_slice_in_dim(
        time_embed(tallies[:, 1]).astype(BF), lax.axis_index(COL) * freq_here, freq_here, 1
    )
    emb = time_embed(steps).astype(BF)
    emb_here = lax.dynamic_slice_in_dim(emb, lax.axis_index(COL) * freq_here, freq_here, 1)
    shift_part = mult(emb_here, w_mod)
    vectors = jnp.concatenate(
        [jnp.stack([g_one, b_one, g_three, b_three, g_two, b_two]).reshape(-1), shift_part[0]]
    )
    gathered = copied_to_each(vectors, ROW_COL)
    gains = jnp.transpose(gathered[:, : 6 * width].reshape(8, 6, width), (1, 0, 2)).reshape(6, D)
    gain_one, offset_one, gain_three, offset_three, gain_two, offset_two = gains
    shift = jnp.sum(gathered[:, 6 * width :].reshape(2, 4, D // 2), axis=1).reshape(D)
    mask = lax.dynamic_slice_in_dim(mask_all, core * HALF + turn, PIECE, 0)

    teacher_blocks = jnp.transpose(
        teacher.reshape(2, CHIPS, PIECE, width), (1, 0, 2, 3)
    ).reshape(2 * CHIPS, PIECE, width)
    teacher_here = jnp.transpose(
        lax.all_to_all(teacher_blocks, ROW_COL, 0, 0, tiled=True), (1, 0, 2)
    ).reshape(PIECE, D)

    wide_text = jnp.transpose(copied_to_each(text[0], ROW_COL), (1, 0, 2)).reshape(TXT, -1)

    cosine, sine = rope_tables(own_tokens(positions.T).T)
    prep = partial(qk_prep, cosine=cosine[:, None, :], sine=sine[:, None, :])

    joined = jnp.concatenate([hidden, skipped], axis=1)
    mine = own_tokens(joined)
    theirs = other_core(other_tokens(joined))
    pairs = jnp.concatenate([mine, theirs], axis=1).astype(F32)
    skip_vectors = jnp.stack([g_skip, b_skip]).reshape(2, 2 * width)
    both_vectors = jnp.concatenate([skip_vectors, other_core(skip_vectors)], axis=1)
    skip_sums = sum_over_chips(jnp.stack([jnp.sum(pairs, axis=1), jnp.sum(pairs * pairs, axis=1)]))
    skip_mean = skip_sums[0] / (2 * D)
    skip_rstd = lax.rsqrt(skip_sums[1] / (2 * D) - skip_mean * skip_mean + epsilon)
    skip_scaled = (pairs - skip_mean[:, None]) * skip_rstd[:, None]
    normed = (skip_scaled * both_vectors[0] + both_vectors[1]).astype(BF)
    stream = scatter_tokens(mult_right(normed, skip_all))

    normed_one, scaled_one, rstd_one = norm_forward(stream, gain_one, offset_one)
    wide_one = gather_tokens((normed_one + shift).astype(BF))
    packed = mult(wide_one, qkv_all).reshape(HALF, heads, 3, HD)
    query_raw = packed[:, :, 0]
    key_raw = packed[:, :, 1]
    query = prep(query_raw, g_query).astype(BF).reshape(shape_four)
    keys_here = prep(key_raw, g_key).astype(BF)
    values_here = packed[:, :, 2].astype(BF)

    def swapped_heads(values):
        return jnp.concatenate([values[:, heads_own:], values[:, :heads_own]], axis=1)

    key_values = other_core(swapped_heads(jnp.concatenate([keys_here, values_here], axis=2)))
    keys = jnp.concatenate([keys_here, key_values[..., :HD]], axis=0)[None]
    values = jnp.concatenate([values_here, key_values[..., HD:]], axis=0)[None]
    mixed, self_totals = attend_forward(query, keys, values)
    mixed_here = mixed.reshape(HALF, heads * HD).astype(BF)
    stream_two = stream + scatter_tokens(mult_right(mixed_here, out_all))

    normed_three, scaled_three, rstd_three = norm_forward(stream_two, gain_three, offset_three)
    wide_three = gather_tokens(normed_three.astype(BF))
    cquery_raw = mult(wide_three, cquery_all).reshape(HALF, heads, HD)
    cquery = prep(cquery_raw, g_cquery).astype(BF).reshape(shape_four)
    ckv = mult(wide_text, ckv_all).reshape(1, TXT, heads, 2, HD)
    ckey_raw = ckv[:, :, :, 0]
    ckeys = head_norm(ckey_raw, g_ckey).astype(BF)
    cvalues = ckv[:, :, :, 1].astype(BF)
    cmixed, cross_totals = attend_forward(cquery, ckeys, cvalues)
    cmixed_here = cmixed.reshape(HALF, heads * HD).astype(BF)
    stream_three = stream_two + scatter_tokens(mult_right(cmixed_here, cout_all))

    normed_two, scaled_two, rstd_two = norm_forward(stream_three, gain_two, offset_two)
    wide_two = gather_tokens(normed_two.astype(BF))
    upper = mult(wide_two, up_all)
    active, gelu_back = jax.vjp(gelu_tanh, upper)
    active_here = active.astype(BF)
    output_here = stream_three + scatter_tokens(mult_right(active_here, down_all))

    diff = output_here - teacher_here.astype(F32)
    sse_local = jnp.sum(mask[:, None] * diff * diff)
    factor = 32.0 * lax.axis_size(DP) / count
    grad_out = factor * mask[:, None] * diff
    output_blocks = jnp.transpose(
        output_here.astype(BF).reshape(PIECE, 2 * CHIPS, width), (1, 0, 2)
    )
    output_back = lax.all_to_all(output_blocks, ROW_COL, 0, 0, tiled=True)
    output = jnp.transpose(
        output_back.reshape(CHIPS, 2, PIECE, width), (1, 0, 2, 3)
    ).reshape(SEQ, width).astype(F32)

    wide_grad = gather_tokens(grad_out.astype(BF))
    d_upper = gelu_back(mult(wide_grad, down_all))[0].astype(BF)
    d_normed_two = scatter_tokens(mult_right(d_upper, up_all))
    two_part = summed_over_latents(
        weight_grads([(wide_two, d_upper), (wide_grad, active_here)])
    )
    back_two, d_g_two, d_b_two = norm_backward(d_normed_two, scaled_two, rstd_two, gain_two)
    grad_three = grad_out + back_two

    wide_three_grad = gather_tokens(grad_three.astype(BF))
    d_cmixed = mult(wide_three_grad, cout_all).astype(BF).reshape(shape_four)
    d_cquery, d_ckeys, d_cvalues = attend_backward(cquery, ckeys, cvalues, cross_totals, d_cmixed)
    unused, cquery_back = jax.vjp(prep, cquery_raw, g_cquery)
    d_cquery_raw, d_g_cquery = cquery_back(d_cquery.reshape(HALF, heads, HD))
    d_cquery_here = d_cquery_raw.reshape(HALF, heads * HD).astype(BF)
    d_normed_three = scatter_tokens(mult_right(d_cquery_here, cquery_all))
    unused, ckey_back = jax.vjp(head_norm, ckey_raw, g_ckey)
    d_ckey_raw, d_g_ckey = ckey_back(d_ckeys)
    d_ckv = jnp.stack([d_ckey_raw, d_cvalues], axis=3).reshape(TXT, heads * 2 * HD).astype(BF)
    back_three, d_g_three, d_b_three = norm_backward(
        d_normed_three, scaled_three, rstd_three, gain_three
    )
    grad_two = grad_three + back_three

    wide_two_grad = gather_tokens(grad_two.astype(BF))
    d_mixed = mult(wide_two_grad, out_all) + settled(two_part)
    d_mixed = d_mixed.astype(BF).reshape(shape_four)
    d_query, d_keys, d_values = attend_backward(query, keys, values, self_totals, d_mixed)
    d_both = jnp.concatenate([d_keys[0], d_values[0]], axis=2)
    d_both = d_both[:HALF] + other_core(swapped_heads(d_both[HALF:]).astype(BF)).astype(F32)
    unused, query_back = jax.vjp(prep, query_raw, g_query)
    d_query_raw, d_g_query = query_back(d_query.reshape(HALF, heads, HD))
    unused, key_back = jax.vjp(prep, key_raw, g_key)
    d_key_raw, d_g_key = key_back(d_both[..., :HD])
    d_packed = (
        jnp.stack([d_query_raw, d_key_raw, d_both[..., HD:]], axis=2)
        .reshape(HALF, heads * 3 * HD)
        .astype(BF)
    )
    d_inputs = scatter_tokens(mult_right(d_packed, qkv_all))
    four_grads = weight_grads(
        [
            (wide_two_grad, mixed_here),
            (wide_three, d_cquery_here),
            (wide_three_grad, cmixed_here),
            (wide_text, d_ckv),
        ]
    )
    four_part = summed_over_latents(four_grads)
    qkv_part = summed_over_latents(weight_grads([(wide_one, d_packed)]))
    d_inputs = d_inputs + settled(four_grads)
    d_shift_part = jnp.sum(d_inputs, axis=0)
    back_one, d_g_one, d_b_one = norm_backward(d_inputs, scaled_one, rstd_one, gain_one)
    grad_one = grad_two + back_one

    wide_one_grad = gather_tokens(grad_one.astype(BF))
    d_skip = weight_grads([(wide_one_grad, normed)])
    skip_part = summed_over_latents(d_skip)
    d_joined = mult(wide_one_grad, skip_all)
    both_gains = both_vectors[0] + settled(d_skip) + settled(four_part)
    weighted = d_joined * both_gains
    back_sums = sum_over_chips(
        jnp.stack([jnp.sum(weighted, axis=1), jnp.sum(weighted * skip_scaled, axis=1)])
    ) / (2 * D)
    back_joined = skip_rstd[:, None] * (
        weighted - back_sums[0][:, None] - skip_scaled * back_sums[1][:, None]
    )
    back_mine = back_joined[:, : 2 * width]
    back_theirs = other_core(back_joined[:, 2 * width :])
    unturn = (CHIPS - chip) % CHIPS * PIECE
    back_mine = turned(back_mine, unturn)
    back_theirs = turned(back_theirs, unturn)
    back_tokens = lax.dynamic_slice_in_dim(
        jnp.concatenate([back_mine, back_theirs, back_mine], axis=0), core * HALF, SEQ, 0
    )
    d_hidden = back_tokens[:, :width]
    d_skipped = back_tokens[:, width:]
    skip_grads = jnp.stack([jnp.sum(d_joined * skip_scaled, axis=0), jnp.sum(d_joined, axis=0)])
    skip_grads = skip_grads[:, : 2 * width] + other_core(skip_grads[:, 2 * width :])

    norm_grads = jnp.stack([d_g_one, d_b_one, d_g_three, d_b_three, d_g_two, d_b_two])
    norm_grads = jnp.transpose(norm_grads.reshape(6, 8, width), (1, 0, 2)).reshape(8, 6 * width)
    shift_grads = jnp.repeat(d_shift_part.reshape(2, D // 2), 4, axis=0)
    shared = jnp.concatenate([d_g_query, d_g_key, d_g_cquery, d_g_ckey, sse_local[None]])
    small = jnp.concatenate(
        [norm_grads, shift_grads, jnp.broadcast_to(shared[None], (8, shared.shape[0]))], axis=1
    )
    small = jnp.sum(lax.all_to_all(small, ROW_COL, 0, 0, tiled=True), axis=0)
    small = jnp.concatenate([small, skip_grads.reshape(-1)])
    small = copied_to_each(small, DP)
    latent_shift = small[:, 6 * width : 6 * width + D // 2].astype(BF)
    d_w_mod = mult_left(all_emb, latent_shift)
    totals = jnp.sum(small, axis=0)
    d_g_one, d_b_one, d_g_three, d_b_three, d_g_two, d_b_two = totals[: 6 * width].reshape(6, width)
    shared = totals[6 * width + D // 2 :]
    d_g_query, d_g_key, d_g_cquery, d_g_ckey = shared[: 4 * HD].reshape(4, HD)
    loss = shared[4 * HD] / (count * D)
    d_g_skip, d_b_skip = shared[4 * HD + 1 :].reshape(2, 2, width)

    two_grads = spread_over_latents(two_part, row)
    four_grads = spread_over_latents(four_part, row)
    last_grads = spread_over_latents(jnp.concatenate([qkv_part, skip_part], axis=1), row, False)

    def columns(summed, start, count):
        n = summed.shape[1] // 2
        return jnp.concatenate(
            [summed[:, start : start + count], summed[:, n + start : n + start + count]], axis=1
        ).astype(F32)

    n_up = w_up.shape[1] // 2
    d_w_up = columns(two_grads, 0, n_up)
    d_w_down = columns(two_grads, n_up, n_up).T
    d_w_out = columns(four_grads, 0, width).T
    d_w_cquery = columns(four_grads, width, width)
    d_w_cout = columns(four_grads, 2 * width, width).T
    d_w_ckv = columns(four_grads, 3 * width, 2 * width)
    count_blocks = max(lax.axis_size(DP) // 2, 1)
    d_w_ckv = d_w_ckv.reshape(count_blocks, -1, 4 * width)[:, : w_ckv.shape[0] // count_blocks]
    d_w_ckv = d_w_ckv.reshape(-1, 4 * width)
    d_w_qkv = columns(last_grads, 0, 3 * width)
    d_w_skip = columns(last_grads, 3 * width, 2 * width).reshape(D // 2, 2, 2, width)
    d_w_skip = jnp.transpose(d_w_skip, (2, 1, 3, 0)).reshape(2, 2 * width, D // 2)
    return (
        output,
        d_hidden,
        d_skipped,
        d_w_skip,
        d_g_skip,
        d_b_skip,
        d_w_mod,
        d_g_one,
        d_b_one,
        d_w_qkv,
        d_g_query,
        d_g_key,
        d_w_out,
        d_g_three,
        d_b_three,
        d_w_cquery,
        d_w_ckv,
        d_g_cquery,
        d_g_ckey,
        d_w_cout,
        d_g_two,
        d_b_two,
        d_w_up,
        d_w_down,
        loss,
    )


def solution(mesh):
    side = math.isqrt(mesh.shape["dp"])
    split = Mesh(
        mesh.devices.reshape(side, side, mesh.shape["row"], 2, 2),
        ("dp_0", "dp_1", "row", "col_0", "col_1"),
    )
    in_specs = (
        P(DP, COL_ROW),
        P(DP, COL_ROW),
        P(DP, None, ROW_COL),
        P(DP, ROW_COL),
        P(DP),
        P(DP),
        P(None, DP),
        P(None, COL, "row"),
        P(None, COL_ROW),
        P(None, COL_ROW),
        P(COL, "row"),
        P(ROW_COL),
        P(ROW_COL),
        P("row", COL),
        P(),
        P(),
        P(COL, "row"),
        P(ROW_COL),
        P(ROW_COL),
        P("row", COL),
        P("row", COL),
        P(),
        P(),
        P(COL, "row"),
        P(ROW_COL),
        P(ROW_COL),
        P("row", COL),
        P(COL, "row"),
    )
    out_specs = (
        P(DP, ROW_COL),
        P(DP, COL_ROW),
        P(DP, COL_ROW),
        P(None, COL, "row"),
        P(None, COL_ROW),
        P(None, COL_ROW),
        P(COL, "row"),
        P(ROW_COL),
        P(ROW_COL),
        P("row", COL),
        P(),
        P(),
        P(COL, "row"),
        P(ROW_COL),
        P(ROW_COL),
        P("row", COL),
        P("row", COL),
        P(),
        P(),
        P(COL, "row"),
        P(ROW_COL),
        P(ROW_COL),
        P("row", COL),
        P(COL, "row"),
        P(),
    )
    return jax.shard_map(local, mesh=split, in_specs=in_specs, out_specs=out_specs, check_vma=False)
```

```python
from functools import partial
import math

import jax
import jax.numpy as jnp
from jax import lax
from jax.sharding import Mesh
from jax.sharding import PartitionSpec as P

D = 1408
HEADS = 16
HD = 88
FREQ = 256
TXT = 333
SEQ = 1024
LINE = ("row", "col_0")
CORE = "col_1"
COL = ("col_0", "col_1")
ROW_COL = ("row", "col_0", "col_1")
DP = ("dp_0", "dp_1")
ALL = ("dp_0", "dp_1", "row", "col_0", "col_1")
COL_ROW = ("col_0", "col_1", "row")
CHIPS = 4
HALF = SEQ // 2
PIECE = HALF // CHIPS
BF = jnp.bfloat16
F32 = jnp.float32


epsilon = 1e-06


def mult(left, right):
    return jnp.dot(left, right, preferred_element_type=jnp.float32)


def mult_left(left, right):
    return lax.dot_general(
        left, right, (((0,), (0,)), ((), ())), preferred_element_type=jnp.float32
    )


def mult_right(left, right):
    return lax.dot_general(
        left, right, (((1,), (1,)), ((), ())), preferred_element_type=jnp.float32
    )


def from_chip(value, ahead):
    return lax.ppermute(value, LINE, [(i, (i - ahead) % CHIPS) for i in range(CHIPS)])


def other_core(value):
    return lax.ppermute(value, CORE, [(0, 1), (1, 0)])


def other_row(value):
    return lax.ppermute(value, "row", [(0, 1), (1, 0)])


def gather_tokens(piece):
    return jnp.concatenate([piece] + [from_chip(piece, j) for j in range(1, CHIPS)], axis=0)


def scatter_tokens(partial_sums):
    total = partial_sums[:PIECE]
    for j in range(1, CHIPS):
        sent = partial_sums[j * PIECE : (j + 1) * PIECE].astype(BF)
        total = total + from_chip(sent, CHIPS - j).astype(F32)
    return total


def sum_over_chips(value):
    total = value
    for j in range(1, CHIPS):
        total = total + jnp.roll(from_chip(value, j), j * PIECE, axis=1)
    return total


def turned(value, start):
    twice = jnp.concatenate([value, value], axis=0)
    return lax.dynamic_slice_in_dim(twice, start, value.shape[0], 0)


def norm_forward(values, gain, offset):
    mean = jnp.mean(values, axis=1, keepdims=True)
    spread = jnp.mean(values * values, axis=1, keepdims=True) - mean * mean
    rstd = lax.rsqrt(spread + epsilon)
    scaled = (values - mean) * rstd
    return (scaled * gain + offset, scaled, rstd)


def norm_backward(grad, scaled, rstd, gain):
    weighted = grad * gain
    first = jnp.mean(weighted, axis=1, keepdims=True)
    second = jnp.mean(weighted * scaled, axis=1, keepdims=True)
    back = rstd * (weighted - first - scaled * second)
    return (back, jnp.sum(grad * scaled, axis=0), jnp.sum(grad, axis=0))


def halves_swapped(weight, dim, row):
    kept = lax.dynamic_slice_in_dim(weight, row * (weight.shape[dim] // 2), weight.shape[dim] // 2, dim)
    sent = lax.dynamic_slice_in_dim(
        weight, (1 - row) * (weight.shape[dim] // 2), weight.shape[dim] // 2, dim
    )
    return (kept, other_row(sent))


def in_row_order(kept, received, dim, row):
    three = jnp.concatenate([received, kept, received], axis=dim)
    return lax.dynamic_slice_in_dim(
        three, (1 - row) * kept.shape[dim], 2 * kept.shape[dim], dim
    )


def settled(value):
    return jnp.minimum(jnp.abs(value[(0,) * value.ndim].astype(F32)), 0.0)


def copied_to_each(value, axis):
    length = lax.axis_size(axis)
    return lax.all_to_all(
        jnp.broadcast_to(value[None], (length, *value.shape)), axis, 0, 0, tiled=True
    )


def in_two(value):
    high = lax.reduce_precision(value, exponent_bits=8, mantissa_bits=7)
    return jnp.concatenate([high.astype(BF), (value - high).astype(BF)], axis=0)


def with_other_core(own):
    return jnp.concatenate([own, other_core(own)], axis=1)


def whole_columns(weight, row):
    kept, received = halves_swapped(weight, 1, row)
    return in_row_order(kept, received, 0, row)


def padded(value):
    return jnp.pad(value, ((0, 0), (0, -value.shape[1] % 128)))


def blocks_by_latents(blocks, row):
    half = lax.axis_size(DP) // 2
    kept, sent = [], []
    for block in blocks:
        n = block.shape[1] // 2
        kept.append(padded(lax.dynamic_slice_in_dim(block, row * n, n, 1)))
        sent.append(padded(lax.dynamic_slice_in_dim(block, (1 - row) * n, n, 1)))
    kept = jnp.concatenate(kept, axis=1) if len(kept) > 1 else kept[0]
    sent = jnp.concatenate(sent, axis=1) if len(sent) > 1 else sent[0]
    return jnp.where(lax.axis_index(DP) // half == row, kept, other_row(sent))


def block_of_rows(weight):
    half = lax.axis_size(DP) // 2
    rows = weight.shape[0] // half
    return lax.dynamic_slice_in_dim(weight, lax.axis_index(DP) % half * rows, rows, 0)


def block_of_columns(weight):
    half = lax.axis_size(DP) // 2
    columns = weight.shape[1] // half
    return lax.dynamic_slice_in_dim(weight, lax.axis_index(DP) % half * columns, columns, 1).T


def weight_grads(pairs):
    def products(part):
        outs = []
        for left, right in pairs:
            n = right.shape[1] // 2
            out = mult_left(left, right[:, part * n : (part + 1) * n])
            short = pairs[0][0].shape[1] - out.shape[0]
            if short:
                count = 2 * max(lax.axis_size(DP) // 2, 1)
                out = out.reshape(count, -1, n)
                out = jnp.pad(out, ((0, 0), (0, short // count), (0, 0))).reshape(-1, n)
            outs.append(out)
        return jnp.concatenate(outs, axis=1) if len(outs) > 1 else outs[0]

    theirs = other_core(products(1).astype(BF))
    return (products(0) + theirs.astype(F32)).astype(BF)


def summed_over_latents(grads, start=0, pairs_of=0):
    count = lax.axis_size(DP)
    if count == 1:
        return grads
    rows, n = grads.shape
    arrived = lax.all_to_all(grads.reshape(count, rows // count, n), DP, 0, 0, tiled=True)
    part = jnp.sum(arrived.astype(F32), axis=0)
    if pairs_of:
        exact = part[:, start : start + pairs_of] + part[:, start + pairs_of : start + 2 * pairs_of]
        rest = part[:, start + 2 * pairs_of :].astype(BF)
        part = jnp.concatenate([part[:, :start].astype(BF), in_two(exact.T).T, rest], axis=1)
    else:
        part = part.astype(BF)
    half = count // 2
    pairs = []
    for i in range(count):
        for r in range(2):
            stays = i // half == r
            pairs.append((2 * i + r, 2 * i + r if stays else 2 * ((i + half) % count) + 1 - r))
    return lax.ppermute(part, DP + ("row",), pairs)


def spread_over_latents(part, row, gather=True):
    count = lax.axis_size(DP)
    if count == 1:
        kept, received = halves_swapped(part, 0, row)
        return in_row_order(kept, received, 1, row)
    rows, n = part.shape
    if gather:
        spread = lax.all_gather(part, DP, axis=0)
    else:
        spread = copied_to_each(part, DP)
    spread = spread.reshape(2, count // 2 * rows, n)
    return jnp.concatenate([spread[0], spread[1]], axis=1)


def head_norm(values, gain):
    mean = jnp.mean(values, axis=-1, keepdims=True)
    spread = jnp.mean(values * values, axis=-1, keepdims=True) - mean * mean
    return (values - mean) * lax.rsqrt(spread + epsilon) * gain


def rotate(values):
    quarter = values.shape[-1] // 4
    return jnp.concatenate(
        [
            -values[..., quarter : 2 * quarter],
            values[..., :quarter],
            -values[..., 3 * quarter :],
            values[..., 2 * quarter : 3 * quarter],
        ],
        axis=-1,
    )


def qk_prep(raw, gain, cosine, sine):
    normal = head_norm(raw, gain)
    return normal * cosine + rotate(normal) * sine


def gelu_tanh(values):
    return jax.nn.gelu(values, approximate=True)


def rope_tables(positions):
    quarter = HD // 4
    freqs = jnp.exp(-math.log(10000.0) * jnp.arange(quarter, dtype=jnp.float32) / quarter)
    rows_angle = positions[0].astype(jnp.float32)[:, None] * freqs[None, :]
    cols_angle = positions[1].astype(jnp.float32)[:, None] * freqs[None, :]
    cosine = jnp.concatenate(
        [jnp.cos(rows_angle), jnp.cos(rows_angle), jnp.cos(cols_angle), jnp.cos(cols_angle)], axis=1
    )
    sine = jnp.concatenate(
        [jnp.sin(rows_angle), jnp.sin(rows_angle), jnp.sin(cols_angle), jnp.sin(cols_angle)], axis=1
    )
    return (cosine, sine)


def time_embed(steps):
    half = FREQ // 2
    freqs = jnp.exp(-math.log(10000.0) * jnp.arange(half, dtype=jnp.float32) / half)
    angles = steps.astype(jnp.float32)[:, None] * freqs[None, :]
    return jnp.concatenate([jnp.cos(angles), jnp.sin(angles)], axis=1)


def attend_forward(query, keys, values):
    scale = HD ** (-0.5)
    length = query.shape[1]
    block = min(512, length)
    outputs = []
    totals = []
    for start in range(0, length, block):
        piece = query[:, start : start + block]
        scores = scale * jnp.einsum(
            "lqhd,lkhd->lhqk", piece, keys, preferred_element_type=jnp.float32
        )
        top = jnp.max(scores, axis=-1, keepdims=True)
        expo = jnp.exp(scores - top)
        summed = jnp.sum(expo, axis=-1, keepdims=True)
        weights = expo / summed
        totals.append(top[..., 0] + jnp.log(summed[..., 0]))
        outputs.append(
            jnp.einsum(
                "lhqk,lkhd->lqhd",
                weights.astype(jnp.bfloat16),
                values,
                preferred_element_type=jnp.float32,
            )
        )
    return (jnp.concatenate(outputs, axis=1), jnp.concatenate(totals, axis=2))


def attend_backward(query, keys, values, totals, grad_out):
    scale = HD ** (-0.5)
    length = query.shape[1]
    block = min(512, length)
    d_keys = jnp.zeros(keys.shape, jnp.float32)
    d_values = jnp.zeros(values.shape, jnp.float32)
    d_query = []
    for start in range(0, length, block):
        piece = query[:, start : start + block]
        grad_piece = grad_out[:, start : start + block]
        scores = scale * jnp.einsum(
            "lqhd,lkhd->lhqk", piece, keys, preferred_element_type=jnp.float32
        )
        weights = jnp.exp(scores - totals[:, :, start : start + block, None])
        d_weights = jnp.einsum(
            "lqhd,lkhd->lhqk", grad_piece, values, preferred_element_type=jnp.float32
        )
        d_scores = weights * (d_weights - jnp.sum(d_weights * weights, axis=-1, keepdims=True))
        d_scores_b = d_scores.astype(jnp.bfloat16)
        d_query.append(
            scale
            * jnp.einsum("lhqk,lkhd->lqhd", d_scores_b, keys, preferred_element_type=jnp.float32)
        )
        d_keys = d_keys + scale * jnp.einsum(
            "lhqk,lqhd->lkhd", d_scores_b, piece, preferred_element_type=jnp.float32
        )
        d_values = d_values + jnp.einsum(
            "lhqk,lqhd->lkhd",
            weights.astype(jnp.bfloat16),
            grad_piece,
            preferred_element_type=jnp.float32,
        )
    return (jnp.concatenate(d_query, axis=1), d_keys, d_values)


def local(
    hidden,
    skipped,
    text,
    teacher,
    valid,
    steps,
    positions,
    w_skip,
    g_skip,
    b_skip,
    w_mod,
    g_one,
    b_one,
    w_qkv,
    g_query,
    g_key,
    w_out,
    g_three,
    b_three,
    w_cquery,
    w_ckv,
    g_cquery,
    g_ckey,
    w_cout,
    g_two,
    b_two,
    w_up,
    w_down,
):
    row = lax.axis_index("row")
    chip = lax.axis_index(LINE)
    core = lax.axis_index(CORE)
    width = hidden.shape[1]
    turn = chip * PIECE
    heads_own = HEADS // (2 * CHIPS)
    heads = 2 * heads_own
    shape_four = (1, HALF, heads, HD)

    def own_tokens(values):
        return turned(lax.dynamic_slice_in_dim(values, core * HALF, HALF, 0), turn)

    def other_tokens(values):
        return turned(lax.dynamic_slice_in_dim(values, (1 - core) * HALF, HALF, 0), turn)

    skip_two = jnp.transpose(w_skip.reshape(2, 2, width, D // 2), (3, 1, 0, 2)).reshape(
        D // 2, 4 * width
    )
    skip_own = whole_columns(skip_two, row)
    skip_other = other_core(skip_own)
    skip_all = jnp.concatenate([skip_own, skip_other], axis=1)
    qkv_all = with_other_core(whole_columns(w_qkv, row))
    if lax.axis_size(DP) == 1:
        out_all = with_other_core(whole_columns(w_out.T, row))
        cquery_all = with_other_core(whole_columns(w_cquery, row))
        cout_all = with_other_core(whole_columns(w_cout.T, row))
        ckv_all = with_other_core(whole_columns(w_ckv, row))
        up_all = with_other_core(whole_columns(w_up, row))
        down_all = with_other_core(whole_columns(w_down.T, row))
    else:
        ckv_block = block_of_rows(w_ckv)
        ckv_rows = ckv_block.shape[0]
        ckv_block = jnp.pad(ckv_block, ((0, D // lax.axis_size(DP) - ckv_rows), (0, 0)))
        four_block = blocks_by_latents(
            [
                block_of_columns(w_out),
                block_of_rows(w_cquery),
                block_of_columns(w_cout),
                ckv_block,
            ],
            row,
        )
        four_own = lax.all_gather(four_block, DP, axis=0, tiled=True)
        two_block = blocks_by_latents([block_of_rows(w_up), block_of_columns(w_down)], row)
        two_block = two_block + settled(four_own).astype(BF)
        two_own = lax.all_gather(two_block, DP, axis=0, tiled=True)
        four_other = other_core(four_own)

        def both(start, count):
            return jnp.concatenate(
                [four_own[:, start : start + count], four_other[:, start : start + count]], axis=1
            )

        step = width + (-width) % 128
        out_all = both(0, width)
        cquery_all = both(step, width)
        cout_all = both(2 * step, width)
        ckv_all = both(3 * step, 2 * width).reshape(lax.axis_size(DP), -1, 4 * width)
        ckv_all = ckv_all[:, :ckv_rows].reshape(-1, 4 * width)
        two_other = other_core(two_own)
        hidden_own = two_own.shape[1] // 2
        up_all = jnp.concatenate([two_own[:, :hidden_own], two_other[:, :hidden_own]], axis=1)
        down_all = jnp.concatenate([two_own[:, hidden_own:], two_other[:, hidden_own:]], axis=1)

    freq_here = w_mod.shape[0]
    mask_all = valid.astype(F32)
    counts = copied_to_each(jnp.broadcast_to(jnp.sum(mask_all), (1, 128)), DP)
    count = jnp.sum(counts[:, 0, 0])
    emb = time_embed(steps).astype(BF)
    emb_here = lax.dynamic_slice_in_dim(emb, lax.axis_index(COL) * freq_here, freq_here, 1)
    shift_part = mult(emb_here, w_mod)
    vectors = jnp.concatenate(
        [jnp.stack([g_one, b_one, g_three, b_three, g_two, b_two]).reshape(-1), shift_part[0]]
    )
    gathered = copied_to_each(vectors, ROW_COL)
    gains = jnp.transpose(gathered[:, : 6 * width].reshape(8, 6, width), (1, 0, 2)).reshape(6, D)
    gain_one, offset_one, gain_three, offset_three, gain_two, offset_two = gains
    shift = jnp.sum(gathered[:, 6 * width :].reshape(2, 4, D // 2), axis=1).reshape(D)
    mask = lax.dynamic_slice_in_dim(mask_all, core * HALF + turn, PIECE, 0)

    teacher_blocks = jnp.transpose(
        teacher.reshape(2, CHIPS, PIECE, width), (1, 0, 2, 3)
    ).reshape(2 * CHIPS, PIECE, width)
    teacher_here = jnp.transpose(
        lax.all_to_all(teacher_blocks, ROW_COL, 0, 0, tiled=True), (1, 0, 2)
    ).reshape(PIECE, D)

    wide_text = jnp.transpose(copied_to_each(text[0], ROW_COL), (1, 0, 2)).reshape(TXT, -1)

    cosine, sine = rope_tables(own_tokens(positions.T).T)
    prep = partial(qk_prep, cosine=cosine[:, None, :], sine=sine[:, None, :])

    joined = jnp.concatenate([hidden, skipped], axis=1)
    mine = own_tokens(joined)
    theirs = other_core(other_tokens(joined))
    pairs = jnp.concatenate([mine, theirs], axis=1).astype(F32)
    skip_vectors = jnp.stack([g_skip, b_skip]).reshape(2, 2 * width)
    both_vectors = jnp.concatenate([skip_vectors, other_core(skip_vectors)], axis=1)
    skip_sums = sum_over_chips(jnp.stack([jnp.sum(pairs, axis=1), jnp.sum(pairs * pairs, axis=1)]))
    skip_mean = skip_sums[0] / (2 * D)
    skip_rstd = lax.rsqrt(skip_sums[1] / (2 * D) - skip_mean * skip_mean + epsilon)
    skip_scaled = (pairs - skip_mean[:, None]) * skip_rstd[:, None]
    normed = (skip_scaled * both_vectors[0] + both_vectors[1]).astype(BF)
    stream = scatter_tokens(mult_right(normed, skip_all))

    normed_one, scaled_one, rstd_one = norm_forward(stream, gain_one, offset_one)
    early = settled(count) + settled(teacher_here) + settled(wide_text)
    wide_one = gather_tokens((normed_one + (shift + early)).astype(BF))
    packed = mult(wide_one, qkv_all).reshape(HALF, heads, 3, HD)
    query_raw = packed[:, :, 0]
    key_raw = packed[:, :, 1]
    query = prep(query_raw, g_query).astype(BF).reshape(shape_four)
    keys_here = prep(key_raw, g_key).astype(BF)
    values_here = packed[:, :, 2].astype(BF)

    def swapped_heads(values):
        return jnp.concatenate([values[:, heads_own:], values[:, :heads_own]], axis=1)

    key_values = other_core(swapped_heads(jnp.concatenate([keys_here, values_here], axis=2)))
    keys = jnp.concatenate([keys_here, key_values[..., :HD]], axis=0)[None]
    values = jnp.concatenate([values_here, key_values[..., HD:]], axis=0)[None]
    mixed, self_totals = attend_forward(query, keys, values)
    mixed_here = mixed.reshape(HALF, heads * HD).astype(BF)
    stream_two = stream + scatter_tokens(mult_right(mixed_here, out_all))

    normed_three, scaled_three, rstd_three = norm_forward(stream_two, gain_three, offset_three)
    wide_three = gather_tokens(normed_three.astype(BF))
    cquery_raw = mult(wide_three, cquery_all).reshape(HALF, heads, HD)
    cquery = prep(cquery_raw, g_cquery).astype(BF).reshape(shape_four)
    ckv = mult(wide_text, ckv_all).reshape(1, TXT, heads, 2, HD)
    ckey_raw = ckv[:, :, :, 0]
    ckeys = head_norm(ckey_raw, g_ckey).astype(BF)
    cvalues = ckv[:, :, :, 1].astype(BF)
    cmixed, cross_totals = attend_forward(cquery, ckeys, cvalues)
    cmixed_here = cmixed.reshape(HALF, heads * HD).astype(BF)
    stream_three = stream_two + scatter_tokens(mult_right(cmixed_here, cout_all))

    normed_two, scaled_two, rstd_two = norm_forward(stream_three, gain_two, offset_two)
    wide_two = gather_tokens(normed_two.astype(BF))
    upper = mult(wide_two, up_all)
    active, gelu_back = jax.vjp(gelu_tanh, upper)
    active_here = active.astype(BF)
    output_here = stream_three + scatter_tokens(mult_right(active_here, down_all))

    diff = output_here - teacher_here.astype(F32)
    sse_local = jnp.sum(mask[:, None] * diff * diff)
    factor = 32.0 * lax.axis_size(DP) / count
    grad_out = factor * mask[:, None] * diff
    output_blocks = jnp.transpose(
        output_here.astype(BF).reshape(PIECE, 2 * CHIPS, width), (1, 0, 2)
    )
    output_back = lax.all_to_all(output_blocks, ROW_COL, 0, 0, tiled=True)
    output = jnp.transpose(
        output_back.reshape(CHIPS, 2, PIECE, width), (1, 0, 2, 3)
    ).reshape(SEQ, width).astype(F32)

    wide_grad = gather_tokens(grad_out.astype(BF))
    d_upper = gelu_back(mult(wide_grad, down_all))[0].astype(BF)
    d_normed_two = scatter_tokens(mult_right(d_upper, up_all))
    two_part = summed_over_latents(
        weight_grads([(wide_two, d_upper), (wide_grad, active_here)])
    )
    back_two, d_g_two, d_b_two = norm_backward(d_normed_two, scaled_two, rstd_two, gain_two)
    grad_three = grad_out + back_two

    wide_three_grad = gather_tokens(grad_three.astype(BF))
    d_cmixed = mult(wide_three_grad, cout_all).astype(BF).reshape(shape_four)
    d_cquery, d_ckeys, d_cvalues = attend_backward(cquery, ckeys, cvalues, cross_totals, d_cmixed)
    unused, cquery_back = jax.vjp(prep, cquery_raw, g_cquery)
    d_cquery_raw, d_g_cquery = cquery_back(d_cquery.reshape(HALF, heads, HD))
    d_cquery_here = d_cquery_raw.reshape(HALF, heads * HD).astype(BF)
    d_normed_three = scatter_tokens(mult_right(d_cquery_here, cquery_all))
    unused, ckey_back = jax.vjp(head_norm, ckey_raw, g_ckey)
    d_ckey_raw, d_g_ckey = ckey_back(d_ckeys)
    d_ckv = jnp.stack([d_ckey_raw, d_cvalues], axis=3).reshape(TXT, heads * 2 * HD).astype(BF)
    back_three, d_g_three, d_b_three = norm_backward(
        d_normed_three, scaled_three, rstd_three, gain_three
    )
    grad_two = grad_three + back_three

    three_grads = weight_grads(
        [(wide_three, d_cquery_here), (wide_three_grad, cmixed_here), (wide_text, d_ckv)]
    )
    three_part = summed_over_latents(three_grads)

    wide_two_grad = gather_tokens(grad_two.astype(BF))
    d_mixed = mult(wide_two_grad, out_all) + settled(three_grads)
    d_mixed = d_mixed.astype(BF).reshape(shape_four)
    d_query, d_keys, d_values = attend_backward(query, keys, values, self_totals, d_mixed)
    d_both = jnp.concatenate([d_keys[0], d_values[0]], axis=2)
    d_both = d_both[:HALF] + other_core(swapped_heads(d_both[HALF:]).astype(BF)).astype(F32)
    unused, query_back = jax.vjp(prep, query_raw, g_query)
    d_query_raw, d_g_query = query_back(d_query.reshape(HALF, heads, HD))
    unused, key_back = jax.vjp(prep, key_raw, g_key)
    d_key_raw, d_g_key = key_back(d_both[..., :HD])
    d_packed = (
        jnp.stack([d_query_raw, d_key_raw, d_both[..., HD:]], axis=2)
        .reshape(HALF, heads * 3 * HD)
        .astype(BF)
    )
    d_inputs = scatter_tokens(mult_right(d_packed, qkv_all))
    d_inputs = d_inputs + (settled(two_part) + settled(three_part))
    back_one, d_g_one, d_b_one = norm_backward(d_inputs, scaled_one, rstd_one, gain_one)
    grad_one = grad_two + back_one

    d_shift_part = jnp.sum(d_inputs, axis=0)
    shared = jnp.concatenate([d_g_query, d_g_key, d_g_cquery, d_g_ckey, sse_local[None]])
    small = jnp.stack(
        [d_g_one, d_b_one, d_g_three, d_b_three, d_g_two, d_b_two, d_shift_part]
        + [jnp.pad(shared, (0, D - shared.shape[0]))]
    )
    piece = jnp.concatenate([grad_one.astype(BF), in_two(small)], axis=0)
    pieces = [piece] + [from_chip(piece, j) for j in range(1, CHIPS)]
    wide_one_grad = jnp.concatenate([p[:PIECE] for p in pieces], axis=0)
    small = sum(p[PIECE:].astype(F32) for p in pieces)
    small = small[:8] + small[8:]
    small = small + other_core(small)
    oq_part = summed_over_latents(
        weight_grads([(wide_two_grad, mixed_here), (wide_one, d_packed)])
    )
    d_joined = mult(wide_one_grad, skip_all)
    skip_sums = jnp.stack([jnp.sum(d_joined * skip_scaled, axis=0), jnp.sum(d_joined, axis=0)])
    skip_sums = skip_sums[:, : 2 * width] + other_core(skip_sums[:, 2 * width :])
    place = lax.axis_index(ROW_COL)
    shared_size = shared.shape[0]
    vector = jnp.concatenate(
        [
            lax.dynamic_slice_in_dim(small[:6], place * width, width, 1).reshape(-1),
            small[7, :shared_size],
            skip_sums.reshape(-1),
        ]
    )
    vector = jnp.pad(vector, (0, -vector.shape[0] % (D // 2))).reshape(-1, D // 2)
    vector_rows = vector.shape[0]
    latent_shift = lax.dynamic_slice_in_dim(small[6], row * (D // 2), D // 2, 0).astype(BF)
    d_w_mod = mult_left(emb_here, latent_shift[None])
    extra = jnp.concatenate([in_two(vector), d_w_mod.astype(BF)], axis=0).T
    extra = jnp.concatenate([extra, extra], axis=0)
    d_skip = weight_grads([(wide_one_grad, normed)])
    skip_part = summed_over_latents(
        jnp.concatenate([d_skip, extra], axis=1), 2 * width, vector_rows
    )
    both_gains = both_vectors[0] + settled(d_skip)
    weighted = d_joined * both_gains
    back_sums = sum_over_chips(
        jnp.stack([jnp.sum(weighted, axis=1), jnp.sum(weighted * skip_scaled, axis=1)])
    ) / (2 * D)
    back_joined = skip_rstd[:, None] * (
        weighted - back_sums[0][:, None] - skip_scaled * back_sums[1][:, None]
    )
    back_mine = back_joined[:, : 2 * width]
    back_theirs = other_core(back_joined[:, 2 * width :])
    unturn = (CHIPS - chip) % CHIPS * PIECE
    back_mine = turned(back_mine, unturn)
    back_theirs = turned(back_theirs, unturn)
    back_tokens = lax.dynamic_slice_in_dim(
        jnp.concatenate([back_mine, back_theirs, back_mine], axis=0), core * HALF, SEQ, 0
    )
    d_hidden = back_tokens[:, :width]
    d_skipped = back_tokens[:, width:]

    two_grads = spread_over_latents(two_part, row)
    three_grads = spread_over_latents(three_part, row)
    last_grads = spread_over_latents(jnp.concatenate([oq_part, skip_part], axis=1), row, False)

    def columns(summed, start, count):
        n = summed.shape[1] // 2
        return jnp.concatenate(
            [summed[:, start : start + count], summed[:, n + start : n + start + count]], axis=1
        ).astype(F32)

    n_up = w_up.shape[1] // 2
    d_w_up = columns(two_grads, 0, n_up)
    d_w_down = columns(two_grads, n_up, n_up).T
    d_w_cquery = columns(three_grads, 0, width)
    d_w_cout = columns(three_grads, width, width).T
    d_w_ckv = columns(three_grads, 2 * width, 2 * width)
    count_blocks = max(lax.axis_size(DP) // 2, 1)
    d_w_ckv = d_w_ckv.reshape(count_blocks, -1, 4 * width)[:, : w_ckv.shape[0] // count_blocks]
    d_w_ckv = d_w_ckv.reshape(-1, 4 * width)
    d_w_out = columns(last_grads, 0, width).T
    d_w_qkv = columns(last_grads, width, 3 * width)
    d_w_skip = columns(last_grads, 4 * width, 2 * width).reshape(D // 2, 2, 2, width)
    d_w_skip = jnp.transpose(d_w_skip, (2, 1, 3, 0)).reshape(2, 2 * width, D // 2)
    extra = last_grads.reshape(D // 2, 2, -1)[:, :, 6 * width :]
    extra = jnp.where(row == 0, extra[:, 0], extra[:, 1]).astype(F32).T
    vector = (extra[:vector_rows] + extra[vector_rows : 2 * vector_rows]).reshape(-1)
    d_w_mod = extra[2 * vector_rows :]
    d_g_one, d_b_one, d_g_three, d_b_three, d_g_two, d_b_two = vector[: 6 * width].reshape(6, width)
    shared = vector[6 * width : 6 * width + shared_size]
    d_g_query, d_g_key, d_g_cquery, d_g_ckey = shared[: 4 * HD].reshape(4, HD)
    loss = shared[4 * HD] / (count * D)
    skip_sums = vector[6 * width + shared_size : 10 * width + shared_size].reshape(2, 2, width)
    d_g_skip, d_b_skip = skip_sums
    return (
        output,
        d_hidden,
        d_skipped,
        d_w_skip,
        d_g_skip,
        d_b_skip,
        d_w_mod,
        d_g_one,
        d_b_one,
        d_w_qkv,
        d_g_query,
        d_g_key,
        d_w_out,
        d_g_three,
        d_b_three,
        d_w_cquery,
        d_w_ckv,
        d_g_cquery,
        d_g_ckey,
        d_w_cout,
        d_g_two,
        d_b_two,
        d_w_up,
        d_w_down,
        loss,
    )


def solution(mesh):
    side = math.isqrt(mesh.shape["dp"])
    split = Mesh(
        mesh.devices.reshape(side, side, mesh.shape["row"], 2, 2),
        ("dp_0", "dp_1", "row", "col_0", "col_1"),
    )
    in_specs = (
        P(DP, COL_ROW),
        P(DP, COL_ROW),
        P(DP, None, ROW_COL),
        P(DP, ROW_COL),
        P(DP),
        P(DP),
        P(None, DP),
        P(None, COL, "row"),
        P(None, COL_ROW),
        P(None, COL_ROW),
        P(COL, "row"),
        P(ROW_COL),
        P(ROW_COL),
        P("row", COL),
        P(),
        P(),
        P(COL, "row"),
        P(ROW_COL),
        P(ROW_COL),
        P("row", COL),
        P("row", COL),
        P(),
        P(),
        P(COL, "row"),
        P(ROW_COL),
        P(ROW_COL),
        P("row", COL),
        P(COL, "row"),
    )
    out_specs = (
        P(DP, ROW_COL),
        P(DP, COL_ROW),
        P(DP, COL_ROW),
        P(None, COL, "row"),
        P(None, COL_ROW),
        P(None, COL_ROW),
        P(COL, "row"),
        P(ROW_COL),
        P(ROW_COL),
        P("row", COL),
        P(),
        P(),
        P(COL, "row"),
        P(ROW_COL),
        P(ROW_COL),
        P("row", COL),
        P("row", COL),
        P(),
        P(),
        P(COL, "row"),
        P(ROW_COL),
        P(ROW_COL),
        P("row", COL),
        P(COL, "row"),
        P(),
    )
    return jax.shard_map(local, mesh=split, in_specs=in_specs, out_specs=out_specs, check_vma=False)
```

```python
from functools import partial
import math

import jax
import jax.numpy as jnp
from jax import lax
from jax.sharding import Mesh
from jax.sharding import PartitionSpec as P

D = 1408
HEADS = 16
HD = 88
FREQ = 256
TXT = 333
SEQ = 1024
LINE = ("row", "col_0")
CORE = "col_1"
COL = ("col_0", "col_1")
ROW_COL = ("row", "col_0", "col_1")
DP = ("dp_0", "dp_1")
ALL = ("dp_0", "dp_1", "row", "col_0", "col_1")
COL_ROW = ("col_0", "col_1", "row")
CHIPS = 4
HALF = SEQ // 2
PIECE = HALF // CHIPS
BF = jnp.bfloat16
F32 = jnp.float32


epsilon = 1e-06


def mult(left, right):
    return jnp.dot(left, right, preferred_element_type=jnp.float32)


def mult_left(left, right):
    return lax.dot_general(
        left, right, (((0,), (0,)), ((), ())), preferred_element_type=jnp.float32
    )


def mult_right(left, right):
    return lax.dot_general(
        left, right, (((1,), (1,)), ((), ())), preferred_element_type=jnp.float32
    )


def from_chip(value, ahead):
    return lax.ppermute(value, LINE, [(i, (i - ahead) % CHIPS) for i in range(CHIPS)])


def other_core(value):
    return lax.ppermute(value, CORE, [(0, 1), (1, 0)])


def other_row(value):
    return lax.ppermute(value, "row", [(0, 1), (1, 0)])


def gather_tokens(piece):
    return jnp.concatenate([piece] + [from_chip(piece, j) for j in range(1, CHIPS)], axis=0)


def scatter_tokens(partial_sums):
    total = partial_sums[:PIECE]
    for j in range(1, CHIPS):
        sent = partial_sums[j * PIECE : (j + 1) * PIECE].astype(BF)
        total = total + from_chip(sent, CHIPS - j).astype(F32)
    return total


def sum_over_chips(value):
    total = value
    for j in range(1, CHIPS):
        total = total + jnp.roll(from_chip(value, j), j * PIECE, axis=1)
    return total


def turned(value, start):
    twice = jnp.concatenate([value, value], axis=0)
    return lax.dynamic_slice_in_dim(twice, start, value.shape[0], 0)


def norm_forward(values, gain, offset):
    mean = jnp.mean(values, axis=1, keepdims=True)
    spread = jnp.mean(values * values, axis=1, keepdims=True) - mean * mean
    rstd = lax.rsqrt(spread + epsilon)
    scaled = (values - mean) * rstd
    return (scaled * gain + offset, scaled, rstd)


def norm_backward(grad, scaled, rstd, gain):
    weighted = grad * gain
    first = jnp.mean(weighted, axis=1, keepdims=True)
    second = jnp.mean(weighted * scaled, axis=1, keepdims=True)
    back = rstd * (weighted - first - scaled * second)
    return (back, jnp.sum(grad * scaled, axis=0), jnp.sum(grad, axis=0))


def halves_swapped(weight, dim, row, after=None):
    kept = lax.dynamic_slice_in_dim(weight, row * (weight.shape[dim] // 2), weight.shape[dim] // 2, dim)
    sent = lax.dynamic_slice_in_dim(
        weight, (1 - row) * (weight.shape[dim] // 2), weight.shape[dim] // 2, dim
    )
    if after is not None:
        sent = sent + settled(after).astype(sent.dtype)
    return (kept, other_row(sent))


def in_row_order(kept, received, dim, row):
    three = jnp.concatenate([received, kept, received], axis=dim)
    return lax.dynamic_slice_in_dim(
        three, (1 - row) * kept.shape[dim], 2 * kept.shape[dim], dim
    )


def settled(value):
    return jnp.minimum(jnp.abs(value[(0,) * value.ndim].astype(F32)), 0.0)


def copied_to_each(value, axis):
    length = lax.axis_size(axis)
    return lax.all_to_all(
        jnp.broadcast_to(value[None], (length, *value.shape)), axis, 0, 0, tiled=True
    )


def in_two(value):
    high = lax.reduce_precision(value, exponent_bits=8, mantissa_bits=7)
    return jnp.concatenate([high.astype(BF), (value - high).astype(BF)], axis=0)


def with_other_core(own):
    return jnp.concatenate([own, other_core(own)], axis=1)


def whole_columns(weight, row, after=None):
    kept, received = halves_swapped(weight, 1, row, after)
    return in_row_order(kept, received, 0, row)


def padded(value):
    return jnp.pad(value, ((0, 0), (0, -value.shape[1] % 128)))


def blocks_by_latents(blocks, row, after):
    half = lax.axis_size(DP) // 2
    kept, sent = [], []
    for block in blocks:
        n = block.shape[1] // 2
        kept.append(padded(lax.dynamic_slice_in_dim(block, row * n, n, 1)))
        sent.append(padded(lax.dynamic_slice_in_dim(block, (1 - row) * n, n, 1)))
    kept = jnp.concatenate(kept, axis=1) if len(kept) > 1 else kept[0]
    sent = jnp.concatenate(sent, axis=1) if len(sent) > 1 else sent[0]
    sent = sent + settled(after).astype(BF)
    return jnp.where(lax.axis_index(DP) // half == row, kept, other_row(sent))


def block_of_rows(weight):
    half = lax.axis_size(DP) // 2
    rows = weight.shape[0] // half
    return lax.dynamic_slice_in_dim(weight, lax.axis_index(DP) % half * rows, rows, 0)


def block_of_columns(weight):
    half = lax.axis_size(DP) // 2
    columns = weight.shape[1] // half
    return lax.dynamic_slice_in_dim(weight, lax.axis_index(DP) % half * columns, columns, 1).T


def weight_grads(pairs):
    def products(part):
        outs = []
        for left, right in pairs:
            n = right.shape[1] // 2
            out = mult_left(left, right[:, part * n : (part + 1) * n])
            short = pairs[0][0].shape[1] - out.shape[0]
            if short:
                count = 2 * max(lax.axis_size(DP) // 2, 1)
                out = out.reshape(count, -1, n)
                out = jnp.pad(out, ((0, 0), (0, short // count), (0, 0))).reshape(-1, n)
            outs.append(out)
        return jnp.concatenate(outs, axis=1) if len(outs) > 1 else outs[0]

    theirs = other_core(products(1).astype(BF))
    return (products(0) + theirs.astype(F32)).astype(BF)


def to_row_half(part):
    count = lax.axis_size(DP)
    half = count // 2
    pairs = []
    for i in range(count):
        for r in range(2):
            stays = i // half == r
            pairs.append((2 * i + r, 2 * i + r if stays else 2 * ((i + half) % count) + 1 - r))
    return lax.ppermute(part, DP + ("row",), pairs)


def scattered_over_latents(grads):
    if lax.axis_size(DP) == 1:
        return grads
    blocks = grads.reshape(lax.axis_size(DP), -1, grads.shape[1])
    return to_row_half(lax.psum_scatter(blocks, DP, scatter_dimension=0))


def summed_over_latents(grads, start=0, pairs_of=0):
    count = lax.axis_size(DP)
    if count == 1:
        return grads
    rows, n = grads.shape
    arrived = lax.all_to_all(grads.reshape(count, rows // count, n), DP, 0, 0, tiled=True)
    part = jnp.sum(arrived.astype(F32), axis=0)
    if pairs_of:
        exact = part[:, start : start + pairs_of] + part[:, start + pairs_of : start + 2 * pairs_of]
        rest = part[:, start + 2 * pairs_of :].astype(BF)
        part = jnp.concatenate([part[:, :start].astype(BF), in_two(exact.T).T, rest], axis=1)
    else:
        part = part.astype(BF)
    return to_row_half(part)


def spread_over_latents(part, row, gather=True):
    count = lax.axis_size(DP)
    if count == 1:
        kept, received = halves_swapped(part, 0, row)
        return in_row_order(kept, received, 1, row)
    rows, n = part.shape
    if gather:
        spread = lax.all_gather(part, DP, axis=0)
    else:
        spread = copied_to_each(part, DP)
    spread = spread.reshape(2, count // 2 * rows, n)
    return jnp.concatenate([spread[0], spread[1]], axis=1)


def head_norm(values, gain):
    mean = jnp.mean(values, axis=-1, keepdims=True)
    spread = jnp.mean(values * values, axis=-1, keepdims=True) - mean * mean
    return (values - mean) * lax.rsqrt(spread + epsilon) * gain


def rotate(values):
    quarter = values.shape[-1] // 4
    return jnp.concatenate(
        [
            -values[..., quarter : 2 * quarter],
            values[..., :quarter],
            -values[..., 3 * quarter :],
            values[..., 2 * quarter : 3 * quarter],
        ],
        axis=-1,
    )


def qk_prep(raw, gain, cosine, sine):
    normal = head_norm(raw, gain)
    return normal * cosine + rotate(normal) * sine


def gelu_tanh(values):
    return jax.nn.gelu(values, approximate=True)


def rope_tables(positions):
    quarter = HD // 4
    freqs = jnp.exp(-math.log(10000.0) * jnp.arange(quarter, dtype=jnp.float32) / quarter)
    rows_angle = positions[0].astype(jnp.float32)[:, None] * freqs[None, :]
    cols_angle = positions[1].astype(jnp.float32)[:, None] * freqs[None, :]
    cosine = jnp.concatenate(
        [jnp.cos(rows_angle), jnp.cos(rows_angle), jnp.cos(cols_angle), jnp.cos(cols_angle)], axis=1
    )
    sine = jnp.concatenate(
        [jnp.sin(rows_angle), jnp.sin(rows_angle), jnp.sin(cols_angle), jnp.sin(cols_angle)], axis=1
    )
    return (cosine, sine)


def time_embed(steps):
    half = FREQ // 2
    freqs = jnp.exp(-math.log(10000.0) * jnp.arange(half, dtype=jnp.float32) / half)
    angles = steps.astype(jnp.float32)[:, None] * freqs[None, :]
    return jnp.concatenate([jnp.cos(angles), jnp.sin(angles)], axis=1)


def attend_forward(query, keys, values):
    scale = HD ** (-0.5)
    length = query.shape[1]
    block = min(512, length)
    outputs = []
    totals = []
    for start in range(0, length, block):
        piece = query[:, start : start + block]
        scores = scale * jnp.einsum(
            "lqhd,lkhd->lhqk", piece, keys, preferred_element_type=jnp.float32
        )
        top = jnp.max(scores, axis=-1, keepdims=True)
        expo = jnp.exp(scores - top)
        summed = jnp.sum(expo, axis=-1, keepdims=True)
        weights = expo / summed
        totals.append(top[..., 0] + jnp.log(summed[..., 0]))
        outputs.append(
            jnp.einsum(
                "lhqk,lkhd->lqhd",
                weights.astype(jnp.bfloat16),
                values,
                preferred_element_type=jnp.float32,
            )
        )
    return (jnp.concatenate(outputs, axis=1), jnp.concatenate(totals, axis=2))


def attend_backward(query, keys, values, totals, grad_out):
    scale = HD ** (-0.5)
    length = query.shape[1]
    block = min(512, length)
    d_keys = jnp.zeros(keys.shape, jnp.float32)
    d_values = jnp.zeros(values.shape, jnp.float32)
    d_query = []
    for start in range(0, length, block):
        piece = query[:, start : start + block]
        grad_piece = grad_out[:, start : start + block]
        scores = scale * jnp.einsum(
            "lqhd,lkhd->lhqk", piece, keys, preferred_element_type=jnp.float32
        )
        weights = jnp.exp(scores - totals[:, :, start : start + block, None])
        d_weights = jnp.einsum(
            "lqhd,lkhd->lhqk", grad_piece, values, preferred_element_type=jnp.float32
        )
        d_scores = weights * (d_weights - jnp.sum(d_weights * weights, axis=-1, keepdims=True))
        d_scores_b = d_scores.astype(jnp.bfloat16)
        d_query.append(
            scale
            * jnp.einsum("lhqk,lkhd->lqhd", d_scores_b, keys, preferred_element_type=jnp.float32)
        )
        d_keys = d_keys + scale * jnp.einsum(
            "lhqk,lqhd->lkhd", d_scores_b, piece, preferred_element_type=jnp.float32
        )
        d_values = d_values + jnp.einsum(
            "lhqk,lqhd->lkhd",
            weights.astype(jnp.bfloat16),
            grad_piece,
            preferred_element_type=jnp.float32,
        )
    return (jnp.concatenate(d_query, axis=1), d_keys, d_values)


def local(
    hidden,
    skipped,
    text,
    teacher,
    valid,
    steps,
    positions,
    w_skip,
    g_skip,
    b_skip,
    w_mod,
    g_one,
    b_one,
    w_qkv,
    g_query,
    g_key,
    w_out,
    g_three,
    b_three,
    w_cquery,
    w_ckv,
    g_cquery,
    g_ckey,
    w_cout,
    g_two,
    b_two,
    w_up,
    w_down,
):
    row = lax.axis_index("row")
    chip = lax.axis_index(LINE)
    core = lax.axis_index(CORE)
    width = hidden.shape[1]
    turn = chip * PIECE
    heads_own = HEADS // (2 * CHIPS)
    heads = 2 * heads_own
    shape_four = (1, HALF, heads, HD)

    def own_tokens(values):
        return turned(lax.dynamic_slice_in_dim(values, core * HALF, HALF, 0), turn)

    def other_tokens(values):
        return turned(lax.dynamic_slice_in_dim(values, (1 - core) * HALF, HALF, 0), turn)

    skip_two = jnp.transpose(w_skip.reshape(2, 2, width, D // 2), (3, 1, 0, 2)).reshape(
        D // 2, 4 * width
    )
    skip_own = whole_columns(skip_two, row)
    skip_other = other_core(skip_own)
    skip_all = jnp.concatenate([skip_own, skip_other], axis=1)
    qkv_all = with_other_core(whole_columns(w_qkv, row, skip_own))
    if lax.axis_size(DP) == 1:
        out_all = with_other_core(whole_columns(w_out.T, row))
        cquery_all = with_other_core(whole_columns(w_cquery, row))
        cout_all = with_other_core(whole_columns(w_cout.T, row))
        ckv_all = with_other_core(whole_columns(w_ckv, row))
        up_all = with_other_core(whole_columns(w_up, row))
        down_all = with_other_core(whole_columns(w_down.T, row))
    else:
        ckv_block = block_of_rows(w_ckv)
        ckv_rows = ckv_block.shape[0]
        ckv_block = jnp.pad(ckv_block, ((0, D // lax.axis_size(DP) - ckv_rows), (0, 0)))
        four_block = blocks_by_latents(
            [
                block_of_columns(w_out),
                block_of_rows(w_cquery),
                block_of_columns(w_cout),
                ckv_block,
            ],
            row,
            skip_own,
        )
        four_own = lax.all_gather(four_block, DP, axis=0, tiled=True)
        two_block = blocks_by_latents([block_of_rows(w_up), block_of_columns(w_down)], row, four_own)
        two_own = lax.all_gather(two_block, DP, axis=0, tiled=True)
        four_other = other_core(four_own)

        def both(start, count):
            return jnp.concatenate(
                [four_own[:, start : start + count], four_other[:, start : start + count]], axis=1
            )

        step = width + (-width) % 128
        out_all = both(0, width)
        cquery_all = both(step, width)
        cout_all = both(2 * step, width)
        ckv_all = both(3 * step, 2 * width).reshape(lax.axis_size(DP), -1, 4 * width)
        ckv_all = ckv_all[:, :ckv_rows].reshape(-1, 4 * width)
        two_other = other_core(two_own)
        hidden_own = two_own.shape[1] // 2
        up_all = jnp.concatenate([two_own[:, :hidden_own], two_other[:, :hidden_own]], axis=1)
        down_all = jnp.concatenate([two_own[:, hidden_own:], two_other[:, hidden_own:]], axis=1)

    freq_here = w_mod.shape[0]
    mask_all = valid.astype(F32)
    counts = copied_to_each(jnp.broadcast_to(jnp.sum(mask_all), (1, 128)), DP)
    count = jnp.sum(counts[:, 0, 0])
    emb = time_embed(steps).astype(BF)
    emb_here = lax.dynamic_slice_in_dim(emb, lax.axis_index(COL) * freq_here, freq_here, 1)
    shift_part = mult(emb_here, w_mod)
    vectors = jnp.concatenate(
        [jnp.stack([g_one, b_one, g_three, b_three, g_two, b_two]).reshape(-1), shift_part[0]]
    )
    gathered = copied_to_each(vectors, ROW_COL)
    gains = jnp.transpose(gathered[:, : 6 * width].reshape(8, 6, width), (1, 0, 2)).reshape(6, D)
    gain_one, offset_one, gain_three, offset_three, gain_two, offset_two = gains
    shift = jnp.sum(gathered[:, 6 * width :].reshape(2, 4, D // 2), axis=1).reshape(D)
    mask = lax.dynamic_slice_in_dim(mask_all, core * HALF + turn, PIECE, 0)

    teacher_blocks = jnp.transpose(
        teacher.reshape(2, CHIPS, PIECE, width), (1, 0, 2, 3)
    ).reshape(2 * CHIPS, PIECE, width)
    teacher_here = jnp.transpose(
        lax.all_to_all(teacher_blocks, ROW_COL, 0, 0, tiled=True), (1, 0, 2)
    ).reshape(PIECE, D)

    wide_text = jnp.transpose(copied_to_each(text[0], ROW_COL), (1, 0, 2)).reshape(TXT, -1)

    cosine, sine = rope_tables(own_tokens(positions.T).T)
    prep = partial(qk_prep, cosine=cosine[:, None, :], sine=sine[:, None, :])

    joined = jnp.concatenate([hidden, skipped], axis=1)
    mine = own_tokens(joined)
    theirs = other_core(other_tokens(joined))
    pairs = jnp.concatenate([mine, theirs], axis=1).astype(F32)
    skip_vectors = jnp.stack([g_skip, b_skip]).reshape(2, 2 * width)
    both_vectors = jnp.concatenate([skip_vectors, other_core(skip_vectors)], axis=1)
    skip_sums = sum_over_chips(jnp.stack([jnp.sum(pairs, axis=1), jnp.sum(pairs * pairs, axis=1)]))
    skip_mean = skip_sums[0] / (2 * D)
    skip_rstd = lax.rsqrt(skip_sums[1] / (2 * D) - skip_mean * skip_mean + epsilon)
    skip_scaled = (pairs - skip_mean[:, None]) * skip_rstd[:, None]
    normed = (skip_scaled * both_vectors[0] + both_vectors[1]).astype(BF)
    stream = scatter_tokens(mult_right(normed, skip_all))

    normed_one, scaled_one, rstd_one = norm_forward(stream, gain_one, offset_one)
    wide_one = gather_tokens((normed_one + shift).astype(BF))
    packed = (mult(wide_one, qkv_all) + settled(wide_text)).reshape(HALF, heads, 3, HD)
    query_raw = packed[:, :, 0]
    key_raw = packed[:, :, 1]
    query = prep(query_raw, g_query).astype(BF).reshape(shape_four)
    keys_here = prep(key_raw, g_key).astype(BF)
    values_here = packed[:, :, 2].astype(BF)

    def swapped_heads(values):
        return jnp.concatenate([values[:, heads_own:], values[:, :heads_own]], axis=1)

    key_values = other_core(swapped_heads(jnp.concatenate([keys_here, values_here], axis=2)))
    keys = jnp.concatenate([keys_here, key_values[..., :HD]], axis=0)[None]
    values = jnp.concatenate([values_here, key_values[..., HD:]], axis=0)[None]
    mixed, self_totals = attend_forward(query, keys, values)
    mixed_here = mixed.reshape(HALF, heads * HD).astype(BF)
    early = settled(count) + settled(teacher_here)
    stream_two = stream + early + scatter_tokens(mult_right(mixed_here, out_all))

    normed_three, scaled_three, rstd_three = norm_forward(stream_two, gain_three, offset_three)
    wide_three = gather_tokens(normed_three.astype(BF))
    cquery_raw = mult(wide_three, cquery_all).reshape(HALF, heads, HD)
    cquery = prep(cquery_raw, g_cquery).astype(BF).reshape(shape_four)
    ckv = mult(wide_text, ckv_all).reshape(1, TXT, heads, 2, HD)
    ckey_raw = ckv[:, :, :, 0]
    ckeys = head_norm(ckey_raw, g_ckey).astype(BF)
    cvalues = ckv[:, :, :, 1].astype(BF)
    cmixed, cross_totals = attend_forward(cquery, ckeys, cvalues)
    cmixed_here = cmixed.reshape(HALF, heads * HD).astype(BF)
    stream_three = stream_two + scatter_tokens(mult_right(cmixed_here, cout_all))

    normed_two, scaled_two, rstd_two = norm_forward(stream_three, gain_two, offset_two)
    wide_two = gather_tokens(normed_two.astype(BF))
    upper = mult(wide_two, up_all)
    active, gelu_back = jax.vjp(gelu_tanh, upper)
    active_here = active.astype(BF)
    output_here = stream_three + scatter_tokens(mult_right(active_here, down_all))

    diff = output_here - teacher_here.astype(F32)
    sse_local = jnp.sum(mask[:, None] * diff * diff)
    factor = 32.0 * lax.axis_size(DP) / count
    grad_out = factor * mask[:, None] * diff
    output_blocks = jnp.transpose(
        output_here.astype(BF).reshape(PIECE, 2 * CHIPS, width), (1, 0, 2)
    )
    output_back = lax.all_to_all(output_blocks, ROW_COL, 0, 0, tiled=True)
    output = jnp.transpose(
        output_back.reshape(CHIPS, 2, PIECE, width), (1, 0, 2, 3)
    ).reshape(SEQ, width).astype(F32)

    wide_grad = gather_tokens(grad_out.astype(BF))
    d_upper = gelu_back(mult(wide_grad, down_all))[0].astype(BF)
    d_normed_two = scatter_tokens(mult_right(d_upper, up_all))
    two_part = scattered_over_latents(
        weight_grads([(wide_two, d_upper), (wide_grad, active_here)])
    )
    back_two, d_g_two, d_b_two = norm_backward(d_normed_two, scaled_two, rstd_two, gain_two)
    grad_three = grad_out + back_two

    wide_three_grad = gather_tokens(grad_three.astype(BF))
    d_cmixed = mult(wide_three_grad, cout_all).astype(BF).reshape(shape_four)
    d_cquery, d_ckeys, d_cvalues = attend_backward(cquery, ckeys, cvalues, cross_totals, d_cmixed)
    unused, cquery_back = jax.vjp(prep, cquery_raw, g_cquery)
    d_cquery_raw, d_g_cquery = cquery_back(d_cquery.reshape(HALF, heads, HD))
    d_cquery_here = d_cquery_raw.reshape(HALF, heads * HD).astype(BF)
    d_normed_three = scatter_tokens(mult_right(d_cquery_here, cquery_all))
    unused, ckey_back = jax.vjp(head_norm, ckey_raw, g_ckey)
    d_ckey_raw, d_g_ckey = ckey_back(d_ckeys)
    d_ckv = jnp.stack([d_ckey_raw, d_cvalues], axis=3).reshape(TXT, heads * 2 * HD).astype(BF)
    back_three, d_g_three, d_b_three = norm_backward(
        d_normed_three, scaled_three, rstd_three, gain_three
    )
    grad_two = grad_three + back_three

    three_grads = weight_grads(
        [(wide_three, d_cquery_here), (wide_three_grad, cmixed_here), (wide_text, d_ckv)]
    )
    three_part = summed_over_latents(three_grads)

    wide_two_grad = gather_tokens(grad_two.astype(BF))
    d_mixed = mult(wide_two_grad, out_all) + settled(three_grads)
    d_mixed = d_mixed.astype(BF).reshape(shape_four)
    d_query, d_keys, d_values = attend_backward(query, keys, values, self_totals, d_mixed)
    d_both = jnp.concatenate([d_keys[0], d_values[0]], axis=2)
    d_both = d_both[:HALF] + other_core(swapped_heads(d_both[HALF:]).astype(BF)).astype(F32)
    unused, query_back = jax.vjp(prep, query_raw, g_query)
    d_query_raw, d_g_query = query_back(d_query.reshape(HALF, heads, HD))
    unused, key_back = jax.vjp(prep, key_raw, g_key)
    d_key_raw, d_g_key = key_back(d_both[..., :HD])
    d_packed = (
        jnp.stack([d_query_raw, d_key_raw, d_both[..., HD:]], axis=2)
        .reshape(HALF, heads * 3 * HD)
        .astype(BF)
    )
    d_inputs = scatter_tokens(mult_right(d_packed, qkv_all))
    d_inputs = d_inputs + (settled(two_part) + settled(three_part))
    back_one, d_g_one, d_b_one = norm_backward(d_inputs, scaled_one, rstd_one, gain_one)
    grad_one = grad_two + back_one

    d_shift_part = jnp.sum(d_inputs, axis=0)
    shared = jnp.concatenate([d_g_query, d_g_key, d_g_cquery, d_g_ckey, sse_local[None]])
    small = jnp.stack(
        [d_g_one, d_b_one, d_g_three, d_b_three, d_g_two, d_b_two, d_shift_part]
        + [jnp.pad(shared, (0, D - shared.shape[0]))]
    )
    piece = jnp.concatenate([grad_one.astype(BF), in_two(small)], axis=0)
    pieces = [piece] + [from_chip(piece, j) for j in range(1, CHIPS)]
    wide_one_grad = jnp.concatenate([p[:PIECE] for p in pieces], axis=0)
    small = sum(p[PIECE:].astype(F32) for p in pieces)
    small = small[:8] + small[8:]
    small = small + other_core(small)
    oq_part = summed_over_latents(
        weight_grads([(wide_two_grad, mixed_here), (wide_one, d_packed)])
    )
    d_joined = mult(wide_one_grad, skip_all) + settled(oq_part)
    skip_sums = jnp.stack([jnp.sum(d_joined * skip_scaled, axis=0), jnp.sum(d_joined, axis=0)])
    skip_sums = skip_sums[:, : 2 * width] + other_core(skip_sums[:, 2 * width :])
    place = lax.axis_index(ROW_COL)
    shared_size = shared.shape[0]
    vector = jnp.concatenate(
        [
            lax.dynamic_slice_in_dim(small[:6], place * width, width, 1).reshape(-1),
            small[7, :shared_size],
            skip_sums.reshape(-1),
        ]
    )
    vector = jnp.pad(vector, (0, -vector.shape[0] % (D // 2))).reshape(-1, D // 2)
    vector_rows = vector.shape[0]
    latent_shift = lax.dynamic_slice_in_dim(small[6], row * (D // 2), D // 2, 0).astype(BF)
    d_w_mod = mult_left(emb_here, latent_shift[None])
    extra = jnp.concatenate([in_two(vector), d_w_mod.astype(BF)], axis=0).T
    extra = jnp.concatenate([extra, extra], axis=0)
    d_skip = weight_grads([(wide_one_grad, normed)])
    skip_part = summed_over_latents(
        jnp.concatenate([d_skip, extra], axis=1), 2 * width, vector_rows
    )
    both_gains = both_vectors[0] + settled(d_skip)
    weighted = d_joined * both_gains
    back_sums = sum_over_chips(
        jnp.stack([jnp.sum(weighted, axis=1), jnp.sum(weighted * skip_scaled, axis=1)])
    ) / (2 * D)
    back_joined = skip_rstd[:, None] * (
        weighted - back_sums[0][:, None] - skip_scaled * back_sums[1][:, None]
    )
    back_mine = back_joined[:, : 2 * width]
    back_theirs = other_core(back_joined[:, 2 * width :])
    unturn = (CHIPS - chip) % CHIPS * PIECE
    back_mine = turned(back_mine, unturn)
    back_theirs = turned(back_theirs, unturn)
    back_tokens = lax.dynamic_slice_in_dim(
        jnp.concatenate([back_mine, back_theirs, back_mine], axis=0), core * HALF, SEQ, 0
    )
    d_hidden = back_tokens[:, :width]
    d_skipped = back_tokens[:, width:]

    five_grads = spread_over_latents(jnp.concatenate([two_part, three_part], axis=1), row)
    last_grads = spread_over_latents(jnp.concatenate([oq_part, skip_part], axis=1), row, False)

    def columns(summed, start, count):
        n = summed.shape[1] // 2
        return jnp.concatenate(
            [summed[:, start : start + count], summed[:, n + start : n + start + count]], axis=1
        ).astype(F32)

    n_up = w_up.shape[1] // 2
    d_w_up = columns(five_grads, 0, n_up)
    d_w_down = columns(five_grads, n_up, n_up).T
    d_w_cquery = columns(five_grads, 2 * n_up, width)
    d_w_cout = columns(five_grads, 2 * n_up + width, width).T
    d_w_ckv = columns(five_grads, 2 * n_up + 2 * width, 2 * width)
    count_blocks = max(lax.axis_size(DP) // 2, 1)
    d_w_ckv = d_w_ckv.reshape(count_blocks, -1, 4 * width)[:, : w_ckv.shape[0] // count_blocks]
    d_w_ckv = d_w_ckv.reshape(-1, 4 * width)
    d_w_out = columns(last_grads, 0, width).T
    d_w_qkv = columns(last_grads, width, 3 * width)
    d_w_skip = columns(last_grads, 4 * width, 2 * width).reshape(D // 2, 2, 2, width)
    d_w_skip = jnp.transpose(d_w_skip, (2, 1, 3, 0)).reshape(2, 2 * width, D // 2)
    extra = last_grads.reshape(D // 2, 2, -1)[:, :, 6 * width :]
    extra = jnp.where(row == 0, extra[:, 0], extra[:, 1]).astype(F32).T
    vector = (extra[:vector_rows] + extra[vector_rows : 2 * vector_rows]).reshape(-1)
    d_w_mod = extra[2 * vector_rows :]
    d_g_one, d_b_one, d_g_three, d_b_three, d_g_two, d_b_two = vector[: 6 * width].reshape(6, width)
    shared = vector[6 * width : 6 * width + shared_size]
    d_g_query, d_g_key, d_g_cquery, d_g_ckey = shared[: 4 * HD].reshape(4, HD)
    loss = shared[4 * HD] / (count * D)
    skip_sums = vector[6 * width + shared_size : 10 * width + shared_size].reshape(2, 2, width)
    d_g_skip, d_b_skip = skip_sums
    return (
        output,
        d_hidden,
        d_skipped,
        d_w_skip,
        d_g_skip,
        d_b_skip,
        d_w_mod,
        d_g_one,
        d_b_one,
        d_w_qkv,
        d_g_query,
        d_g_key,
        d_w_out,
        d_g_three,
        d_b_three,
        d_w_cquery,
        d_w_ckv,
        d_g_cquery,
        d_g_ckey,
        d_w_cout,
        d_g_two,
        d_b_two,
        d_w_up,
        d_w_down,
        loss,
    )


def solution(mesh):
    side = math.isqrt(mesh.shape["dp"])
    split = Mesh(
        mesh.devices.reshape(side, side, mesh.shape["row"], 2, 2),
        ("dp_0", "dp_1", "row", "col_0", "col_1"),
    )
    in_specs = (
        P(DP, COL_ROW),
        P(DP, COL_ROW),
        P(DP, None, ROW_COL),
        P(DP, ROW_COL),
        P(DP),
        P(DP),
        P(None, DP),
        P(None, COL, "row"),
        P(None, COL_ROW),
        P(None, COL_ROW),
        P(COL, "row"),
        P(ROW_COL),
        P(ROW_COL),
        P("row", COL),
        P(),
        P(),
        P(COL, "row"),
        P(ROW_COL),
        P(ROW_COL),
        P("row", COL),
        P("row", COL),
        P(),
        P(),
        P(COL, "row"),
        P(ROW_COL),
        P(ROW_COL),
        P("row", COL),
        P(COL, "row"),
    )
    out_specs = (
        P(DP, ROW_COL),
        P(DP, COL_ROW),
        P(DP, COL_ROW),
        P(None, COL, "row"),
        P(None, COL_ROW),
        P(None, COL_ROW),
        P(COL, "row"),
        P(ROW_COL),
        P(ROW_COL),
        P("row", COL),
        P(),
        P(),
        P(COL, "row"),
        P(ROW_COL),
        P(ROW_COL),
        P("row", COL),
        P("row", COL),
        P(),
        P(),
        P(COL, "row"),
        P(ROW_COL),
        P(ROW_COL),
        P("row", COL),
        P(COL, "row"),
        P(),
    )
    return jax.shard_map(local, mesh=split, in_specs=in_specs, out_specs=out_specs, check_vma=False)
```

```python
from functools import partial
import math

import jax
import jax.numpy as jnp
from jax import lax
from jax.sharding import Mesh
from jax.sharding import PartitionSpec as P

D = 1408
HEADS = 16
HD = 88
FREQ = 256
TXT = 333
SEQ = 1024
LINE = ("row", "col_0")
CORE = "col_1"
COL = ("col_0", "col_1")
ROW_COL = ("row", "col_0", "col_1")
DP = ("dp_0", "dp_1")
ALL = ("dp_0", "dp_1", "row", "col_0", "col_1")
COL_ROW = ("col_0", "col_1", "row")
CHIPS = 4
HALF = SEQ // 2
PIECE = HALF // CHIPS
BF = jnp.bfloat16
F32 = jnp.float32


epsilon = 1e-06


def mult(left, right):
    return jnp.dot(left, right, preferred_element_type=jnp.float32)


def mult_left(left, right):
    return lax.dot_general(
        left, right, (((0,), (0,)), ((), ())), preferred_element_type=jnp.float32
    )


def mult_right(left, right):
    return lax.dot_general(
        left, right, (((1,), (1,)), ((), ())), preferred_element_type=jnp.float32
    )


def from_chip(value, ahead):
    return lax.ppermute(value, LINE, [(i, (i - ahead) % CHIPS) for i in range(CHIPS)])


def other_core(value):
    return lax.ppermute(value, CORE, [(0, 1), (1, 0)])


def other_row(value):
    return lax.ppermute(value, "row", [(0, 1), (1, 0)])


def gather_tokens(piece):
    return jnp.concatenate([piece] + [from_chip(piece, j) for j in range(1, CHIPS)], axis=0)


def scatter_tokens(partial_sums):
    total = partial_sums[:PIECE]
    for j in range(1, CHIPS):
        sent = partial_sums[j * PIECE : (j + 1) * PIECE].astype(BF)
        total = total + from_chip(sent, CHIPS - j).astype(F32)
    return total


def sum_over_chips(value):
    total = value
    for j in range(1, CHIPS):
        total = total + jnp.roll(from_chip(value, j), j * PIECE, axis=1)
    return total


def turned(value, start):
    twice = jnp.concatenate([value, value], axis=0)
    return lax.dynamic_slice_in_dim(twice, start, value.shape[0], 0)


def norm_forward(values, gain, offset):
    mean = jnp.mean(values, axis=1, keepdims=True)
    spread = jnp.mean(values * values, axis=1, keepdims=True) - mean * mean
    rstd = lax.rsqrt(spread + epsilon)
    scaled = (values - mean) * rstd
    return (scaled * gain + offset, scaled, rstd)


def norm_backward(grad, scaled, rstd, gain):
    weighted = grad * gain
    first = jnp.mean(weighted, axis=1, keepdims=True)
    second = jnp.mean(weighted * scaled, axis=1, keepdims=True)
    back = rstd * (weighted - first - scaled * second)
    return (back, jnp.sum(grad * scaled, axis=0), jnp.sum(grad, axis=0))


def halves_swapped(weight, dim, row, after=None):
    if after is not None:
        row = row + settled_index(after)
    kept = lax.dynamic_slice_in_dim(weight, row * (weight.shape[dim] // 2), weight.shape[dim] // 2, dim)
    sent = lax.dynamic_slice_in_dim(
        weight, (1 - row) * (weight.shape[dim] // 2), weight.shape[dim] // 2, dim
    )
    return (kept, other_row(sent))


def in_row_order(kept, received, dim, row):
    three = jnp.concatenate([received, kept, received], axis=dim)
    return lax.dynamic_slice_in_dim(
        three, (1 - row) * kept.shape[dim], 2 * kept.shape[dim], dim
    )


def settled(value):
    return jnp.minimum(jnp.abs(value[(0,) * value.ndim].astype(F32)), 0.0)


def settled_index(value):
    return settled(value).astype(jnp.int32)


def copied_to_each(value, axis):
    length = lax.axis_size(axis)
    return lax.all_to_all(
        jnp.broadcast_to(value[None], (length, *value.shape)), axis, 0, 0, tiled=True
    )


def in_two(value):
    high = lax.reduce_precision(value, exponent_bits=8, mantissa_bits=7)
    return jnp.concatenate([high.astype(BF), (value - high).astype(BF)], axis=0)


def with_other_core(own):
    return jnp.concatenate([own, other_core(own)], axis=1)


def whole_columns(weight, row, after=None):
    kept, received = halves_swapped(weight, 1, row, after)
    return in_row_order(kept, received, 0, row)


def padded(value):
    return jnp.pad(value, ((0, 0), (0, -value.shape[1] % 128)))


def blocks_by_latents(blocks, row):
    half = lax.axis_size(DP) // 2
    kept, sent = [], []
    for block in blocks:
        n = block.shape[1] // 2
        kept.append(padded(lax.dynamic_slice_in_dim(block, row * n, n, 1)))
        sent.append(padded(lax.dynamic_slice_in_dim(block, (1 - row) * n, n, 1)))
    kept = jnp.concatenate(kept, axis=1) if len(kept) > 1 else kept[0]
    sent = jnp.concatenate(sent, axis=1) if len(sent) > 1 else sent[0]
    return jnp.where(lax.axis_index(DP) // half == row, kept, other_row(sent))


def block_of_rows(weight, after):
    half = lax.axis_size(DP) // 2
    rows = weight.shape[0] // half
    place = lax.axis_index(DP) % half + settled_index(after)
    return lax.dynamic_slice_in_dim(weight, place * rows, rows, 0)


def block_of_columns(weight, after):
    half = lax.axis_size(DP) // 2
    columns = weight.shape[1] // half
    place = lax.axis_index(DP) % half + settled_index(after)
    return lax.dynamic_slice_in_dim(weight, place * columns, columns, 1).T


def weight_grads(pairs):
    def products(part):
        outs = []
        for left, right in pairs:
            n = right.shape[1] // 2
            out = mult_left(left, right[:, part * n : (part + 1) * n])
            short = pairs[0][0].shape[1] - out.shape[0]
            if short:
                count = 2 * max(lax.axis_size(DP) // 2, 1)
                out = out.reshape(count, -1, n)
                out = jnp.pad(out, ((0, 0), (0, short // count), (0, 0))).reshape(-1, n)
            outs.append(out)
        return jnp.concatenate(outs, axis=1) if len(outs) > 1 else outs[0]

    theirs = other_core(products(1).astype(BF))
    return (products(0) + theirs.astype(F32)).astype(BF)


def to_row_half(part):
    count = lax.axis_size(DP)
    half = count // 2
    pairs = []
    for i in range(count):
        for r in range(2):
            stays = i // half == r
            pairs.append((2 * i + r, 2 * i + r if stays else 2 * ((i + half) % count) + 1 - r))
    return lax.ppermute(part, DP + ("row",), pairs)


def scattered_over_latents(grads):
    if lax.axis_size(DP) == 1:
        return grads
    blocks = grads.reshape(lax.axis_size(DP), -1, grads.shape[1])
    return to_row_half(lax.psum_scatter(blocks, DP, scatter_dimension=0))


def summed_over_latents(grads, start=0, pairs_of=0):
    count = lax.axis_size(DP)
    if count == 1:
        return grads
    rows, n = grads.shape
    arrived = lax.all_to_all(grads.reshape(count, rows // count, n), DP, 0, 0, tiled=True)
    part = jnp.sum(arrived.astype(F32), axis=0)
    if pairs_of:
        exact = part[:, start : start + pairs_of] + part[:, start + pairs_of : start + 2 * pairs_of]
        rest = part[:, start + 2 * pairs_of :].astype(BF)
        part = jnp.concatenate([part[:, :start].astype(BF), in_two(exact.T).T, rest], axis=1)
    else:
        part = part.astype(BF)
    return to_row_half(part)


def spread_over_latents(part, row, gather=True):
    count = lax.axis_size(DP)
    if count == 1:
        kept, received = halves_swapped(part, 0, row)
        return in_row_order(kept[None], received[None], 0, row)
    rows, n = part.shape
    if gather:
        spread = lax.all_gather(part, DP, axis=0)
    else:
        spread = copied_to_each(part, DP)
    return spread.reshape(2, count // 2 * rows, n)


def head_norm(values, gain):
    mean = jnp.mean(values, axis=-1, keepdims=True)
    spread = jnp.mean(values * values, axis=-1, keepdims=True) - mean * mean
    return (values - mean) * lax.rsqrt(spread + epsilon) * gain


def rotate(values):
    quarter = values.shape[-1] // 4
    return jnp.concatenate(
        [
            -values[..., quarter : 2 * quarter],
            values[..., :quarter],
            -values[..., 3 * quarter :],
            values[..., 2 * quarter : 3 * quarter],
        ],
        axis=-1,
    )


def qk_prep(raw, gain, cosine, sine):
    normal = head_norm(raw, gain)
    return normal * cosine + rotate(normal) * sine


def gelu_tanh(values):
    return jax.nn.gelu(values, approximate=True)


def rope_tables(positions):
    quarter = HD // 4
    freqs = jnp.exp(-math.log(10000.0) * jnp.arange(quarter, dtype=jnp.float32) / quarter)
    rows_angle = positions[0].astype(jnp.float32)[:, None] * freqs[None, :]
    cols_angle = positions[1].astype(jnp.float32)[:, None] * freqs[None, :]
    cosine = jnp.concatenate(
        [jnp.cos(rows_angle), jnp.cos(rows_angle), jnp.cos(cols_angle), jnp.cos(cols_angle)], axis=1
    )
    sine = jnp.concatenate(
        [jnp.sin(rows_angle), jnp.sin(rows_angle), jnp.sin(cols_angle), jnp.sin(cols_angle)], axis=1
    )
    return (cosine, sine)


def time_embed(steps):
    half = FREQ // 2
    freqs = jnp.exp(-math.log(10000.0) * jnp.arange(half, dtype=jnp.float32) / half)
    angles = steps.astype(jnp.float32)[:, None] * freqs[None, :]
    return jnp.concatenate([jnp.cos(angles), jnp.sin(angles)], axis=1)


def attend_forward(query, keys, values):
    scale = HD ** (-0.5)
    length = query.shape[1]
    block = min(512, length)
    outputs = []
    totals = []
    for start in range(0, length, block):
        piece = query[:, start : start + block]
        scores = scale * jnp.einsum(
            "lqhd,lkhd->lhqk", piece, keys, preferred_element_type=jnp.float32
        )
        top = jnp.max(scores, axis=-1, keepdims=True)
        expo = jnp.exp(scores - top)
        summed = jnp.sum(expo, axis=-1, keepdims=True)
        weights = expo / summed
        totals.append(top[..., 0] + jnp.log(summed[..., 0]))
        outputs.append(
            jnp.einsum(
                "lhqk,lkhd->lqhd",
                weights.astype(jnp.bfloat16),
                values,
                preferred_element_type=jnp.float32,
            )
        )
    return (jnp.concatenate(outputs, axis=1), jnp.concatenate(totals, axis=2))


def attend_backward(query, keys, values, totals, grad_out):
    scale = HD ** (-0.5)
    length = query.shape[1]
    block = min(512, length)
    d_keys = jnp.zeros(keys.shape, jnp.float32)
    d_values = jnp.zeros(values.shape, jnp.float32)
    d_query = []
    for start in range(0, length, block):
        piece = query[:, start : start + block]
        grad_piece = grad_out[:, start : start + block]
        scores = scale * jnp.einsum(
            "lqhd,lkhd->lhqk", piece, keys, preferred_element_type=jnp.float32
        )
        weights = jnp.exp(scores - totals[:, :, start : start + block, None])
        d_weights = jnp.einsum(
            "lqhd,lkhd->lhqk", grad_piece, values, preferred_element_type=jnp.float32
        )
        d_scores = weights * (d_weights - jnp.sum(d_weights * weights, axis=-1, keepdims=True))
        d_scores_b = d_scores.astype(jnp.bfloat16)
        d_query.append(
            scale
            * jnp.einsum("lhqk,lkhd->lqhd", d_scores_b, keys, preferred_element_type=jnp.float32)
        )
        d_keys = d_keys + scale * jnp.einsum(
            "lhqk,lqhd->lkhd", d_scores_b, piece, preferred_element_type=jnp.float32
        )
        d_values = d_values + jnp.einsum(
            "lhqk,lqhd->lkhd",
            weights.astype(jnp.bfloat16),
            grad_piece,
            preferred_element_type=jnp.float32,
        )
    return (jnp.concatenate(d_query, axis=1), d_keys, d_values)


def local(
    hidden,
    skipped,
    text,
    teacher,
    valid,
    steps,
    positions,
    w_skip,
    g_skip,
    b_skip,
    w_mod,
    g_one,
    b_one,
    w_qkv,
    g_query,
    g_key,
    w_out,
    g_three,
    b_three,
    w_cquery,
    w_ckv,
    g_cquery,
    g_ckey,
    w_cout,
    g_two,
    b_two,
    w_up,
    w_down,
):
    row = lax.axis_index("row")
    chip = lax.axis_index(LINE)
    core = lax.axis_index(CORE)
    width = hidden.shape[1]
    turn = chip * PIECE
    heads_own = HEADS // (2 * CHIPS)
    heads = 2 * heads_own
    shape_four = (1, HALF, heads, HD)

    def own_tokens(values):
        return turned(lax.dynamic_slice_in_dim(values, core * HALF, HALF, 0), turn)

    def other_tokens(values):
        return turned(lax.dynamic_slice_in_dim(values, (1 - core) * HALF, HALF, 0), turn)

    skip_two = jnp.transpose(w_skip.reshape(2, 2, width, D // 2), (3, 1, 0, 2)).reshape(
        D // 2, 4 * width
    )
    skip_kept, skip_received = halves_swapped(skip_two, 1, row)
    skip_own = in_row_order(skip_kept, skip_received, 0, row)
    skip_other = other_core(skip_own)
    skip_all = jnp.concatenate([skip_own, skip_other], axis=1)
    qkv_all = with_other_core(whole_columns(w_qkv, row, skip_received))
    if lax.axis_size(DP) == 1:
        out_all = with_other_core(whole_columns(w_out.T, row))
        cquery_all = with_other_core(whole_columns(w_cquery, row))
        cout_all = with_other_core(whole_columns(w_cout.T, row))
        ckv_all = with_other_core(whole_columns(w_ckv, row))
        up_all = with_other_core(whole_columns(w_up, row))
        down_all = with_other_core(whole_columns(w_down.T, row))
    else:
        ckv_block = block_of_rows(w_ckv, skip_received)
        ckv_rows = ckv_block.shape[0]
        ckv_block = jnp.pad(ckv_block, ((0, D // lax.axis_size(DP) - ckv_rows), (0, 0)))
        four_block = blocks_by_latents(
            [
                block_of_columns(w_out, skip_received),
                block_of_rows(w_cquery, skip_received),
                block_of_columns(w_cout, skip_received),
                ckv_block,
            ],
            row,
        )
        four_own = lax.all_gather(four_block, DP, axis=0, tiled=True)
        two_block = blocks_by_latents(
            [block_of_rows(w_up, four_own), block_of_columns(w_down, four_own)], row
        )
        two_own = lax.all_gather(two_block, DP, axis=0, tiled=True)
        four_other = other_core(four_own)

        def both(start, count):
            return jnp.concatenate(
                [four_own[:, start : start + count], four_other[:, start : start + count]], axis=1
            )

        step = width + (-width) % 128
        out_all = both(0, width)
        cquery_all = both(step, width)
        cout_all = both(2 * step, width)
        ckv_all = both(3 * step, 2 * width).reshape(lax.axis_size(DP), -1, 4 * width)
        ckv_all = ckv_all[:, :ckv_rows].reshape(-1, 4 * width)
        two_other = other_core(two_own)
        hidden_own = two_own.shape[1] // 2
        up_all = jnp.concatenate([two_own[:, :hidden_own], two_other[:, :hidden_own]], axis=1)
        down_all = jnp.concatenate([two_own[:, hidden_own:], two_other[:, hidden_own:]], axis=1)

    freq_here = w_mod.shape[0]
    mask_all = valid.astype(F32)
    emb = time_embed(steps).astype(BF)
    emb_here = lax.dynamic_slice_in_dim(emb, lax.axis_index(COL) * freq_here, freq_here, 1)
    shift_part = mult(emb_here, w_mod)
    vectors = jnp.concatenate(
        [jnp.stack([g_one, b_one, g_three, b_three, g_two, b_two]).reshape(-1), shift_part[0]]
    )
    gathered = copied_to_each(vectors, ROW_COL)
    gains = jnp.transpose(gathered[:, : 6 * width].reshape(8, 6, width), (1, 0, 2)).reshape(6, D)
    gain_one, offset_one, gain_three, offset_three, gain_two, offset_two = gains
    shift = jnp.sum(gathered[:, 6 * width :].reshape(2, 4, D // 2), axis=1).reshape(D)
    mask = lax.dynamic_slice_in_dim(mask_all, core * HALF + turn, PIECE, 0)

    cosine, sine = rope_tables(own_tokens(positions.T).T)
    prep = partial(qk_prep, cosine=cosine[:, None, :], sine=sine[:, None, :])

    joined = jnp.concatenate([hidden, skipped], axis=1)
    mine = own_tokens(joined)
    theirs = other_core(other_tokens(joined))
    pairs = jnp.concatenate([mine, theirs], axis=1).astype(F32)
    skip_vectors = jnp.stack([g_skip, b_skip]).reshape(2, 2 * width)
    both_vectors = jnp.concatenate([skip_vectors, other_core(skip_vectors)], axis=1)
    skip_sums = sum_over_chips(jnp.stack([jnp.sum(pairs, axis=1), jnp.sum(pairs * pairs, axis=1)]))
    skip_mean = skip_sums[0] / (2 * D)
    skip_rstd = lax.rsqrt(skip_sums[1] / (2 * D) - skip_mean * skip_mean + epsilon)
    skip_scaled = (pairs - skip_mean[:, None]) * skip_rstd[:, None]
    normed = (skip_scaled * both_vectors[0] + both_vectors[1]).astype(BF)
    stream = scatter_tokens(mult_right(normed, skip_all))

    normed_one, scaled_one, rstd_one = norm_forward(stream, gain_one, offset_one)
    text_sent = text[0] + settled(rstd_one).astype(BF)
    wide_text = jnp.transpose(copied_to_each(text_sent, ROW_COL), (1, 0, 2)).reshape(TXT, -1)
    wide_one = gather_tokens((normed_one + shift).astype(BF))
    packed = (mult(wide_one, qkv_all) + settled(wide_text)).reshape(HALF, heads, 3, HD)
    query_raw = packed[:, :, 0]
    key_raw = packed[:, :, 1]
    query = prep(query_raw, g_query).astype(BF).reshape(shape_four)
    keys_here = prep(key_raw, g_key).astype(BF)
    values_here = packed[:, :, 2].astype(BF)

    def swapped_heads(values):
        return jnp.concatenate([values[:, heads_own:], values[:, :heads_own]], axis=1)

    key_values = other_core(swapped_heads(jnp.concatenate([keys_here, values_here], axis=2)))
    keys = jnp.concatenate([keys_here, key_values[..., :HD]], axis=0)[None]
    values = jnp.concatenate([values_here, key_values[..., HD:]], axis=0)[None]
    mixed, self_totals = attend_forward(query, keys, values)
    mixed_here = mixed.reshape(HALF, heads * HD).astype(BF)
    late = settled(mixed_here)
    counts = copied_to_each(jnp.broadcast_to(jnp.sum(mask_all), (1, 128)) + late, DP)
    count = jnp.sum(counts[:, 0, 0])
    teacher_blocks = jnp.transpose(
        teacher.reshape(2, CHIPS, PIECE, width) + late.astype(BF), (1, 0, 2, 3)
    ).reshape(2 * CHIPS, PIECE, width)
    teacher_here = jnp.transpose(
        lax.all_to_all(teacher_blocks, ROW_COL, 0, 0, tiled=True), (1, 0, 2)
    ).reshape(PIECE, D)
    early = settled(count) + settled(teacher_here)
    stream_two = stream + early + scatter_tokens(mult_right(mixed_here, out_all))

    normed_three, scaled_three, rstd_three = norm_forward(stream_two, gain_three, offset_three)
    wide_three = gather_tokens(normed_three.astype(BF))
    cquery_raw = mult(wide_three, cquery_all).reshape(HALF, heads, HD)
    cquery = prep(cquery_raw, g_cquery).astype(BF).reshape(shape_four)
    ckv = mult(wide_text, ckv_all).reshape(1, TXT, heads, 2, HD)
    ckey_raw = ckv[:, :, :, 0]
    ckeys = head_norm(ckey_raw, g_ckey).astype(BF)
    cvalues = ckv[:, :, :, 1].astype(BF)
    cmixed, cross_totals = attend_forward(cquery, ckeys, cvalues)
    cmixed_here = cmixed.reshape(HALF, heads * HD).astype(BF)
    stream_three = stream_two + scatter_tokens(mult_right(cmixed_here, cout_all))

    normed_two, scaled_two, rstd_two = norm_forward(stream_three, gain_two, offset_two)
    wide_two = gather_tokens(normed_two.astype(BF))
    upper = mult(wide_two, up_all)
    active, gelu_back = jax.vjp(gelu_tanh, upper)
    active_here = active.astype(BF)
    output_here = stream_three + scatter_tokens(mult_right(active_here, down_all))

    diff = output_here - teacher_here.astype(F32)
    sse_local = jnp.sum(mask[:, None] * diff * diff)
    factor = 32.0 * lax.axis_size(DP) / count
    grad_out = factor * mask[:, None] * diff
    output_blocks = jnp.transpose(
        output_here.astype(BF).reshape(PIECE, 2 * CHIPS, width), (1, 0, 2)
    )
    output_back = lax.all_to_all(output_blocks, ROW_COL, 0, 0, tiled=True)
    output = jnp.transpose(
        output_back.reshape(CHIPS, 2, PIECE, width), (1, 0, 2, 3)
    ).reshape(SEQ, width).astype(F32)

    wide_grad = gather_tokens(grad_out.astype(BF))
    d_upper = gelu_back(mult(wide_grad, down_all))[0].astype(BF)
    d_normed_two = scatter_tokens(mult_right(d_upper, up_all))
    two_grads = weight_grads([(wide_two, d_upper), (wide_grad, active_here)])
    two_part = scattered_over_latents(two_grads)
    back_two, d_g_two, d_b_two = norm_backward(d_normed_two, scaled_two, rstd_two, gain_two)
    grad_three = grad_out + back_two

    wide_three_grad = gather_tokens(grad_three.astype(BF))
    d_cmixed = mult(wide_three_grad, cout_all) + settled(two_grads)
    d_cmixed = d_cmixed.astype(BF).reshape(shape_four)
    d_cquery, d_ckeys, d_cvalues = attend_backward(cquery, ckeys, cvalues, cross_totals, d_cmixed)
    unused, cquery_back = jax.vjp(prep, cquery_raw, g_cquery)
    d_cquery_raw, d_g_cquery = cquery_back(d_cquery.reshape(HALF, heads, HD))
    d_cquery_here = d_cquery_raw.reshape(HALF, heads * HD).astype(BF)
    d_normed_three = scatter_tokens(mult_right(d_cquery_here, cquery_all))
    unused, ckey_back = jax.vjp(head_norm, ckey_raw, g_ckey)
    d_ckey_raw, d_g_ckey = ckey_back(d_ckeys)
    d_ckv = jnp.stack([d_ckey_raw, d_cvalues], axis=3).reshape(TXT, heads * 2 * HD).astype(BF)
    back_three, d_g_three, d_b_three = norm_backward(
        d_normed_three + settled(output_back), scaled_three, rstd_three, gain_three
    )
    grad_two = grad_three + back_three

    three_grads = weight_grads(
        [(wide_three, d_cquery_here), (wide_three_grad, cmixed_here), (wide_text, d_ckv)]
    )
    three_part = summed_over_latents(three_grads)

    wide_two_grad = gather_tokens(grad_two.astype(BF))
    d_mixed = mult(wide_two_grad, out_all) + settled(three_grads)
    d_mixed = d_mixed.astype(BF).reshape(shape_four)
    d_query, d_keys, d_values = attend_backward(query, keys, values, self_totals, d_mixed)
    d_both = jnp.concatenate([d_keys[0], d_values[0]], axis=2)
    d_both = d_both[:HALF] + other_core(swapped_heads(d_both[HALF:]).astype(BF)).astype(F32)
    unused, query_back = jax.vjp(prep, query_raw, g_query)
    d_query_raw, d_g_query = query_back(d_query.reshape(HALF, heads, HD))
    unused, key_back = jax.vjp(prep, key_raw, g_key)
    d_key_raw, d_g_key = key_back(d_both[..., :HD])
    d_packed = (
        jnp.stack([d_query_raw, d_key_raw, d_both[..., HD:]], axis=2)
        .reshape(HALF, heads * 3 * HD)
        .astype(BF)
    )
    d_inputs = scatter_tokens(mult_right(d_packed, qkv_all))
    d_inputs = d_inputs + (settled(two_part) + settled(three_part))
    back_one, d_g_one, d_b_one = norm_backward(d_inputs, scaled_one, rstd_one, gain_one)
    grad_one = grad_two + back_one

    d_shift_part = jnp.sum(d_inputs, axis=0)
    shared = jnp.concatenate([d_g_query, d_g_key, d_g_cquery, d_g_ckey, sse_local[None]])
    small = jnp.stack(
        [d_g_one, d_b_one, d_g_three, d_b_three, d_g_two, d_b_two, d_shift_part]
        + [jnp.pad(shared, (0, D - shared.shape[0]))]
    )
    piece = jnp.concatenate([grad_one.astype(BF), in_two(small)], axis=0)
    pieces = [piece] + [from_chip(piece, j) for j in range(1, CHIPS)]
    wide_one_grad = jnp.concatenate([p[:PIECE] for p in pieces], axis=0)
    small = sum(p[PIECE:].astype(F32) for p in pieces)
    small = small[:8] + small[8:]
    small = small + other_core(small)
    oq_part = summed_over_latents(
        weight_grads([(wide_two_grad, mixed_here), (wide_one, d_packed)])
    )
    d_joined = mult(wide_one_grad, skip_all) + settled(oq_part)
    skip_sums = jnp.stack([jnp.sum(d_joined * skip_scaled, axis=0), jnp.sum(d_joined, axis=0)])
    skip_sums = skip_sums[:, : 2 * width] + other_core(skip_sums[:, 2 * width :])
    place = lax.axis_index(ROW_COL)
    shared_size = shared.shape[0]
    vector = jnp.concatenate(
        [
            lax.dynamic_slice_in_dim(small[:6], place * width, width, 1).reshape(-1),
            small[7, :shared_size],
            skip_sums.reshape(-1),
        ]
    )
    vector = jnp.pad(vector, (0, -vector.shape[0] % (D // 2))).reshape(-1, D // 2)
    vector_rows = vector.shape[0]
    latent_shift = lax.dynamic_slice_in_dim(small[6], row * (D // 2), D // 2, 0).astype(BF)
    d_w_mod = mult_left(emb_here, latent_shift[None])
    extra = jnp.concatenate([in_two(vector), d_w_mod.astype(BF)], axis=0).T
    extra = jnp.concatenate([extra, extra], axis=0)
    d_skip = weight_grads([(wide_one_grad, normed)])
    last_sent = jnp.concatenate([d_skip, extra], axis=1)
    skip_part = summed_over_latents(last_sent, 2 * width, vector_rows)
    both_gains = both_vectors[0] + settled(d_skip) + settled(skip_sums)
    weighted = d_joined * both_gains
    back_sums = sum_over_chips(
        jnp.stack([jnp.sum(weighted, axis=1), jnp.sum(weighted * skip_scaled, axis=1)])
    ) / (2 * D)
    back_joined = skip_rstd[:, None] * (
        weighted - back_sums[0][:, None] - skip_scaled * back_sums[1][:, None]
    )
    back_mine = back_joined[:, : 2 * width]
    back_theirs = other_core(back_joined[:, 2 * width :])
    unturn = (CHIPS - chip) % CHIPS * PIECE
    back_mine = turned(back_mine, unturn)
    back_theirs = turned(back_theirs, unturn)
    back_tokens = lax.dynamic_slice_in_dim(
        jnp.concatenate([back_mine, back_theirs, back_mine], axis=0), core * HALF, SEQ, 0
    )
    d_hidden = back_tokens[:, :width]
    d_skipped = back_tokens[:, width:]

    five_grads = spread_over_latents(jnp.concatenate([two_part, three_part], axis=1), row)
    def columns(summed, start, count):
        return jnp.concatenate(
            [summed[0, :, start : start + count], summed[1, :, start : start + count]], axis=1
        ).astype(F32)

    n_up = w_up.shape[1] // 2
    d_w_up = columns(five_grads, 0, n_up)
    d_w_down = columns(five_grads, n_up, n_up).T
    d_w_cquery = columns(five_grads, 2 * n_up, width)
    d_w_cout = columns(five_grads, 2 * n_up + width, width).T
    d_w_ckv = columns(five_grads, 2 * n_up + 2 * width, 2 * width)
    count_blocks = max(lax.axis_size(DP) // 2, 1)
    d_w_ckv = d_w_ckv.reshape(count_blocks, -1, 4 * width)[:, : w_ckv.shape[0] // count_blocks]
    d_w_ckv = d_w_ckv.reshape(-1, 4 * width)
    last_grads = spread_over_latents(jnp.concatenate([oq_part, skip_part], axis=1), row, False)
    last_grads = last_grads + (
        settled(d_w_up) + settled(d_w_down) + settled(d_w_cquery) + settled(d_w_cout) + settled(d_w_ckv)
    ).astype(BF)
    d_w_out = columns(last_grads, 0, width).T
    d_w_qkv = columns(last_grads, width, 3 * width)
    d_w_skip = columns(last_grads, 4 * width, 2 * width).reshape(D // 2, 2, 2, width)
    d_w_skip = jnp.transpose(d_w_skip, (2, 1, 3, 0)).reshape(2, 2 * width, D // 2)
    extra = last_grads[:, :, 6 * width :]
    extra = jnp.where(row == 0, extra[0], extra[1]).astype(F32).T
    vector = (extra[:vector_rows] + extra[vector_rows : 2 * vector_rows]).reshape(-1)
    d_w_mod = extra[2 * vector_rows :]
    d_g_one, d_b_one, d_g_three, d_b_three, d_g_two, d_b_two = vector[: 6 * width].reshape(6, width)
    shared = vector[6 * width : 6 * width + shared_size]
    d_g_query, d_g_key, d_g_cquery, d_g_ckey = shared[: 4 * HD].reshape(4, HD)
    loss = shared[4 * HD] / (count * D)
    skip_sums = vector[6 * width + shared_size : 10 * width + shared_size].reshape(2, 2, width)
    d_g_skip, d_b_skip = skip_sums
    return (
        output,
        d_hidden,
        d_skipped,
        d_w_skip,
        d_g_skip,
        d_b_skip,
        d_w_mod,
        d_g_one,
        d_b_one,
        d_w_qkv,
        d_g_query,
        d_g_key,
        d_w_out,
        d_g_three,
        d_b_three,
        d_w_cquery,
        d_w_ckv,
        d_g_cquery,
        d_g_ckey,
        d_w_cout,
        d_g_two,
        d_b_two,
        d_w_up,
        d_w_down,
        loss,
    )


def solution(mesh):
    side = math.isqrt(mesh.shape["dp"])
    split = Mesh(
        mesh.devices.reshape(side, side, mesh.shape["row"], 2, 2),
        ("dp_0", "dp_1", "row", "col_0", "col_1"),
    )
    in_specs = (
        P(DP, COL_ROW),
        P(DP, COL_ROW),
        P(DP, None, ROW_COL),
        P(DP, ROW_COL),
        P(DP),
        P(DP),
        P(None, DP),
        P(None, COL, "row"),
        P(None, COL_ROW),
        P(None, COL_ROW),
        P(COL, "row"),
        P(ROW_COL),
        P(ROW_COL),
        P("row", COL),
        P(),
        P(),
        P(COL, "row"),
        P(ROW_COL),
        P(ROW_COL),
        P("row", COL),
        P("row", COL),
        P(),
        P(),
        P(COL, "row"),
        P(ROW_COL),
        P(ROW_COL),
        P("row", COL),
        P(COL, "row"),
    )
    out_specs = (
        P(DP, ROW_COL),
        P(DP, COL_ROW),
        P(DP, COL_ROW),
        P(None, COL, "row"),
        P(None, COL_ROW),
        P(None, COL_ROW),
        P(COL, "row"),
        P(ROW_COL),
        P(ROW_COL),
        P("row", COL),
        P(),
        P(),
        P(COL, "row"),
        P(ROW_COL),
        P(ROW_COL),
        P("row", COL),
        P("row", COL),
        P(),
        P(),
        P(COL, "row"),
        P(ROW_COL),
        P(ROW_COL),
        P("row", COL),
        P(COL, "row"),
        P(),
    )
    return jax.shard_map(local, mesh=split, in_specs=in_specs, out_specs=out_specs, check_vma=False)
```

```python
from functools import partial
import math

import jax
import jax.numpy as jnp
from jax import lax
from jax.sharding import Mesh
from jax.sharding import PartitionSpec as P

D = 1408
HEADS = 16
HD = 88
FREQ = 256
TXT = 333
SEQ = 1024
LINE = ("row", "col_0")
CORE = "col_1"
COL = ("col_0", "col_1")
ROW_COL = ("row", "col_0", "col_1")
DP = ("dp_0", "dp_1")
ALL = ("dp_0", "dp_1", "row", "col_0", "col_1")
COL_ROW = ("col_0", "col_1", "row")
CHIPS = 4
HALF = SEQ // 2
PIECE = HALF // CHIPS
BF = jnp.bfloat16
F32 = jnp.float32


epsilon = 1e-06


def mult(left, right):
    return jnp.dot(left, right, preferred_element_type=jnp.float32)


def mult_left(left, right):
    return lax.dot_general(
        left, right, (((0,), (0,)), ((), ())), preferred_element_type=jnp.float32
    )


def mult_right(left, right):
    return lax.dot_general(
        left, right, (((1,), (1,)), ((), ())), preferred_element_type=jnp.float32
    )


def from_chip(value, ahead):
    return lax.ppermute(value, LINE, [(i, (i - ahead) % CHIPS) for i in range(CHIPS)])


def other_core(value):
    return lax.ppermute(value, CORE, [(0, 1), (1, 0)])


def other_row(value):
    return lax.ppermute(value, "row", [(0, 1), (1, 0)])


def gather_tokens(piece):
    return jnp.concatenate([piece] + [from_chip(piece, j) for j in range(1, CHIPS)], axis=0)


def scatter_tokens(partial_sums):
    total = partial_sums[:PIECE]
    for j in range(1, CHIPS):
        sent = partial_sums[j * PIECE : (j + 1) * PIECE].astype(BF)
        total = total + from_chip(sent, CHIPS - j).astype(F32)
    return total


def sum_over_chips(value):
    total = value
    for j in range(1, CHIPS):
        total = total + jnp.roll(from_chip(value, j), j * PIECE, axis=1)
    return total


def turned(value, start):
    twice = jnp.concatenate([value, value], axis=0)
    return lax.dynamic_slice_in_dim(twice, start, value.shape[0], 0)


def norm_forward(values, gain, offset):
    mean = jnp.mean(values, axis=1, keepdims=True)
    spread = jnp.mean(values * values, axis=1, keepdims=True) - mean * mean
    rstd = lax.rsqrt(spread + epsilon)
    scaled = (values - mean) * rstd
    return (scaled * gain + offset, scaled, rstd)


def norm_backward(grad, scaled, rstd, gain):
    weighted = grad * gain
    first = jnp.mean(weighted, axis=1, keepdims=True)
    second = jnp.mean(weighted * scaled, axis=1, keepdims=True)
    back = rstd * (weighted - first - scaled * second)
    return (back, jnp.sum(grad * scaled, axis=0), jnp.sum(grad, axis=0))


def halves_swapped(weight, dim, row, after=None):
    if after is not None:
        row = row + settled_index(after)
    kept = lax.dynamic_slice_in_dim(weight, row * (weight.shape[dim] // 2), weight.shape[dim] // 2, dim)
    sent = lax.dynamic_slice_in_dim(
        weight, (1 - row) * (weight.shape[dim] // 2), weight.shape[dim] // 2, dim
    )
    return (kept, other_row(sent))


def in_row_order(kept, received, dim, row):
    three = jnp.concatenate([received, kept, received], axis=dim)
    return lax.dynamic_slice_in_dim(
        three, (1 - row) * kept.shape[dim], 2 * kept.shape[dim], dim
    )


def settled(value):
    return jnp.minimum(jnp.abs(value[(0,) * value.ndim].astype(F32)), 0.0)


def settled_index(value):
    return settled(value).astype(jnp.int32)


def copied_to_each(value, axis):
    length = lax.axis_size(axis)
    return lax.all_to_all(
        jnp.broadcast_to(value[None], (length, *value.shape)), axis, 0, 0, tiled=True
    )


def in_two(value):
    high = lax.reduce_precision(value, exponent_bits=8, mantissa_bits=7)
    return jnp.concatenate([high.astype(BF), (value - high).astype(BF)], axis=0)


def with_other_core(own):
    return jnp.concatenate([own, other_core(own)], axis=1)


def whole_columns(weight, row, after=None):
    kept, received = halves_swapped(weight, 1, row, after)
    return in_row_order(kept, received, 0, row)


def padded(value):
    return jnp.pad(value, ((0, 0), (0, -value.shape[1] % 128)))


def blocks_by_latents(blocks, row):
    half = lax.axis_size(DP) // 2
    kept, sent = [], []
    for block in blocks:
        n = block.shape[1] // 2
        kept.append(padded(lax.dynamic_slice_in_dim(block, row * n, n, 1)))
        sent.append(padded(lax.dynamic_slice_in_dim(block, (1 - row) * n, n, 1)))
    kept = jnp.concatenate(kept, axis=1) if len(kept) > 1 else kept[0]
    sent = jnp.concatenate(sent, axis=1) if len(sent) > 1 else sent[0]
    return jnp.where(lax.axis_index(DP) // half == row, kept, other_row(sent))


def block_of_rows(weight, after):
    half = lax.axis_size(DP) // 2
    rows = weight.shape[0] // half
    place = lax.axis_index(DP) % half + settled_index(after)
    return lax.dynamic_slice_in_dim(weight, place * rows, rows, 0)


def block_of_columns(weight, after):
    half = lax.axis_size(DP) // 2
    columns = weight.shape[1] // half
    place = lax.axis_index(DP) % half + settled_index(after)
    return lax.dynamic_slice_in_dim(weight, place * columns, columns, 1).T


def weight_grads(pairs):
    def products(part):
        outs = []
        for left, right in pairs:
            n = right.shape[1] // 2
            out = mult_left(left, right[:, part * n : (part + 1) * n])
            short = pairs[0][0].shape[1] - out.shape[0]
            if short:
                count = 2 * max(lax.axis_size(DP) // 2, 1)
                out = out.reshape(count, -1, n)
                out = jnp.pad(out, ((0, 0), (0, short // count), (0, 0))).reshape(-1, n)
            outs.append(out)
        return jnp.concatenate(outs, axis=1) if len(outs) > 1 else outs[0]

    theirs = other_core(products(1).astype(BF))
    return (products(0) + theirs.astype(F32)).astype(BF)


def to_row_half(part):
    count = lax.axis_size(DP)
    half = count // 2
    pairs = []
    for i in range(count):
        for r in range(2):
            stays = i // half == r
            pairs.append((2 * i + r, 2 * i + r if stays else 2 * ((i + half) % count) + 1 - r))
    return lax.ppermute(part, DP + ("row",), pairs)


def row_halves(grads, row):
    kept, received = halves_swapped(grads, 0, row)
    first = row == 0
    return (jnp.where(first, kept, received), jnp.where(first, received, kept))


def summed_over_latents(grads, start=0, pairs_of=0, after=()):
    count = lax.axis_size(DP)
    if count == 1:
        return grads
    rows, n = grads.shape
    arrived = lax.all_to_all(grads.reshape(count, rows // count, n), DP, 0, 0, tiled=True)
    part = jnp.sum(arrived.astype(F32), axis=0)
    for value in after:
        part = part + settled(value)
    if pairs_of:
        exact = part[:, start : start + pairs_of] + part[:, start + pairs_of : start + 2 * pairs_of]
        rest = part[:, start + 2 * pairs_of :].astype(BF)
        part = jnp.concatenate([part[:, :start].astype(BF), in_two(exact.T).T, rest], axis=1)
    else:
        part = part.astype(BF)
    return to_row_half(part)


def spread_over_latents(part, row, gather=True):
    count = lax.axis_size(DP)
    if count == 1:
        return jnp.stack(row_halves(part, row))
    rows, n = part.shape
    if gather:
        spread = lax.all_gather(part, DP, axis=0)
    else:
        spread = copied_to_each(part, DP)
    return spread.reshape(2, count // 2 * rows, n)


def head_norm(values, gain):
    mean = jnp.mean(values, axis=-1, keepdims=True)
    spread = jnp.mean(values * values, axis=-1, keepdims=True) - mean * mean
    return (values - mean) * lax.rsqrt(spread + epsilon) * gain


def rotate(values):
    quarter = values.shape[-1] // 4
    return jnp.concatenate(
        [
            -values[..., quarter : 2 * quarter],
            values[..., :quarter],
            -values[..., 3 * quarter :],
            values[..., 2 * quarter : 3 * quarter],
        ],
        axis=-1,
    )


def qk_prep(raw, gain, cosine, sine):
    normal = head_norm(raw, gain)
    return normal * cosine + rotate(normal) * sine


def gelu_tanh(values):
    return jax.nn.gelu(values, approximate=True)


def rope_tables(positions):
    quarter = HD // 4
    freqs = jnp.exp(-math.log(10000.0) * jnp.arange(quarter, dtype=jnp.float32) / quarter)
    rows_angle = positions[0].astype(jnp.float32)[:, None] * freqs[None, :]
    cols_angle = positions[1].astype(jnp.float32)[:, None] * freqs[None, :]
    cosine = jnp.concatenate(
        [jnp.cos(rows_angle), jnp.cos(rows_angle), jnp.cos(cols_angle), jnp.cos(cols_angle)], axis=1
    )
    sine = jnp.concatenate(
        [jnp.sin(rows_angle), jnp.sin(rows_angle), jnp.sin(cols_angle), jnp.sin(cols_angle)], axis=1
    )
    return (cosine, sine)


def time_embed(steps):
    half = FREQ // 2
    freqs = jnp.exp(-math.log(10000.0) * jnp.arange(half, dtype=jnp.float32) / half)
    angles = steps.astype(jnp.float32)[:, None] * freqs[None, :]
    return jnp.concatenate([jnp.cos(angles), jnp.sin(angles)], axis=1)


def attend_forward(query, keys, values):
    scale = HD ** (-0.5)
    length = query.shape[1]
    block = min(512, length)
    outputs = []
    totals = []
    for start in range(0, length, block):
        piece = query[:, start : start + block]
        scores = scale * jnp.einsum(
            "lqhd,lkhd->lhqk", piece, keys, preferred_element_type=jnp.float32
        )
        top = jnp.max(scores, axis=-1, keepdims=True)
        expo = jnp.exp(scores - top)
        summed = jnp.sum(expo, axis=-1, keepdims=True)
        weights = expo / summed
        totals.append(top[..., 0] + jnp.log(summed[..., 0]))
        outputs.append(
            jnp.einsum(
                "lhqk,lkhd->lqhd",
                weights.astype(jnp.bfloat16),
                values,
                preferred_element_type=jnp.float32,
            )
        )
    return (jnp.concatenate(outputs, axis=1), jnp.concatenate(totals, axis=2))


def attend_backward(query, keys, values, totals, grad_out):
    scale = HD ** (-0.5)
    length = query.shape[1]
    block = min(512, length)
    d_keys = jnp.zeros(keys.shape, jnp.float32)
    d_values = jnp.zeros(values.shape, jnp.float32)
    d_query = []
    for start in range(0, length, block):
        piece = query[:, start : start + block]
        grad_piece = grad_out[:, start : start + block]
        scores = scale * jnp.einsum(
            "lqhd,lkhd->lhqk", piece, keys, preferred_element_type=jnp.float32
        )
        weights = jnp.exp(scores - totals[:, :, start : start + block, None])
        d_weights = jnp.einsum(
            "lqhd,lkhd->lhqk", grad_piece, values, preferred_element_type=jnp.float32
        )
        d_scores = weights * (d_weights - jnp.sum(d_weights * weights, axis=-1, keepdims=True))
        d_scores_b = d_scores.astype(jnp.bfloat16)
        d_query.append(
            scale
            * jnp.einsum("lhqk,lkhd->lqhd", d_scores_b, keys, preferred_element_type=jnp.float32)
        )
        d_keys = d_keys + scale * jnp.einsum(
            "lhqk,lqhd->lkhd", d_scores_b, piece, preferred_element_type=jnp.float32
        )
        d_values = d_values + jnp.einsum(
            "lhqk,lqhd->lkhd",
            weights.astype(jnp.bfloat16),
            grad_piece,
            preferred_element_type=jnp.float32,
        )
    return (jnp.concatenate(d_query, axis=1), d_keys, d_values)


def local(
    hidden,
    skipped,
    text,
    teacher,
    valid,
    steps,
    positions,
    w_skip,
    g_skip,
    b_skip,
    w_mod,
    g_one,
    b_one,
    w_qkv,
    g_query,
    g_key,
    w_out,
    g_three,
    b_three,
    w_cquery,
    w_ckv,
    g_cquery,
    g_ckey,
    w_cout,
    g_two,
    b_two,
    w_up,
    w_down,
):
    row = lax.axis_index("row")
    chip = lax.axis_index(LINE)
    core = lax.axis_index(CORE)
    width = hidden.shape[1]
    turn = chip * PIECE
    heads_own = HEADS // (2 * CHIPS)
    heads = 2 * heads_own
    shape_four = (1, HALF, heads, HD)

    def own_tokens(values):
        return turned(lax.dynamic_slice_in_dim(values, core * HALF, HALF, 0), turn)

    def other_tokens(values):
        return turned(lax.dynamic_slice_in_dim(values, (1 - core) * HALF, HALF, 0), turn)

    skip_two = jnp.transpose(w_skip.reshape(2, 2, width, D // 2), (3, 1, 0, 2)).reshape(
        D // 2, 4 * width
    )
    skip_kept, skip_received = halves_swapped(skip_two, 1, row)
    skip_own = in_row_order(skip_kept, skip_received, 0, row)
    skip_other = other_core(skip_own)
    skip_all = jnp.concatenate([skip_own, skip_other], axis=1)
    qkv_all = with_other_core(whole_columns(w_qkv, row, skip_received))
    mask_all = valid.astype(F32)
    if lax.axis_size(DP) == 1:
        count = jnp.sum(mask_all)
        out_all = with_other_core(whole_columns(w_out.T, row))
        cquery_all = with_other_core(whole_columns(w_cquery, row))
        cout_all = with_other_core(whole_columns(w_cout.T, row))
        ckv_all = with_other_core(whole_columns(w_ckv, row))
        up_all = with_other_core(whole_columns(w_up, row))
        down_all = with_other_core(whole_columns(w_down.T, row))
    else:
        ckv_block = block_of_rows(w_ckv, skip_received)
        ckv_rows = ckv_block.shape[0]
        ckv_block = jnp.pad(ckv_block, ((0, D // lax.axis_size(DP) - ckv_rows), (0, 0)))
        four_block = blocks_by_latents(
            [
                block_of_columns(w_out, skip_received),
                block_of_rows(w_cquery, skip_received),
                block_of_columns(w_cout, skip_received),
                ckv_block,
            ],
            row,
        )
        tally = jnp.sum(mask_all)
        parts = jnp.stack([jnp.floor(tally / 32.0), tally - 32.0 * jnp.floor(tally / 32.0)])
        four_block = lax.dynamic_update_slice(four_block, parts.astype(BF)[None], (0, width))
        four_own = lax.all_gather(four_block, DP, axis=0, tiled=True)
        parts = four_own.reshape(lax.axis_size(DP), -1, four_own.shape[1])[:, 0, width : width + 2]
        count = jnp.sum(parts.astype(F32) @ jnp.array([32.0, 1.0], F32))
        two_block = blocks_by_latents(
            [block_of_rows(w_up, four_own), block_of_columns(w_down, four_own)], row
        )
        two_own = lax.all_gather(two_block, DP, axis=0, tiled=True)
        four_other = other_core(four_own)

        def both(start, count):
            return jnp.concatenate(
                [four_own[:, start : start + count], four_other[:, start : start + count]], axis=1
            )

        step = width + (-width) % 128
        out_all = both(0, width)
        cquery_all = both(step, width)
        cout_all = both(2 * step, width)
        ckv_all = both(3 * step, 2 * width).reshape(lax.axis_size(DP), -1, 4 * width)
        ckv_all = ckv_all[:, :ckv_rows].reshape(-1, 4 * width)
        two_other = other_core(two_own)
        hidden_own = two_own.shape[1] // 2
        up_all = jnp.concatenate([two_own[:, :hidden_own], two_other[:, :hidden_own]], axis=1)
        down_all = jnp.concatenate([two_own[:, hidden_own:], two_other[:, hidden_own:]], axis=1)

    freq_here = w_mod.shape[0]
    mask_all = valid.astype(F32)
    emb = time_embed(steps).astype(BF)
    emb_here = lax.dynamic_slice_in_dim(emb, lax.axis_index(COL) * freq_here, freq_here, 1)
    shift_part = mult(emb_here, w_mod)
    vectors = jnp.concatenate(
        [jnp.stack([g_one, b_one, g_three, b_three, g_two, b_two]).reshape(-1), shift_part[0]]
    )
    gathered = copied_to_each(vectors, ROW_COL)
    gains = jnp.transpose(gathered[:, : 6 * width].reshape(8, 6, width), (1, 0, 2)).reshape(6, D)
    gain_one, offset_one, gain_three, offset_three, gain_two, offset_two = gains
    shift = jnp.sum(gathered[:, 6 * width :].reshape(2, 4, D // 2), axis=1).reshape(D)
    mask = lax.dynamic_slice_in_dim(mask_all, core * HALF + turn, PIECE, 0)

    cosine, sine = rope_tables(own_tokens(positions.T).T)
    prep = partial(qk_prep, cosine=cosine[:, None, :], sine=sine[:, None, :])

    joined = jnp.concatenate([hidden, skipped], axis=1)
    mine = own_tokens(joined)
    theirs = other_core(other_tokens(joined))
    pairs = jnp.concatenate([mine, theirs], axis=1).astype(F32)
    skip_vectors = jnp.stack([g_skip, b_skip]).reshape(2, 2 * width)
    both_vectors = jnp.concatenate([skip_vectors, other_core(skip_vectors)], axis=1)
    skip_sums = sum_over_chips(jnp.stack([jnp.sum(pairs, axis=1), jnp.sum(pairs * pairs, axis=1)]))
    skip_mean = skip_sums[0] / (2 * D)
    skip_rstd = lax.rsqrt(skip_sums[1] / (2 * D) - skip_mean * skip_mean + epsilon)
    skip_scaled = (pairs - skip_mean[:, None]) * skip_rstd[:, None]
    normed = (skip_scaled * both_vectors[0] + both_vectors[1]).astype(BF)
    stream = scatter_tokens(mult_right(normed, skip_all))

    normed_one, scaled_one, rstd_one = norm_forward(stream, gain_one, offset_one)
    text_sent = text[0] + settled(rstd_one).astype(BF)
    wide_text = jnp.transpose(copied_to_each(text_sent, ROW_COL), (1, 0, 2)).reshape(TXT, -1)
    wide_one = gather_tokens((normed_one + shift).astype(BF))
    packed = (mult(wide_one, qkv_all) + settled(wide_text)).reshape(HALF, heads, 3, HD)
    query_raw = packed[:, :, 0]
    key_raw = packed[:, :, 1]
    query = prep(query_raw, g_query).astype(BF).reshape(shape_four)
    keys_here = prep(key_raw, g_key).astype(BF)
    values_here = packed[:, :, 2].astype(BF)

    def swapped_heads(values):
        return jnp.concatenate([values[:, heads_own:], values[:, :heads_own]], axis=1)

    key_values = other_core(swapped_heads(jnp.concatenate([keys_here, values_here], axis=2)))
    keys = jnp.concatenate([keys_here, key_values[..., :HD]], axis=0)[None]
    values = jnp.concatenate([values_here, key_values[..., HD:]], axis=0)[None]
    mixed, self_totals = attend_forward(query, keys, values)
    mixed_here = mixed.reshape(HALF, heads * HD).astype(BF)
    stream_two = stream + scatter_tokens(mult_right(mixed_here, out_all))

    normed_three, scaled_three, rstd_three = norm_forward(stream_two, gain_three, offset_three)
    teacher_blocks = jnp.transpose(
        teacher.reshape(2, CHIPS, PIECE, width) + settled(rstd_three).astype(BF), (1, 0, 2, 3)
    ).reshape(2 * CHIPS, PIECE, width)
    teacher_here = jnp.transpose(
        lax.all_to_all(teacher_blocks, ROW_COL, 0, 0, tiled=True), (1, 0, 2)
    ).reshape(PIECE, D)
    wide_three = gather_tokens(normed_three.astype(BF))
    cquery_raw = mult(wide_three, cquery_all) + settled(teacher_here)
    cquery_raw = cquery_raw.reshape(HALF, heads, HD)
    cquery = prep(cquery_raw, g_cquery).astype(BF).reshape(shape_four)
    ckv = mult(wide_text, ckv_all).reshape(1, TXT, heads, 2, HD)
    ckey_raw = ckv[:, :, :, 0]
    ckeys = head_norm(ckey_raw, g_ckey).astype(BF)
    cvalues = ckv[:, :, :, 1].astype(BF)
    cmixed, cross_totals = attend_forward(cquery, ckeys, cvalues)
    cmixed_here = cmixed.reshape(HALF, heads * HD).astype(BF)
    stream_three = stream_two + scatter_tokens(mult_right(cmixed_here, cout_all))

    normed_two, scaled_two, rstd_two = norm_forward(stream_three, gain_two, offset_two)
    wide_two = gather_tokens(normed_two.astype(BF))
    upper = mult(wide_two, up_all)
    active, gelu_back = jax.vjp(gelu_tanh, upper)
    active_here = active.astype(BF)
    output_here = stream_three + scatter_tokens(mult_right(active_here, down_all))

    diff = output_here - teacher_here.astype(F32)
    sse_local = jnp.sum(mask[:, None] * diff * diff)
    factor = 32.0 * lax.axis_size(DP) / count
    grad_out = factor * mask[:, None] * diff
    output_blocks = jnp.transpose(
        output_here.astype(BF).reshape(PIECE, 2 * CHIPS, width), (1, 0, 2)
    )
    output_back = lax.all_to_all(output_blocks, ROW_COL, 0, 0, tiled=True)
    output = jnp.transpose(
        output_back.reshape(CHIPS, 2, PIECE, width), (1, 0, 2, 3)
    ).reshape(SEQ, width).astype(F32)

    wide_grad = gather_tokens(grad_out.astype(BF))
    d_upper = gelu_back(mult(wide_grad, down_all))[0].astype(BF)
    d_normed_two = scatter_tokens(mult_right(d_upper, up_all))
    two_grads = weight_grads([(wide_two, d_upper), (wide_grad, active_here)])
    d_normed_two = d_normed_two + settled(output_back)
    back_two, d_g_two, d_b_two = norm_backward(d_normed_two, scaled_two, rstd_two, gain_two)
    grad_three = grad_out + back_two

    wide_three_grad = gather_tokens(grad_three.astype(BF))
    d_cmixed = mult(wide_three_grad, cout_all).astype(BF).reshape(shape_four)
    d_cquery, d_ckeys, d_cvalues = attend_backward(cquery, ckeys, cvalues, cross_totals, d_cmixed)
    unused, cquery_back = jax.vjp(prep, cquery_raw, g_cquery)
    d_cquery_raw, d_g_cquery = cquery_back(d_cquery.reshape(HALF, heads, HD))
    d_cquery_here = d_cquery_raw.reshape(HALF, heads * HD).astype(BF)
    d_normed_three = scatter_tokens(mult_right(d_cquery_here, cquery_all))
    unused, ckey_back = jax.vjp(head_norm, ckey_raw, g_ckey)
    d_ckey_raw, d_g_ckey = ckey_back(d_ckeys)
    d_ckv = jnp.stack([d_ckey_raw, d_cvalues], axis=3).reshape(TXT, heads * 2 * HD).astype(BF)
    back_three, d_g_three, d_b_three = norm_backward(
        d_normed_three, scaled_three, rstd_three, gain_three
    )
    grad_two = grad_three + back_three

    three_grads = weight_grads(
        [(wide_three, d_cquery_here), (wide_three_grad, cmixed_here), (wide_text, d_ckv)]
    )
    two_sum, three_sum = lax.psum((two_grads, three_grads), DP)

    wide_two_grad = gather_tokens(grad_two.astype(BF))
    d_mixed = mult(wide_two_grad, out_all) + (settled(two_grads) + settled(three_grads))
    d_mixed = d_mixed.astype(BF).reshape(shape_four)
    d_query, d_keys, d_values = attend_backward(query, keys, values, self_totals, d_mixed)
    d_both = jnp.concatenate([d_keys[0], d_values[0]], axis=2)
    d_both = d_both[:HALF] + other_core(swapped_heads(d_both[HALF:]).astype(BF)).astype(F32)
    unused, query_back = jax.vjp(prep, query_raw, g_query)
    d_query_raw, d_g_query = query_back(d_query.reshape(HALF, heads, HD))
    unused, key_back = jax.vjp(prep, key_raw, g_key)
    d_key_raw, d_g_key = key_back(d_both[..., :HD])
    d_packed = (
        jnp.stack([d_query_raw, d_key_raw, d_both[..., HD:]], axis=2)
        .reshape(HALF, heads * 3 * HD)
        .astype(BF)
    )
    d_inputs = scatter_tokens(mult_right(d_packed, qkv_all))
    back_one, d_g_one, d_b_one = norm_backward(d_inputs, scaled_one, rstd_one, gain_one)
    grad_one = grad_two + back_one

    d_shift_part = jnp.sum(d_inputs, axis=0)
    shared = jnp.concatenate([d_g_query, d_g_key, d_g_cquery, d_g_ckey, sse_local[None]])
    small = jnp.stack(
        [d_g_one, d_b_one, d_g_three, d_b_three, d_g_two, d_b_two, d_shift_part]
        + [jnp.pad(shared, (0, D - shared.shape[0]))]
    )
    piece = jnp.concatenate([grad_one.astype(BF), in_two(small)], axis=0)
    pieces = [piece] + [from_chip(piece, j) for j in range(1, CHIPS)]
    wide_one_grad = jnp.concatenate([p[:PIECE] for p in pieces], axis=0)
    small = sum(p[PIECE:].astype(F32) for p in pieces)
    small = small[:8] + small[8:]
    small = small + other_core(small)
    oq_part = summed_over_latents(
        weight_grads([(wide_two_grad, mixed_here), (wide_one, d_packed)])
    )
    d_joined = mult(wide_one_grad, skip_all) + settled(oq_part)
    skip_sums = jnp.stack([jnp.sum(d_joined * skip_scaled, axis=0), jnp.sum(d_joined, axis=0)])
    skip_sums = skip_sums[:, : 2 * width] + other_core(skip_sums[:, 2 * width :])
    place = lax.axis_index(ROW_COL)
    shared_size = shared.shape[0]
    vector = jnp.concatenate(
        [
            lax.dynamic_slice_in_dim(small[:6], place * width, width, 1).reshape(-1),
            small[7, :shared_size],
            skip_sums.reshape(-1),
        ]
    )
    vector = jnp.pad(vector, (0, -vector.shape[0] % (D // 2))).reshape(-1, D // 2)
    vector_rows = vector.shape[0]
    latent_shift = lax.dynamic_slice_in_dim(small[6], row * (D // 2), D // 2, 0).astype(BF)
    d_w_mod = mult_left(emb_here, latent_shift[None])
    extra = jnp.concatenate([in_two(vector), d_w_mod.astype(BF)], axis=0).T
    extra = jnp.concatenate([extra, extra], axis=0)
    d_skip = weight_grads([(wide_one_grad, normed)])
    last_sent = jnp.concatenate([d_skip, extra], axis=1)
    n_up = w_up.shape[1] // 2
    up_halves = row_halves(two_sum[:, :n_up], row)
    down_halves = row_halves(two_sum[:, n_up:], row)
    three_halves = row_halves(three_sum, row)
    skip_part = summed_over_latents(
        last_sent, 2 * width, vector_rows, up_halves + three_halves
    )
    both_gains = both_vectors[0] + settled(d_skip) + settled(skip_sums)
    weighted = d_joined * both_gains
    back_sums = sum_over_chips(
        jnp.stack([jnp.sum(weighted, axis=1), jnp.sum(weighted * skip_scaled, axis=1)])
    ) / (2 * D)
    back_joined = skip_rstd[:, None] * (
        weighted - back_sums[0][:, None] - skip_scaled * back_sums[1][:, None]
    )
    back_mine = back_joined[:, : 2 * width]
    back_theirs = other_core(back_joined[:, 2 * width :])
    unturn = (CHIPS - chip) % CHIPS * PIECE
    back_mine = turned(back_mine, unturn)
    back_theirs = turned(back_theirs, unturn)
    back_tokens = lax.dynamic_slice_in_dim(
        jnp.concatenate([back_mine, back_theirs, back_mine], axis=0), core * HALF, SEQ, 0
    )
    d_hidden = back_tokens[:, :width]
    d_skipped = back_tokens[:, width:]

    def columns(summed, start, count):
        return jnp.concatenate(
            [summed[0][:, start : start + count], summed[1][:, start : start + count]], axis=1
        ).astype(F32)

    d_w_up = columns(up_halves, 0, n_up)
    d_w_down = columns(down_halves, 0, n_up).T
    d_w_cquery = columns(three_halves, 0, width)
    d_w_cout = columns(three_halves, width, width).T
    d_w_ckv = columns(three_halves, 2 * width, 2 * width)
    count_blocks = max(lax.axis_size(DP) // 2, 1)
    d_w_ckv = d_w_ckv.reshape(count_blocks, -1, 4 * width)[:, : w_ckv.shape[0] // count_blocks]
    d_w_ckv = d_w_ckv.reshape(-1, 4 * width)
    oq_grads = spread_over_latents(oq_part, row)
    last_grads = spread_over_latents(skip_part, row, False)
    d_w_out = columns(oq_grads, 0, width).T
    d_w_qkv = columns(oq_grads, width, 3 * width)
    d_w_skip = columns(last_grads, 0, 2 * width).reshape(D // 2, 2, 2, width)
    d_w_skip = jnp.transpose(d_w_skip, (2, 1, 3, 0)).reshape(2, 2 * width, D // 2)
    extra = last_grads[:, :, 2 * width :]
    extra = jnp.where(row == 0, extra[0], extra[1]).astype(F32).T
    vector = (extra[:vector_rows] + extra[vector_rows : 2 * vector_rows]).reshape(-1)
    d_w_mod = extra[2 * vector_rows :]
    d_g_one, d_b_one, d_g_three, d_b_three, d_g_two, d_b_two = vector[: 6 * width].reshape(6, width)
    shared = vector[6 * width : 6 * width + shared_size]
    d_g_query, d_g_key, d_g_cquery, d_g_ckey = shared[: 4 * HD].reshape(4, HD)
    loss = shared[4 * HD] / (count * D)
    skip_sums = vector[6 * width + shared_size : 10 * width + shared_size].reshape(2, 2, width)
    d_g_skip, d_b_skip = skip_sums
    return (
        output,
        d_hidden,
        d_skipped,
        d_w_skip,
        d_g_skip,
        d_b_skip,
        d_w_mod,
        d_g_one,
        d_b_one,
        d_w_qkv,
        d_g_query,
        d_g_key,
        d_w_out,
        d_g_three,
        d_b_three,
        d_w_cquery,
        d_w_ckv,
        d_g_cquery,
        d_g_ckey,
        d_w_cout,
        d_g_two,
        d_b_two,
        d_w_up,
        d_w_down,
        loss,
    )


def solution(mesh):
    side = math.isqrt(mesh.shape["dp"])
    split = Mesh(
        mesh.devices.reshape(side, side, mesh.shape["row"], 2, 2),
        ("dp_0", "dp_1", "row", "col_0", "col_1"),
    )
    in_specs = (
        P(DP, COL_ROW),
        P(DP, COL_ROW),
        P(DP, None, ROW_COL),
        P(DP, ROW_COL),
        P(DP),
        P(DP),
        P(None, DP),
        P(None, COL, "row"),
        P(None, COL_ROW),
        P(None, COL_ROW),
        P(COL, "row"),
        P(ROW_COL),
        P(ROW_COL),
        P("row", COL),
        P(),
        P(),
        P(COL, "row"),
        P(ROW_COL),
        P(ROW_COL),
        P("row", COL),
        P("row", COL),
        P(),
        P(),
        P(COL, "row"),
        P(ROW_COL),
        P(ROW_COL),
        P("row", COL),
        P(COL, "row"),
    )
    out_specs = (
        P(DP, ROW_COL),
        P(DP, COL_ROW),
        P(DP, COL_ROW),
        P(None, COL, "row"),
        P(None, COL_ROW),
        P(None, COL_ROW),
        P(COL, "row"),
        P(ROW_COL),
        P(ROW_COL),
        P("row", COL),
        P(),
        P(),
        P(COL, "row"),
        P(ROW_COL),
        P(ROW_COL),
        P("row", COL),
        P("row", COL),
        P(),
        P(),
        P(COL, "row"),
        P(ROW_COL),
        P(ROW_COL),
        P("row", COL),
        P(COL, "row"),
        P(),
    )
    return jax.shard_map(local, mesh=split, in_specs=in_specs, out_specs=out_specs, check_vma=False)
```

```python
from functools import partial
import math

import jax
import jax.numpy as jnp
from jax import lax
from jax.sharding import Mesh
from jax.sharding import PartitionSpec as P

D = 1408
HEADS = 16
HD = 88
FREQ = 256
TXT = 333
SEQ = 1024
LINE = ("row", "col_0")
CORE = "col_1"
COL = ("col_0", "col_1")
ROW_COL = ("row", "col_0", "col_1")
DP = ("dp_0", "dp_1")
ALL = ("dp_0", "dp_1", "row", "col_0", "col_1")
COL_ROW = ("col_0", "col_1", "row")
CHIPS = 4
HALF = SEQ // 2
PIECE = HALF // CHIPS
BF = jnp.bfloat16
F32 = jnp.float32


epsilon = 1e-06


def mult(left, right):
    return jnp.dot(left, right, preferred_element_type=jnp.float32)


def mult_left(left, right):
    return lax.dot_general(
        left, right, (((0,), (0,)), ((), ())), preferred_element_type=jnp.float32
    )


def mult_right(left, right):
    return lax.dot_general(
        left, right, (((1,), (1,)), ((), ())), preferred_element_type=jnp.float32
    )


def from_chip(value, ahead):
    return lax.ppermute(value, LINE, [(i, (i - ahead) % CHIPS) for i in range(CHIPS)])


def other_core(value):
    return lax.ppermute(value, CORE, [(0, 1), (1, 0)])


def other_row(value):
    return lax.ppermute(value, "row", [(0, 1), (1, 0)])


def gather_tokens(piece):
    return jnp.concatenate([piece] + [from_chip(piece, j) for j in range(1, CHIPS)], axis=0)


def scatter_tokens(partial_sums):
    total = partial_sums[:PIECE]
    for j in range(1, CHIPS):
        sent = partial_sums[j * PIECE : (j + 1) * PIECE].astype(BF)
        total = total + from_chip(sent, CHIPS - j).astype(F32)
    return total


def sum_over_chips(value):
    total = value
    for j in range(1, CHIPS):
        total = total + jnp.roll(from_chip(value, j), j * PIECE, axis=1)
    return total


def turned(value, start):
    twice = jnp.concatenate([value, value], axis=0)
    return lax.dynamic_slice_in_dim(twice, start, value.shape[0], 0)


def norm_forward(values, gain, offset):
    mean = jnp.mean(values, axis=1, keepdims=True)
    spread = jnp.mean(values * values, axis=1, keepdims=True) - mean * mean
    rstd = lax.rsqrt(spread + epsilon)
    scaled = (values - mean) * rstd
    return (scaled * gain + offset, scaled, rstd)


def norm_backward(grad, scaled, rstd, gain):
    weighted = grad * gain
    first = jnp.mean(weighted, axis=1, keepdims=True)
    second = jnp.mean(weighted * scaled, axis=1, keepdims=True)
    back = rstd * (weighted - first - scaled * second)
    return (back, jnp.sum(grad * scaled, axis=0), jnp.sum(grad, axis=0))


def halves_swapped(weight, dim, row, after=None):
    if after is not None:
        row = row + settled_index(after)
    kept = lax.dynamic_slice_in_dim(weight, row * (weight.shape[dim] // 2), weight.shape[dim] // 2, dim)
    sent = lax.dynamic_slice_in_dim(
        weight, (1 - row) * (weight.shape[dim] // 2), weight.shape[dim] // 2, dim
    )
    return (kept, other_row(sent))


def in_row_order(kept, received, dim, row):
    three = jnp.concatenate([received, kept, received], axis=dim)
    return lax.dynamic_slice_in_dim(
        three, (1 - row) * kept.shape[dim], 2 * kept.shape[dim], dim
    )


def settled(value):
    first = jnp.abs(value[(0,) * value.ndim].astype(F32))
    last = jnp.abs(value[(-1,) * value.ndim].astype(F32))
    return jnp.minimum(first + last, 0.0)


def settled_index(value):
    return settled(value).astype(jnp.int32)


def copied_to_each(value, axis):
    length = lax.axis_size(axis)
    return lax.all_to_all(
        jnp.broadcast_to(value[None], (length, *value.shape)), axis, 0, 0, tiled=True
    )


def in_two(value):
    high = lax.reduce_precision(value, exponent_bits=8, mantissa_bits=7)
    return jnp.concatenate([high.astype(BF), (value - high).astype(BF)], axis=0)


def with_other_core(own):
    return jnp.concatenate([own, other_core(own)], axis=1)


def whole_columns(weight, row, after=None):
    kept, received = halves_swapped(weight, 1, row, after)
    return in_row_order(kept, received, 0, row)


def padded(value):
    return jnp.pad(value, ((0, 0), (0, -value.shape[1] % 128)))


def blocks_by_latents(blocks, row):
    half = lax.axis_size(DP) // 2
    kept, sent = [], []
    for block in blocks:
        n = block.shape[1] // 2
        kept.append(padded(lax.dynamic_slice_in_dim(block, row * n, n, 1)))
        sent.append(padded(lax.dynamic_slice_in_dim(block, (1 - row) * n, n, 1)))
    kept = jnp.concatenate(kept, axis=1) if len(kept) > 1 else kept[0]
    sent = jnp.concatenate(sent, axis=1) if len(sent) > 1 else sent[0]
    return jnp.where(lax.axis_index(DP) // half == row, kept, other_row(sent))


def block_of_rows(weight, after):
    half = lax.axis_size(DP) // 2
    rows = weight.shape[0] // half
    place = lax.axis_index(DP) % half + settled_index(after)
    return lax.dynamic_slice_in_dim(weight, place * rows, rows, 0)


def block_of_columns(weight, after):
    half = lax.axis_size(DP) // 2
    columns = weight.shape[1] // half
    place = lax.axis_index(DP) % half + settled_index(after)
    return lax.dynamic_slice_in_dim(weight, place * columns, columns, 1).T


def products(pairs, part, added=None):
    outs = []
    start = 0
    for left, right in pairs:
        n = right.shape[1] // 2
        out = mult_left(left, right[:, part * n : (part + 1) * n])
        short = pairs[0][0].shape[1] - out.shape[0]
        if short:
            count = 2 * max(lax.axis_size(DP) // 2, 1)
            out = out.reshape(count, -1, n)
            out = jnp.pad(out, ((0, 0), (0, short // count), (0, 0))).reshape(-1, n)
        if added is not None:
            out = out + added[:, start : start + n].astype(F32)
        outs.append(out.astype(BF))
        start += n
    return jnp.concatenate(outs, axis=1) if len(outs) > 1 else outs[0]


def weight_grads(pairs):
    return products(pairs, 0, other_core(products(pairs, 1)))


def to_row_half(part):
    count = lax.axis_size(DP)
    half = count // 2
    pairs = []
    for i in range(count):
        for r in range(2):
            stays = i // half == r
            pairs.append((2 * i + r, 2 * i + r if stays else 2 * ((i + half) % count) + 1 - r))
    return lax.ppermute(part, DP + ("row",), pairs)


def scattered_over_latents(grads):
    count = lax.axis_size(DP)
    if count == 1:
        return grads
    blocks = grads.reshape(count, -1, grads.shape[1])
    return to_row_half(lax.psum_scatter(blocks, DP, scatter_dimension=0))


def row_halves(grads, row):
    kept, received = halves_swapped(grads, 0, row)
    first = row == 0
    return (jnp.where(first, kept, received), jnp.where(first, received, kept))


def summed_over_latents(grads, start=0, pairs_of=0, after=()):
    count = lax.axis_size(DP)
    if count == 1:
        return grads
    rows, n = grads.shape
    arrived = lax.all_to_all(grads.reshape(count, rows // count, n), DP, 0, 0, tiled=True)
    part = jnp.sum(arrived.astype(F32), axis=0)
    for value in after:
        part = part + settled(value)
    if pairs_of:
        exact = part[:, start : start + pairs_of] + part[:, start + pairs_of : start + 2 * pairs_of]
        rest = part[:, start + 2 * pairs_of :].astype(BF)
        part = jnp.concatenate([part[:, :start].astype(BF), in_two(exact.T).T, rest], axis=1)
    else:
        part = part.astype(BF)
    return to_row_half(part)


def spread_over_latents(part, row, gather=True):
    count = lax.axis_size(DP)
    if count == 1:
        return jnp.stack(row_halves(part, row))
    rows, n = part.shape
    if gather:
        spread = lax.all_gather(part, DP, axis=0)
    else:
        spread = copied_to_each(part, DP)
    return spread.reshape(2, count // 2 * rows, n)


def head_norm(values, gain):
    mean = jnp.mean(values, axis=-1, keepdims=True)
    spread = jnp.mean(values * values, axis=-1, keepdims=True) - mean * mean
    return (values - mean) * lax.rsqrt(spread + epsilon) * gain


def rotate(values):
    quarter = values.shape[-1] // 4
    return jnp.concatenate(
        [
            -values[..., quarter : 2 * quarter],
            values[..., :quarter],
            -values[..., 3 * quarter :],
            values[..., 2 * quarter : 3 * quarter],
        ],
        axis=-1,
    )


def qk_prep(raw, gain, cosine, sine):
    normal = head_norm(raw, gain)
    return normal * cosine + rotate(normal) * sine


def gelu_tanh(values):
    return jax.nn.gelu(values, approximate=True)


def rope_tables(positions):
    quarter = HD // 4
    freqs = jnp.exp(-math.log(10000.0) * jnp.arange(quarter, dtype=jnp.float32) / quarter)
    rows_angle = positions[0].astype(jnp.float32)[:, None] * freqs[None, :]
    cols_angle = positions[1].astype(jnp.float32)[:, None] * freqs[None, :]
    cosine = jnp.concatenate(
        [jnp.cos(rows_angle), jnp.cos(rows_angle), jnp.cos(cols_angle), jnp.cos(cols_angle)], axis=1
    )
    sine = jnp.concatenate(
        [jnp.sin(rows_angle), jnp.sin(rows_angle), jnp.sin(cols_angle), jnp.sin(cols_angle)], axis=1
    )
    return (cosine, sine)


def time_embed(steps):
    half = FREQ // 2
    freqs = jnp.exp(-math.log(10000.0) * jnp.arange(half, dtype=jnp.float32) / half)
    angles = steps.astype(jnp.float32)[:, None] * freqs[None, :]
    return jnp.concatenate([jnp.cos(angles), jnp.sin(angles)], axis=1)


def attend_forward(query, keys, values):
    scale = HD ** (-0.5)
    length = query.shape[1]
    block = min(512, length)
    outputs = []
    totals = []
    for start in range(0, length, block):
        piece = query[:, start : start + block]
        scores = scale * jnp.einsum(
            "lqhd,lkhd->lhqk", piece, keys, preferred_element_type=jnp.float32
        )
        top = jnp.max(scores, axis=-1, keepdims=True)
        expo = jnp.exp(scores - top)
        summed = jnp.sum(expo, axis=-1, keepdims=True)
        weights = expo / summed
        totals.append(top[..., 0] + jnp.log(summed[..., 0]))
        outputs.append(
            jnp.einsum(
                "lhqk,lkhd->lqhd",
                weights.astype(jnp.bfloat16),
                values,
                preferred_element_type=jnp.float32,
            )
        )
    return (jnp.concatenate(outputs, axis=1), jnp.concatenate(totals, axis=2))


def attend_backward(query, keys, values, totals, grad_out):
    scale = HD ** (-0.5)
    length = query.shape[1]
    block = min(512, length)
    d_keys = jnp.zeros(keys.shape, jnp.float32)
    d_values = jnp.zeros(values.shape, jnp.float32)
    d_query = []
    for start in range(0, length, block):
        piece = query[:, start : start + block]
        grad_piece = grad_out[:, start : start + block]
        scores = scale * jnp.einsum(
            "lqhd,lkhd->lhqk", piece, keys, preferred_element_type=jnp.float32
        )
        weights = jnp.exp(scores - totals[:, :, start : start + block, None])
        d_weights = jnp.einsum(
            "lqhd,lkhd->lhqk", grad_piece, values, preferred_element_type=jnp.float32
        )
        d_scores = weights * (d_weights - jnp.sum(d_weights * weights, axis=-1, keepdims=True))
        d_scores_b = d_scores.astype(jnp.bfloat16)
        d_query.append(
            scale
            * jnp.einsum("lhqk,lkhd->lqhd", d_scores_b, keys, preferred_element_type=jnp.float32)
        )
        d_keys = d_keys + scale * jnp.einsum(
            "lhqk,lqhd->lkhd", d_scores_b, piece, preferred_element_type=jnp.float32
        )
        d_values = d_values + jnp.einsum(
            "lhqk,lqhd->lkhd",
            weights.astype(jnp.bfloat16),
            grad_piece,
            preferred_element_type=jnp.float32,
        )
    return (jnp.concatenate(d_query, axis=1), d_keys, d_values)


def local(
    hidden,
    skipped,
    text,
    teacher,
    valid,
    steps,
    positions,
    w_skip,
    g_skip,
    b_skip,
    w_mod,
    g_one,
    b_one,
    w_qkv,
    g_query,
    g_key,
    w_out,
    g_three,
    b_three,
    w_cquery,
    w_ckv,
    g_cquery,
    g_ckey,
    w_cout,
    g_two,
    b_two,
    w_up,
    w_down,
):
    row = lax.axis_index("row")
    chip = lax.axis_index(LINE)
    core = lax.axis_index(CORE)
    width = hidden.shape[1]
    turn = chip * PIECE
    heads_own = HEADS // (2 * CHIPS)
    heads = 2 * heads_own
    shape_four = (1, HALF, heads, HD)

    def own_tokens(values):
        return turned(lax.dynamic_slice_in_dim(values, core * HALF, HALF, 0), turn)

    def other_tokens(values):
        return turned(lax.dynamic_slice_in_dim(values, (1 - core) * HALF, HALF, 0), turn)

    skip_two = jnp.transpose(w_skip.reshape(2, 2, width, D // 2), (3, 1, 0, 2)).reshape(
        D // 2, 4 * width
    )
    skip_kept, skip_received = halves_swapped(skip_two, 1, row)
    skip_own = in_row_order(skip_kept, skip_received, 0, row)
    skip_other = other_core(skip_own)
    skip_all = jnp.concatenate([skip_own, skip_other], axis=1)
    qkv_all = with_other_core(whole_columns(w_qkv, row, skip_received))
    mask_all = valid.astype(F32)
    if lax.axis_size(DP) == 1:
        count = jnp.sum(mask_all)
        out_all = with_other_core(whole_columns(w_out.T, row))
        cquery_all = with_other_core(whole_columns(w_cquery, row))
        cout_all = with_other_core(whole_columns(w_cout.T, row))
        ckv_all = with_other_core(whole_columns(w_ckv, row))
        up_all = with_other_core(whole_columns(w_up, row))
        down_all = with_other_core(whole_columns(w_down.T, row))
    else:
        ckv_block = block_of_rows(w_ckv, skip_received)
        ckv_rows = ckv_block.shape[0]
        ckv_block = jnp.pad(ckv_block, ((0, D // lax.axis_size(DP) - ckv_rows), (0, 0)))
        four_block = blocks_by_latents(
            [
                block_of_columns(w_out, skip_received),
                block_of_rows(w_cquery, skip_received),
                block_of_columns(w_cout, skip_received),
                ckv_block,
            ],
            row,
        )
        tally = jnp.sum(mask_all)
        parts = jnp.stack([jnp.floor(tally / 32.0), tally - 32.0 * jnp.floor(tally / 32.0)])
        four_block = lax.dynamic_update_slice(four_block, parts.astype(BF)[None], (0, width))
        four_own = lax.all_gather(four_block, DP, axis=0, tiled=True)
        parts = four_own.reshape(lax.axis_size(DP), -1, four_own.shape[1])[:, 0, width : width + 2]
        count = jnp.sum(parts.astype(F32) @ jnp.array([32.0, 1.0], F32))
        two_block = blocks_by_latents(
            [block_of_rows(w_up, four_own), block_of_columns(w_down, four_own)], row
        )
        two_own = lax.all_gather(two_block, DP, axis=0, tiled=True)
        four_other = other_core(four_own)

        def both(start, count):
            return jnp.concatenate(
                [four_own[:, start : start + count], four_other[:, start : start + count]], axis=1
            )

        step = width + (-width) % 128
        out_all = both(0, width)
        cquery_all = both(step, width)
        cout_all = both(2 * step, width)
        ckv_all = both(3 * step, 2 * width).reshape(lax.axis_size(DP), -1, 4 * width)
        ckv_all = ckv_all[:, :ckv_rows].reshape(-1, 4 * width)
        two_other = other_core(two_own)
        hidden_own = two_own.shape[1] // 2
        up_all = jnp.concatenate([two_own[:, :hidden_own], two_other[:, :hidden_own]], axis=1)
        down_all = jnp.concatenate([two_own[:, hidden_own:], two_other[:, hidden_own:]], axis=1)

    freq_here = w_mod.shape[0]
    mask_all = valid.astype(F32)
    emb = time_embed(steps).astype(BF)
    emb_here = lax.dynamic_slice_in_dim(emb, lax.axis_index(COL) * freq_here, freq_here, 1)
    shift_part = mult(emb_here, w_mod)
    vectors = jnp.concatenate(
        [jnp.stack([g_one, b_one, g_three, b_three, g_two, b_two]).reshape(-1), shift_part[0]]
    ) + settled(skip_received)
    gathered = copied_to_each(vectors, ROW_COL)
    gains = jnp.transpose(gathered[:, : 6 * width].reshape(8, 6, width), (1, 0, 2)).reshape(6, D)
    gain_one, offset_one, gain_three, offset_three, gain_two, offset_two = gains
    shift = jnp.sum(gathered[:, 6 * width :].reshape(2, 4, D // 2), axis=1).reshape(D)
    mask = lax.dynamic_slice_in_dim(mask_all, core * HALF + turn, PIECE, 0)

    cosine, sine = rope_tables(own_tokens(positions.T).T)
    prep = partial(qk_prep, cosine=cosine[:, None, :], sine=sine[:, None, :])

    joined = jnp.concatenate([hidden, skipped], axis=1)
    mine = own_tokens(joined)
    theirs = other_core(other_tokens(joined))
    pairs = jnp.concatenate([mine, theirs], axis=1).astype(F32)
    skip_vectors = jnp.stack([g_skip, b_skip]).reshape(2, 2 * width)
    both_vectors = jnp.concatenate([skip_vectors, other_core(skip_vectors)], axis=1)
    skip_sums = sum_over_chips(jnp.stack([jnp.sum(pairs, axis=1), jnp.sum(pairs * pairs, axis=1)]))
    skip_mean = skip_sums[0] / (2 * D)
    skip_rstd = lax.rsqrt(skip_sums[1] / (2 * D) - skip_mean * skip_mean + epsilon)
    skip_scaled = (pairs - skip_mean[:, None]) * skip_rstd[:, None]
    normed = (skip_scaled * both_vectors[0] + both_vectors[1]).astype(BF)
    stream = scatter_tokens(mult_right(normed, skip_all))

    normed_one, scaled_one, rstd_one = norm_forward(stream, gain_one, offset_one)
    text_sent = text[0] + settled(rstd_one).astype(BF)
    wide_text = jnp.transpose(copied_to_each(text_sent, ROW_COL), (1, 0, 2)).reshape(TXT, -1)
    wide_one = gather_tokens((normed_one + shift).astype(BF))
    packed = (mult(wide_one, qkv_all) + settled(wide_text)).reshape(HALF, heads, 3, HD)
    query_raw = packed[:, :, 0]
    key_raw = packed[:, :, 1]
    query = prep(query_raw, g_query).astype(BF).reshape(shape_four)
    keys_here = prep(key_raw, g_key).astype(BF)
    values_here = packed[:, :, 2].astype(BF)

    def swapped_heads(values):
        return jnp.concatenate([values[:, heads_own:], values[:, :heads_own]], axis=1)

    key_values = other_core(swapped_heads(jnp.concatenate([keys_here, values_here], axis=2)))
    keys = jnp.concatenate([keys_here, key_values[..., :HD]], axis=0)[None]
    values = jnp.concatenate([values_here, key_values[..., HD:]], axis=0)[None]
    mixed, self_totals = attend_forward(query, keys, values)
    mixed_here = mixed.reshape(HALF, heads * HD).astype(BF)
    stream_two = stream + scatter_tokens(mult_right(mixed_here, out_all))

    normed_three, scaled_three, rstd_three = norm_forward(stream_two, gain_three, offset_three)
    teacher_blocks = jnp.transpose(
        teacher.reshape(2, CHIPS, PIECE, width) + settled(rstd_three).astype(BF), (1, 0, 2, 3)
    ).reshape(2 * CHIPS, PIECE, width)
    teacher_here = jnp.transpose(
        lax.all_to_all(teacher_blocks, ROW_COL, 0, 0, tiled=True), (1, 0, 2)
    ).reshape(PIECE, D)
    wide_three = gather_tokens(normed_three.astype(BF))
    cquery_raw = mult(wide_three, cquery_all) + settled(teacher_here)
    cquery_raw = cquery_raw.reshape(HALF, heads, HD)
    cquery = prep(cquery_raw, g_cquery).astype(BF).reshape(shape_four)
    ckv = mult(wide_text, ckv_all).reshape(1, TXT, heads, 2, HD)
    ckey_raw = ckv[:, :, :, 0]
    ckeys = head_norm(ckey_raw, g_ckey).astype(BF)
    cvalues = ckv[:, :, :, 1].astype(BF)
    cmixed, cross_totals = attend_forward(cquery, ckeys, cvalues)
    cmixed_here = cmixed.reshape(HALF, heads * HD).astype(BF)
    stream_three = stream_two + scatter_tokens(mult_right(cmixed_here, cout_all))

    normed_two, scaled_two, rstd_two = norm_forward(stream_three, gain_two, offset_two)
    wide_two = gather_tokens(normed_two.astype(BF))
    upper = mult(wide_two, up_all)
    active, gelu_back = jax.vjp(gelu_tanh, upper)
    active_here = active.astype(BF)
    output_here = stream_three + scatter_tokens(mult_right(active_here, down_all))

    diff = output_here - teacher_here.astype(F32)
    sse_local = jnp.sum(mask[:, None] * diff * diff)
    factor = 32.0 * lax.axis_size(DP) / count
    grad_out = factor * mask[:, None] * diff
    output_blocks = jnp.transpose(
        output_here.astype(BF).reshape(PIECE, 2 * CHIPS, width), (1, 0, 2)
    )
    output_back = lax.all_to_all(output_blocks, ROW_COL, 0, 0, tiled=True)
    output = jnp.transpose(
        output_back.reshape(CHIPS, 2, PIECE, width), (1, 0, 2, 3)
    ).reshape(SEQ, width).astype(F32)

    wide_grad = gather_tokens(grad_out.astype(BF))
    d_upper = gelu_back(mult(wide_grad, down_all))[0].astype(BF)
    d_normed_two = scatter_tokens(mult_right(d_upper, up_all))
    two_pairs = [(wide_two, d_upper), (wide_grad, active_here)]
    two_theirs = other_core(products(two_pairs, 1))
    d_normed_two = d_normed_two + (settled(output_back) + settled(two_theirs))
    two_grads = products(two_pairs, 0, two_theirs)
    two_part = scattered_over_latents(two_grads)
    back_two, d_g_two, d_b_two = norm_backward(d_normed_two, scaled_two, rstd_two, gain_two)
    grad_three = grad_out + back_two

    wide_three_grad = gather_tokens(grad_three.astype(BF))
    d_cmixed = mult(wide_three_grad, cout_all) + settled(two_grads)
    d_cmixed = d_cmixed.astype(BF).reshape(shape_four)
    d_cquery, d_ckeys, d_cvalues = attend_backward(cquery, ckeys, cvalues, cross_totals, d_cmixed)
    unused, cquery_back = jax.vjp(prep, cquery_raw, g_cquery)
    d_cquery_raw, d_g_cquery = cquery_back(d_cquery.reshape(HALF, heads, HD))
    d_cquery_here = d_cquery_raw.reshape(HALF, heads * HD).astype(BF)
    d_normed_three = scatter_tokens(mult_right(d_cquery_here, cquery_all))
    unused, ckey_back = jax.vjp(head_norm, ckey_raw, g_ckey)
    d_ckey_raw, d_g_ckey = ckey_back(d_ckeys)
    d_ckv = jnp.stack([d_ckey_raw, d_cvalues], axis=3).reshape(TXT, heads * 2 * HD).astype(BF)
    back_three, d_g_three, d_b_three = norm_backward(
        d_normed_three, scaled_three, rstd_three, gain_three
    )
    grad_two = grad_three + back_three

    three_grads = weight_grads(
        [(wide_three, d_cquery_here), (wide_three_grad, cmixed_here), (wide_text, d_ckv)]
    )

    wide_two_grad = gather_tokens(grad_two.astype(BF))
    d_mixed = mult(wide_two_grad, out_all) + settled(three_grads)
    d_mixed = d_mixed.astype(BF).reshape(shape_four)
    d_query, d_keys, d_values = attend_backward(query, keys, values, self_totals, d_mixed)
    d_both = jnp.concatenate([d_keys[0], d_values[0]], axis=2)
    d_both = d_both[:HALF] + other_core(swapped_heads(d_both[HALF:]).astype(BF)).astype(F32)
    unused, query_back = jax.vjp(prep, query_raw, g_query)
    d_query_raw, d_g_query = query_back(d_query.reshape(HALF, heads, HD))
    unused, key_back = jax.vjp(prep, key_raw, g_key)
    d_key_raw, d_g_key = key_back(d_both[..., :HD])
    d_packed = (
        jnp.stack([d_query_raw, d_key_raw, d_both[..., HD:] + settled(two_part)], axis=2)
        .reshape(HALF, heads * 3 * HD)
        .astype(BF)
    )
    d_inputs = scatter_tokens(mult_right(d_packed, qkv_all))
    back_one, d_g_one, d_b_one = norm_backward(d_inputs, scaled_one, rstd_one, gain_one)
    grad_one = grad_two + back_one

    d_shift_part = jnp.sum(d_inputs, axis=0)
    shared = jnp.concatenate([d_g_query, d_g_key, d_g_cquery, d_g_ckey, sse_local[None]])
    small = jnp.stack(
        [d_g_one, d_b_one, d_g_three, d_b_three, d_g_two, d_b_two, d_shift_part]
        + [jnp.pad(shared, (0, D - shared.shape[0]))]
    )
    piece = jnp.concatenate([grad_one.astype(BF), in_two(small)], axis=0)
    pieces = [piece] + [from_chip(piece, j) for j in range(1, CHIPS)]
    wide_one_grad = jnp.concatenate([p[:PIECE] for p in pieces], axis=0)
    small = sum(p[PIECE:].astype(F32) for p in pieces)
    small = small[:8] + small[8:]
    small = small + other_core(small)
    oq_grads = weight_grads([(wide_two_grad, mixed_here), (wide_one, d_packed)])
    five_part = summed_over_latents(jnp.concatenate([oq_grads, three_grads], axis=1))
    d_joined = mult(wide_one_grad, skip_all)
    skip_sums = jnp.stack([jnp.sum(d_joined * skip_scaled, axis=0), jnp.sum(d_joined, axis=0)])
    skip_sums = skip_sums[:, : 2 * width] + other_core(skip_sums[:, 2 * width :])
    place = lax.axis_index(ROW_COL)
    shared_size = shared.shape[0]
    vector = jnp.concatenate(
        [
            lax.dynamic_slice_in_dim(small[:6], place * width, width, 1).reshape(-1),
            small[7, :shared_size],
            skip_sums.reshape(-1),
        ]
    )
    vector = jnp.pad(vector, (0, -vector.shape[0] % (D // 2))).reshape(-1, D // 2)
    vector_rows = vector.shape[0]
    latent_shift = lax.dynamic_slice_in_dim(small[6], row * (D // 2), D // 2, 0).astype(BF)
    d_w_mod = mult_left(emb_here, latent_shift[None])
    extra = jnp.concatenate([in_two(vector), d_w_mod.astype(BF)], axis=0).T
    extra = jnp.concatenate([extra, extra], axis=0)
    d_skip = weight_grads([(wide_one_grad, normed)])
    last_sent = jnp.concatenate([d_skip, extra], axis=1)
    n_up = w_up.shape[1] // 2
    two_halves = spread_over_latents(two_part, row)
    skip_part = summed_over_latents(
        last_sent, 2 * width, vector_rows
    )
    both_gains = both_vectors[0] + settled(d_skip) + settled(skip_sums)
    weighted = d_joined * both_gains
    back_sums = sum_over_chips(
        jnp.stack([jnp.sum(weighted, axis=1), jnp.sum(weighted * skip_scaled, axis=1)])
    ) / (2 * D)
    back_joined = skip_rstd[:, None] * (
        weighted - back_sums[0][:, None] - skip_scaled * back_sums[1][:, None]
    )
    back_mine = back_joined[:, : 2 * width]
    pinned = settled(skip_part) + settled(two_halves)
    back_theirs = other_core(back_joined[:, 2 * width :] + pinned)
    unturn = (CHIPS - chip) % CHIPS * PIECE
    back_mine = turned(back_mine, unturn)
    back_theirs = turned(back_theirs, unturn)
    back_tokens = lax.dynamic_slice_in_dim(
        jnp.concatenate([back_mine, back_theirs, back_mine], axis=0), core * HALF, SEQ, 0
    )
    d_hidden = back_tokens[:, :width]
    d_skipped = back_tokens[:, width:]

    def columns(summed, start, count):
        return jnp.concatenate(
            [summed[0][:, start : start + count], summed[1][:, start : start + count]], axis=1
        ).astype(F32)

    d_w_up = columns(two_halves, 0, n_up)
    d_w_down = columns(two_halves, n_up, n_up).T
    five_grads = spread_over_latents(five_part, row)
    d_w_cquery = columns(five_grads, 4 * width, width)
    d_w_cout = columns(five_grads, 5 * width, width).T
    d_w_ckv = columns(five_grads, 6 * width, 2 * width)
    count_blocks = max(lax.axis_size(DP) // 2, 1)
    d_w_ckv = d_w_ckv.reshape(count_blocks, -1, 4 * width)[:, : w_ckv.shape[0] // count_blocks]
    d_w_ckv = d_w_ckv.reshape(-1, 4 * width)
    last_grads = spread_over_latents(skip_part, row, False)
    d_w_out = columns(five_grads, 0, width).T
    d_w_qkv = columns(five_grads, width, 3 * width)
    d_w_skip = columns(last_grads, 0, 2 * width).reshape(D // 2, 2, 2, width)
    d_w_skip = jnp.transpose(d_w_skip, (2, 1, 3, 0)).reshape(2, 2 * width, D // 2)
    extra = last_grads[:, :, 2 * width :]
    extra = jnp.where(row == 0, extra[0], extra[1]).astype(F32).T
    vector = (extra[:vector_rows] + extra[vector_rows : 2 * vector_rows]).reshape(-1)
    d_w_mod = extra[2 * vector_rows :]
    d_g_one, d_b_one, d_g_three, d_b_three, d_g_two, d_b_two = vector[: 6 * width].reshape(6, width)
    shared = vector[6 * width : 6 * width + shared_size]
    d_g_query, d_g_key, d_g_cquery, d_g_ckey = shared[: 4 * HD].reshape(4, HD)
    loss = shared[4 * HD] / (count * D)
    skip_sums = vector[6 * width + shared_size : 10 * width + shared_size].reshape(2, 2, width)
    d_g_skip, d_b_skip = skip_sums
    return (
        output,
        d_hidden,
        d_skipped,
        d_w_skip,
        d_g_skip,
        d_b_skip,
        d_w_mod,
        d_g_one,
        d_b_one,
        d_w_qkv,
        d_g_query,
        d_g_key,
        d_w_out,
        d_g_three,
        d_b_three,
        d_w_cquery,
        d_w_ckv,
        d_g_cquery,
        d_g_ckey,
        d_w_cout,
        d_g_two,
        d_b_two,
        d_w_up,
        d_w_down,
        loss,
    )


def solution(mesh):
    side = math.isqrt(mesh.shape["dp"])
    split = Mesh(
        mesh.devices.reshape(side, side, mesh.shape["row"], 2, 2),
        ("dp_0", "dp_1", "row", "col_0", "col_1"),
    )
    in_specs = (
        P(DP, COL_ROW),
        P(DP, COL_ROW),
        P(DP, None, ROW_COL),
        P(DP, ROW_COL),
        P(DP),
        P(DP),
        P(None, DP),
        P(None, COL, "row"),
        P(None, COL_ROW),
        P(None, COL_ROW),
        P(COL, "row"),
        P(ROW_COL),
        P(ROW_COL),
        P("row", COL),
        P(),
        P(),
        P(COL, "row"),
        P(ROW_COL),
        P(ROW_COL),
        P("row", COL),
        P("row", COL),
        P(),
        P(),
        P(COL, "row"),
        P(ROW_COL),
        P(ROW_COL),
        P("row", COL),
        P(COL, "row"),
    )
    out_specs = (
        P(DP, ROW_COL),
        P(DP, COL_ROW),
        P(DP, COL_ROW),
        P(None, COL, "row"),
        P(None, COL_ROW),
        P(None, COL_ROW),
        P(COL, "row"),
        P(ROW_COL),
        P(ROW_COL),
        P("row", COL),
        P(),
        P(),
        P(COL, "row"),
        P(ROW_COL),
        P(ROW_COL),
        P("row", COL),
        P("row", COL),
        P(),
        P(),
        P(COL, "row"),
        P(ROW_COL),
        P(ROW_COL),
        P("row", COL),
        P(COL, "row"),
        P(),
    )
    return jax.shard_map(local, mesh=split, in_specs=in_specs, out_specs=out_specs, check_vma=False)
```

```python
from functools import partial
import math

import jax
import jax.numpy as jnp
from jax import lax
from jax.sharding import Mesh
from jax.sharding import PartitionSpec as P

D = 1408
HEADS = 16
HD = 88
FREQ = 256
TXT = 333
SEQ = 1024
LINE = ("row", "col_0")
CORE = "col_1"
COL = ("col_0", "col_1")
ROW_COL = ("row", "col_0", "col_1")
DP = ("dp_0", "dp_1")
ALL = ("dp_0", "dp_1", "row", "col_0", "col_1")
COL_ROW = ("col_0", "col_1", "row")
CHIPS = 4
HALF = SEQ // 2
PIECE = HALF // CHIPS
BF = jnp.bfloat16
F32 = jnp.float32


epsilon = 1e-06


def mult(left, right):
    return jnp.dot(left, right, preferred_element_type=jnp.float32)


def mult_left(left, right):
    return lax.dot_general(
        left, right, (((0,), (0,)), ((), ())), preferred_element_type=jnp.float32
    )


def mult_right(left, right):
    return lax.dot_general(
        left, right, (((1,), (1,)), ((), ())), preferred_element_type=jnp.float32
    )


def from_chip(value, ahead):
    return lax.ppermute(value, LINE, [(i, (i - ahead) % CHIPS) for i in range(CHIPS)])


def other_core(value):
    return lax.ppermute(value, CORE, [(0, 1), (1, 0)])


def other_row(value):
    return lax.ppermute(value, "row", [(0, 1), (1, 0)])


def gather_tokens(piece):
    return jnp.concatenate([piece] + [from_chip(piece, j) for j in range(1, CHIPS)], axis=0)


def scatter_tokens(partial_sums):
    total = partial_sums[:PIECE]
    for j in range(1, CHIPS):
        sent = partial_sums[j * PIECE : (j + 1) * PIECE].astype(BF)
        total = total + from_chip(sent, CHIPS - j).astype(F32)
    return total


def sum_over_chips(value):
    total = value
    for j in range(1, CHIPS):
        total = total + jnp.roll(from_chip(value, j), j * PIECE, axis=1)
    return total


def turned(value, start):
    twice = jnp.concatenate([value, value], axis=0)
    return lax.dynamic_slice_in_dim(twice, start, value.shape[0], 0)


def norm_forward(values, gain, offset):
    mean = jnp.mean(values, axis=1, keepdims=True)
    spread = jnp.mean(values * values, axis=1, keepdims=True) - mean * mean
    rstd = lax.rsqrt(spread + epsilon)
    scaled = (values - mean) * rstd
    return (scaled * gain + offset, scaled, rstd)


def norm_backward(grad, scaled, rstd, gain):
    weighted = grad * gain
    first = jnp.mean(weighted, axis=1, keepdims=True)
    second = jnp.mean(weighted * scaled, axis=1, keepdims=True)
    back = rstd * (weighted - first - scaled * second)
    return (back, jnp.sum(grad * scaled, axis=0), jnp.sum(grad, axis=0))


def halves_swapped(weight, dim, row, after=None):
    if after is not None:
        row = row + settled_index(after)
    kept = lax.dynamic_slice_in_dim(weight, row * (weight.shape[dim] // 2), weight.shape[dim] // 2, dim)
    sent = lax.dynamic_slice_in_dim(
        weight, (1 - row) * (weight.shape[dim] // 2), weight.shape[dim] // 2, dim
    )
    return (kept, other_row(sent))


def in_row_order(kept, received, dim, row):
    three = jnp.concatenate([received, kept, received], axis=dim)
    return lax.dynamic_slice_in_dim(
        three, (1 - row) * kept.shape[dim], 2 * kept.shape[dim], dim
    )


def settled(value):
    first = jnp.abs(value[(0,) * value.ndim].astype(F32))
    last = jnp.abs(value[(-1,) * value.ndim].astype(F32))
    return jnp.minimum(first + last, 0.0)


def settled_index(value):
    return settled(value).astype(jnp.int32)


def copied_to_each(value, axis):
    length = lax.axis_size(axis)
    return lax.all_to_all(
        jnp.broadcast_to(value[None], (length, *value.shape)), axis, 0, 0, tiled=True
    )


def in_two(value):
    high = lax.reduce_precision(value, exponent_bits=8, mantissa_bits=7)
    return jnp.concatenate([high.astype(BF), (value - high).astype(BF)], axis=0)


def with_other_core(own):
    return jnp.concatenate([own, other_core(own)], axis=1)


def whole_columns(weight, row, after=None):
    kept, received = halves_swapped(weight, 1, row, after)
    return in_row_order(kept, received, 0, row)


def padded(value):
    return jnp.pad(value, ((0, 0), (0, -value.shape[1] % 128)))


def blocks_by_latents(blocks, row):
    half = lax.axis_size(DP) // 2
    kept, sent = [], []
    for block in blocks:
        n = block.shape[1] // 2
        kept.append(padded(lax.dynamic_slice_in_dim(block, row * n, n, 1)))
        sent.append(padded(lax.dynamic_slice_in_dim(block, (1 - row) * n, n, 1)))
    kept = jnp.concatenate(kept, axis=1) if len(kept) > 1 else kept[0]
    sent = jnp.concatenate(sent, axis=1) if len(sent) > 1 else sent[0]
    return jnp.where(lax.axis_index(DP) // half == row, kept, other_row(sent))


def block_of_rows(weight, after):
    half = lax.axis_size(DP) // 2
    rows = weight.shape[0] // half
    place = lax.axis_index(DP) % half + settled_index(after)
    return lax.dynamic_slice_in_dim(weight, place * rows, rows, 0)


def block_of_columns(weight, after):
    half = lax.axis_size(DP) // 2
    columns = weight.shape[1] // half
    place = lax.axis_index(DP) % half + settled_index(after)
    return lax.dynamic_slice_in_dim(weight, place * columns, columns, 1).T


def products(pairs, part, added=None):
    outs = []
    start = 0
    for left, right in pairs:
        n = right.shape[1] // 2
        out = mult_left(left, right[:, part * n : (part + 1) * n])
        short = pairs[0][0].shape[1] - out.shape[0]
        if short:
            count = 2 * max(lax.axis_size(DP) // 2, 1)
            out = out.reshape(count, -1, n)
            out = jnp.pad(out, ((0, 0), (0, short // count), (0, 0))).reshape(-1, n)
        if added is not None:
            out = out + added[:, start : start + n].astype(F32)
        outs.append(out.astype(BF))
        start += n
    return jnp.concatenate(outs, axis=1) if len(outs) > 1 else outs[0]


def weight_grads(pairs, after=None):
    theirs = other_core(products(pairs, 1))
    if after is not None:
        theirs = theirs + settled(after).astype(BF)
    return products(pairs, 0, theirs)


def to_row_half(part):
    count = lax.axis_size(DP)
    half = count // 2
    pairs = []
    for i in range(count):
        for r in range(2):
            stays = i // half == r
            pairs.append((2 * i + r, 2 * i + r if stays else 2 * ((i + half) % count) + 1 - r))
    return lax.ppermute(part, DP + ("row",), pairs)


def scattered_over_latents(grads):
    count = lax.axis_size(DP)
    if count == 1:
        return grads
    blocks = grads.reshape(count, -1, grads.shape[1])
    return to_row_half(lax.psum_scatter(blocks, DP, scatter_dimension=0))


def row_halves(grads, row):
    kept, received = halves_swapped(grads, 0, row)
    first = row == 0
    return (jnp.where(first, kept, received), jnp.where(first, received, kept))


def summed_over_latents(grads, start=0, pairs_of=0, after=()):
    count = lax.axis_size(DP)
    if count == 1:
        return grads
    rows, n = grads.shape
    arrived = lax.all_to_all(grads.reshape(count, rows // count, n), DP, 0, 0, tiled=True)
    part = jnp.sum(arrived.astype(F32), axis=0)
    for value in after:
        part = part + settled(value)
    if pairs_of:
        exact = part[:, start : start + pairs_of] + part[:, start + pairs_of : start + 2 * pairs_of]
        rest = part[:, start + 2 * pairs_of :].astype(BF)
        part = jnp.concatenate([part[:, :start].astype(BF), in_two(exact.T).T, rest], axis=1)
    else:
        part = part.astype(BF)
    return to_row_half(part)


def spread_over_latents(part, row, gather=True):
    count = lax.axis_size(DP)
    if count == 1:
        return jnp.stack(row_halves(part, row))
    rows, n = part.shape
    if gather:
        spread = lax.all_gather(part, DP, axis=0)
    else:
        spread = copied_to_each(part, DP)
    return spread.reshape(2, count // 2 * rows, n)


def head_norm(values, gain):
    mean = jnp.mean(values, axis=-1, keepdims=True)
    spread = jnp.mean(values * values, axis=-1, keepdims=True) - mean * mean
    return (values - mean) * lax.rsqrt(spread + epsilon) * gain


def rotate(values):
    quarter = values.shape[-1] // 4
    return jnp.concatenate(
        [
            -values[..., quarter : 2 * quarter],
            values[..., :quarter],
            -values[..., 3 * quarter :],
            values[..., 2 * quarter : 3 * quarter],
        ],
        axis=-1,
    )


def qk_prep(raw, gain, cosine, sine):
    normal = head_norm(raw, gain)
    return normal * cosine + rotate(normal) * sine


def gelu_tanh(values):
    return jax.nn.gelu(values, approximate=True)


def rope_tables(positions):
    quarter = HD // 4
    freqs = jnp.exp(-math.log(10000.0) * jnp.arange(quarter, dtype=jnp.float32) / quarter)
    rows_angle = positions[0].astype(jnp.float32)[:, None] * freqs[None, :]
    cols_angle = positions[1].astype(jnp.float32)[:, None] * freqs[None, :]
    cosine = jnp.concatenate(
        [jnp.cos(rows_angle), jnp.cos(rows_angle), jnp.cos(cols_angle), jnp.cos(cols_angle)], axis=1
    )
    sine = jnp.concatenate(
        [jnp.sin(rows_angle), jnp.sin(rows_angle), jnp.sin(cols_angle), jnp.sin(cols_angle)], axis=1
    )
    return (cosine, sine)


def time_embed(steps):
    half = FREQ // 2
    freqs = jnp.exp(-math.log(10000.0) * jnp.arange(half, dtype=jnp.float32) / half)
    angles = steps.astype(jnp.float32)[:, None] * freqs[None, :]
    return jnp.concatenate([jnp.cos(angles), jnp.sin(angles)], axis=1)


def attend_forward(query, keys, values):
    scale = HD ** (-0.5)
    length = query.shape[1]
    block = min(512, length)
    outputs = []
    totals = []
    for start in range(0, length, block):
        piece = query[:, start : start + block]
        scores = scale * jnp.einsum(
            "lqhd,lkhd->lhqk", piece, keys, preferred_element_type=jnp.float32
        )
        top = jnp.max(scores, axis=-1, keepdims=True)
        expo = jnp.exp(scores - top)
        summed = jnp.sum(expo, axis=-1, keepdims=True)
        weights = expo / summed
        totals.append(top[..., 0] + jnp.log(summed[..., 0]))
        outputs.append(
            jnp.einsum(
                "lhqk,lkhd->lqhd",
                weights.astype(jnp.bfloat16),
                values,
                preferred_element_type=jnp.float32,
            )
        )
    return (jnp.concatenate(outputs, axis=1), jnp.concatenate(totals, axis=2))


def attend_backward(query, keys, values, totals, grad_out):
    scale = HD ** (-0.5)
    length = query.shape[1]
    block = min(512, length)
    d_keys = jnp.zeros(keys.shape, jnp.float32)
    d_values = jnp.zeros(values.shape, jnp.float32)
    d_query = []
    for start in range(0, length, block):
        piece = query[:, start : start + block]
        grad_piece = grad_out[:, start : start + block]
        scores = scale * jnp.einsum(
            "lqhd,lkhd->lhqk", piece, keys, preferred_element_type=jnp.float32
        )
        weights = jnp.exp(scores - totals[:, :, start : start + block, None])
        d_weights = jnp.einsum(
            "lqhd,lkhd->lhqk", grad_piece, values, preferred_element_type=jnp.float32
        )
        d_scores = weights * (d_weights - jnp.sum(d_weights * weights, axis=-1, keepdims=True))
        d_scores_b = d_scores.astype(jnp.bfloat16)
        d_query.append(
            scale
            * jnp.einsum("lhqk,lkhd->lqhd", d_scores_b, keys, preferred_element_type=jnp.float32)
        )
        d_keys = d_keys + scale * jnp.einsum(
            "lhqk,lqhd->lkhd", d_scores_b, piece, preferred_element_type=jnp.float32
        )
        d_values = d_values + jnp.einsum(
            "lhqk,lqhd->lkhd",
            weights.astype(jnp.bfloat16),
            grad_piece,
            preferred_element_type=jnp.float32,
        )
    return (jnp.concatenate(d_query, axis=1), d_keys, d_values)


def local(
    hidden,
    skipped,
    text,
    teacher,
    valid,
    steps,
    positions,
    w_skip,
    g_skip,
    b_skip,
    w_mod,
    g_one,
    b_one,
    w_qkv,
    g_query,
    g_key,
    w_out,
    g_three,
    b_three,
    w_cquery,
    w_ckv,
    g_cquery,
    g_ckey,
    w_cout,
    g_two,
    b_two,
    w_up,
    w_down,
):
    row = lax.axis_index("row")
    chip = lax.axis_index(LINE)
    core = lax.axis_index(CORE)
    width = hidden.shape[1]
    turn = chip * PIECE
    heads_own = HEADS // (2 * CHIPS)
    heads = 2 * heads_own
    shape_four = (1, HALF, heads, HD)

    def own_tokens(values):
        return turned(lax.dynamic_slice_in_dim(values, core * HALF, HALF, 0), turn)

    def other_tokens(values):
        return turned(lax.dynamic_slice_in_dim(values, (1 - core) * HALF, HALF, 0), turn)

    skip_two = jnp.transpose(w_skip.reshape(2, 2, width, D // 2), (3, 1, 0, 2)).reshape(
        D // 2, 4 * width
    )
    skip_kept, skip_received = halves_swapped(skip_two, 1, row)
    skip_own = in_row_order(skip_kept, skip_received, 0, row)
    skip_other = other_core(skip_own)
    skip_all = jnp.concatenate([skip_own, skip_other], axis=1)
    qkv_all = with_other_core(whole_columns(w_qkv, row, skip_received))
    mask_all = valid.astype(F32)
    if lax.axis_size(DP) == 1:
        count = jnp.sum(mask_all)
        out_all = with_other_core(whole_columns(w_out.T, row))
        cquery_all = with_other_core(whole_columns(w_cquery, row))
        cout_all = with_other_core(whole_columns(w_cout.T, row))
        ckv_all = with_other_core(whole_columns(w_ckv, row))
        up_all = with_other_core(whole_columns(w_up, row))
        down_all = with_other_core(whole_columns(w_down.T, row))
    else:
        ckv_block = block_of_rows(w_ckv, skip_received)
        ckv_rows = ckv_block.shape[0]
        ckv_block = jnp.pad(ckv_block, ((0, D // lax.axis_size(DP) - ckv_rows), (0, 0)))
        four_block = blocks_by_latents(
            [
                block_of_columns(w_out, skip_received),
                block_of_rows(w_cquery, skip_received),
                block_of_columns(w_cout, skip_received),
                ckv_block,
            ],
            row,
        )
        tally = jnp.sum(mask_all)
        parts = jnp.stack([jnp.floor(tally / 32.0), tally - 32.0 * jnp.floor(tally / 32.0)])
        four_block = lax.dynamic_update_slice(four_block, parts.astype(BF)[None], (0, width))
        four_own = lax.all_gather(four_block, DP, axis=0, tiled=True)
        parts = four_own.reshape(lax.axis_size(DP), -1, four_own.shape[1])[:, 0, width : width + 2]
        count = jnp.sum(parts.astype(F32) @ jnp.array([32.0, 1.0], F32))
        two_block = blocks_by_latents(
            [block_of_rows(w_up, four_own), block_of_columns(w_down, four_own)], row
        )
        two_own = lax.all_gather(two_block, DP, axis=0, tiled=True)
        four_other = other_core(four_own)

        def both(start, count):
            return jnp.concatenate(
                [four_own[:, start : start + count], four_other[:, start : start + count]], axis=1
            )

        step = width + (-width) % 128
        out_all = both(0, width)
        cquery_all = both(step, width)
        cout_all = both(2 * step, width)
        ckv_all = both(3 * step, 2 * width).reshape(lax.axis_size(DP), -1, 4 * width)
        ckv_all = ckv_all[:, :ckv_rows].reshape(-1, 4 * width)
        two_other = other_core(two_own)
        hidden_own = two_own.shape[1] // 2
        up_all = jnp.concatenate([two_own[:, :hidden_own], two_other[:, :hidden_own]], axis=1)
        down_all = jnp.concatenate([two_own[:, hidden_own:], two_other[:, hidden_own:]], axis=1)

    freq_here = w_mod.shape[0]
    mask_all = valid.astype(F32)
    emb = time_embed(steps).astype(BF)
    emb_here = lax.dynamic_slice_in_dim(emb, lax.axis_index(COL) * freq_here, freq_here, 1)
    shift_part = mult(emb_here, w_mod)
    vectors = jnp.concatenate(
        [jnp.stack([g_one, b_one, g_three, b_three, g_two, b_two]).reshape(-1), shift_part[0]]
    ) + settled(skip_received)
    gathered = copied_to_each(vectors, ROW_COL)
    gains = jnp.transpose(gathered[:, : 6 * width].reshape(8, 6, width), (1, 0, 2)).reshape(6, D)
    gain_one, offset_one, gain_three, offset_three, gain_two, offset_two = gains
    shift = jnp.sum(gathered[:, 6 * width :].reshape(2, 4, D // 2), axis=1).reshape(D)
    mask = lax.dynamic_slice_in_dim(mask_all, core * HALF + turn, PIECE, 0)

    cosine, sine = rope_tables(own_tokens(positions.T).T)
    prep = partial(qk_prep, cosine=cosine[:, None, :], sine=sine[:, None, :])

    joined = jnp.concatenate([hidden, skipped], axis=1)
    mine = own_tokens(joined)
    theirs = other_core(other_tokens(joined))
    pairs = jnp.concatenate([mine, theirs], axis=1).astype(F32)
    skip_vectors = jnp.stack([g_skip, b_skip]).reshape(2, 2 * width)
    both_vectors = jnp.concatenate([skip_vectors, other_core(skip_vectors)], axis=1)
    skip_sums = sum_over_chips(jnp.stack([jnp.sum(pairs, axis=1), jnp.sum(pairs * pairs, axis=1)]))
    skip_mean = skip_sums[0] / (2 * D)
    skip_rstd = lax.rsqrt(skip_sums[1] / (2 * D) - skip_mean * skip_mean + epsilon)
    skip_scaled = (pairs - skip_mean[:, None]) * skip_rstd[:, None]
    normed = (skip_scaled * both_vectors[0] + both_vectors[1]).astype(BF)
    stream = scatter_tokens(mult_right(normed, skip_all))

    normed_one, scaled_one, rstd_one = norm_forward(stream, gain_one, offset_one)
    text_sent = text[0] + settled(rstd_one).astype(BF)
    wide_text = jnp.transpose(copied_to_each(text_sent, ROW_COL), (1, 0, 2)).reshape(TXT, -1)
    wide_one = gather_tokens((normed_one + shift).astype(BF))
    packed = (mult(wide_one, qkv_all) + settled(wide_text)).reshape(HALF, heads, 3, HD)
    query_raw = packed[:, :, 0]
    key_raw = packed[:, :, 1]
    query = prep(query_raw, g_query).astype(BF).reshape(shape_four)
    keys_here = prep(key_raw, g_key).astype(BF)
    values_here = packed[:, :, 2].astype(BF)

    def swapped_heads(values):
        return jnp.concatenate([values[:, heads_own:], values[:, :heads_own]], axis=1)

    key_values = other_core(swapped_heads(jnp.concatenate([keys_here, values_here], axis=2)))
    keys = jnp.concatenate([keys_here, key_values[..., :HD]], axis=0)[None]
    values = jnp.concatenate([values_here, key_values[..., HD:]], axis=0)[None]
    mixed, self_totals = attend_forward(query, keys, values)
    mixed_here = mixed.reshape(HALF, heads * HD).astype(BF)
    stream_two = stream + scatter_tokens(mult_right(mixed_here, out_all))

    normed_three, scaled_three, rstd_three = norm_forward(stream_two, gain_three, offset_three)
    teacher_blocks = jnp.transpose(
        teacher.reshape(2, CHIPS, PIECE, width) + settled(rstd_three).astype(BF), (1, 0, 2, 3)
    ).reshape(2 * CHIPS, PIECE, width)
    teacher_here = jnp.transpose(
        lax.all_to_all(teacher_blocks, ROW_COL, 0, 0, tiled=True), (1, 0, 2)
    ).reshape(PIECE, D)
    wide_three = gather_tokens(normed_three.astype(BF))
    cquery_raw = mult(wide_three, cquery_all) + settled(teacher_here)
    cquery_raw = cquery_raw.reshape(HALF, heads, HD)
    cquery = prep(cquery_raw, g_cquery).astype(BF).reshape(shape_four)
    ckv = mult(wide_text, ckv_all).reshape(1, TXT, heads, 2, HD)
    ckey_raw = ckv[:, :, :, 0]
    ckeys = head_norm(ckey_raw, g_ckey).astype(BF)
    cvalues = ckv[:, :, :, 1].astype(BF)
    cmixed, cross_totals = attend_forward(cquery, ckeys, cvalues)
    cmixed_here = cmixed.reshape(HALF, heads * HD).astype(BF)
    stream_three = stream_two + scatter_tokens(mult_right(cmixed_here, cout_all))

    normed_two, scaled_two, rstd_two = norm_forward(stream_three, gain_two, offset_two)
    wide_two = gather_tokens(normed_two.astype(BF))
    upper = mult(wide_two, up_all)
    active, gelu_back = jax.vjp(gelu_tanh, upper)
    active_here = active.astype(BF)
    output_here = stream_three + scatter_tokens(mult_right(active_here, down_all))

    diff = output_here - teacher_here.astype(F32)
    sse_local = jnp.sum(mask[:, None] * diff * diff)
    factor = 32.0 * lax.axis_size(DP) / count
    grad_out = factor * mask[:, None] * diff
    output_blocks = jnp.transpose(
        output_here.astype(BF).reshape(PIECE, 2 * CHIPS, width), (1, 0, 2)
    )
    output_back = lax.all_to_all(output_blocks, ROW_COL, 0, 0, tiled=True)
    output = jnp.transpose(
        output_back.reshape(CHIPS, 2, PIECE, width), (1, 0, 2, 3)
    ).reshape(SEQ, width).astype(F32)

    wide_grad = gather_tokens(grad_out.astype(BF))
    d_upper = gelu_back(mult(wide_grad, down_all))[0].astype(BF)
    d_normed_two = scatter_tokens(mult_right(d_upper, up_all))
    two_pairs = [(wide_two, d_upper), (wide_grad, active_here)]
    two_theirs = other_core(products(two_pairs, 1))
    d_normed_two = d_normed_two + (settled(output_back) + settled(two_theirs))
    two_grads = products(two_pairs, 0, two_theirs)
    two_part = scattered_over_latents(two_grads)
    back_two, d_g_two, d_b_two = norm_backward(d_normed_two, scaled_two, rstd_two, gain_two)
    grad_three = grad_out + back_two

    wide_three_grad = gather_tokens(grad_three.astype(BF))
    d_cmixed = mult(wide_three_grad, cout_all) + settled(two_grads)
    d_cmixed = d_cmixed.astype(BF).reshape(shape_four)
    d_cquery, d_ckeys, d_cvalues = attend_backward(cquery, ckeys, cvalues, cross_totals, d_cmixed)
    unused, cquery_back = jax.vjp(prep, cquery_raw, g_cquery)
    d_cquery_raw, d_g_cquery = cquery_back(d_cquery.reshape(HALF, heads, HD))
    d_cquery_here = d_cquery_raw.reshape(HALF, heads * HD).astype(BF)
    d_normed_three = scatter_tokens(mult_right(d_cquery_here, cquery_all))
    unused, ckey_back = jax.vjp(head_norm, ckey_raw, g_ckey)
    d_ckey_raw, d_g_ckey = ckey_back(d_ckeys)
    d_ckv = jnp.stack([d_ckey_raw, d_cvalues], axis=3).reshape(TXT, heads * 2 * HD).astype(BF)
    back_three, d_g_three, d_b_three = norm_backward(
        d_normed_three, scaled_three, rstd_three, gain_three
    )
    grad_two = grad_three + back_three

    three_grads = weight_grads(
        [(wide_three, d_cquery_here), (wide_three_grad, cmixed_here), (wide_text, d_ckv)]
    )

    wide_two_grad = gather_tokens(grad_two.astype(BF))
    d_mixed = mult(wide_two_grad, out_all) + settled(three_grads)
    d_mixed = d_mixed.astype(BF).reshape(shape_four)
    d_query, d_keys, d_values = attend_backward(query, keys, values, self_totals, d_mixed)
    d_both = jnp.concatenate([d_keys[0], d_values[0]], axis=2)
    d_both = d_both[:HALF] + other_core(swapped_heads(d_both[HALF:]).astype(BF)).astype(F32)
    unused, query_back = jax.vjp(prep, query_raw, g_query)
    d_query_raw, d_g_query = query_back(d_query.reshape(HALF, heads, HD))
    unused, key_back = jax.vjp(prep, key_raw, g_key)
    d_key_raw, d_g_key = key_back(d_both[..., :HD])
    d_packed = (
        jnp.stack([d_query_raw, d_key_raw, d_both[..., HD:]], axis=2)
        .reshape(HALF, heads * 3 * HD)
        .astype(BF)
    )
    d_inputs_part = mult_right(d_packed, qkv_all) + settled(two_part)
    late = settled(d_inputs_part).astype(BF)
    three_part = summed_over_latents(three_grads + late)
    d_packed_late = d_packed + late
    d_inputs = scatter_tokens(d_inputs_part)
    d_inputs = d_inputs + settled(three_part)
    back_one, d_g_one, d_b_one = norm_backward(d_inputs, scaled_one, rstd_one, gain_one)
    grad_one = grad_two + back_one

    d_shift_part = jnp.sum(d_inputs, axis=0)
    shared = jnp.concatenate([d_g_query, d_g_key, d_g_cquery, d_g_ckey, sse_local[None]])
    small = jnp.stack(
        [d_g_one, d_b_one, d_g_three, d_b_three, d_g_two, d_b_two, d_shift_part]
        + [jnp.pad(shared, (0, D - shared.shape[0]))]
    )
    piece = jnp.concatenate([grad_one.astype(BF), in_two(small)], axis=0)
    pieces = [piece] + [from_chip(piece, j) for j in range(1, CHIPS)]
    wide_one_grad = jnp.concatenate([p[:PIECE] for p in pieces], axis=0)
    small = sum(p[PIECE:].astype(F32) for p in pieces)
    small = small[:8] + small[8:]
    small = small + other_core(small)
    oq_grads = weight_grads([(wide_two_grad, mixed_here), (wide_one, d_packed_late)], grad_one)
    oq_part = summed_over_latents(oq_grads)
    d_joined = mult(wide_one_grad, skip_all)
    skip_sums = jnp.stack([jnp.sum(d_joined * skip_scaled, axis=0), jnp.sum(d_joined, axis=0)])
    skip_sums = skip_sums[:, : 2 * width] + other_core(skip_sums[:, 2 * width :])
    place = lax.axis_index(ROW_COL)
    shared_size = shared.shape[0]
    vector = jnp.concatenate(
        [
            lax.dynamic_slice_in_dim(small[:6], place * width, width, 1).reshape(-1),
            small[7, :shared_size],
            skip_sums.reshape(-1),
        ]
    )
    vector = jnp.pad(vector, (0, -vector.shape[0] % (D // 2))).reshape(-1, D // 2)
    vector_rows = vector.shape[0]
    latent_shift = lax.dynamic_slice_in_dim(small[6], row * (D // 2), D // 2, 0).astype(BF)
    d_w_mod = mult_left(emb_here, latent_shift[None])
    extra = jnp.concatenate([in_two(vector), d_w_mod.astype(BF)], axis=0).T
    extra = jnp.concatenate([extra, extra], axis=0)
    d_skip = weight_grads([(wide_one_grad, normed)])
    last_sent = jnp.concatenate([d_skip, extra], axis=1)
    def columns(summed, start, count):
        return jnp.concatenate(
            [summed[0][:, start : start + count], summed[1][:, start : start + count]], axis=1
        ).astype(F32)

    n_up = w_up.shape[1] // 2
    two_halves = spread_over_latents(two_part, row)
    d_w_up = columns(two_halves, 0, n_up)
    d_w_down = columns(two_halves, n_up, n_up).T
    skip_part = summed_over_latents(
        last_sent, 2 * width, vector_rows, (d_w_up, d_w_down)
    )
    both_gains = both_vectors[0] + settled(d_skip) + settled(skip_sums)
    weighted = d_joined * both_gains
    back_sums = sum_over_chips(
        jnp.stack([jnp.sum(weighted, axis=1), jnp.sum(weighted * skip_scaled, axis=1)])
    ) / (2 * D)
    back_joined = skip_rstd[:, None] * (
        weighted - back_sums[0][:, None] - skip_scaled * back_sums[1][:, None]
    )
    back_mine = back_joined[:, : 2 * width]
    pinned = settled(skip_part)
    back_theirs = other_core(back_joined[:, 2 * width :] + pinned)
    unturn = (CHIPS - chip) % CHIPS * PIECE
    back_mine = turned(back_mine, unturn)
    back_theirs = turned(back_theirs, unturn)
    back_tokens = lax.dynamic_slice_in_dim(
        jnp.concatenate([back_mine, back_theirs, back_mine], axis=0), core * HALF, SEQ, 0
    )
    d_hidden = back_tokens[:, :width]
    d_skipped = back_tokens[:, width:]

    five_grads = spread_over_latents(jnp.concatenate([oq_part, three_part], axis=1), row)
    d_w_cquery = columns(five_grads, 4 * width, width)
    d_w_cout = columns(five_grads, 5 * width, width).T
    d_w_ckv = columns(five_grads, 6 * width, 2 * width)
    count_blocks = max(lax.axis_size(DP) // 2, 1)
    d_w_ckv = d_w_ckv.reshape(count_blocks, -1, 4 * width)[:, : w_ckv.shape[0] // count_blocks]
    d_w_ckv = d_w_ckv.reshape(-1, 4 * width)
    last_grads = spread_over_latents(skip_part, row, False)
    d_w_out = columns(five_grads, 0, width).T
    d_w_qkv = columns(five_grads, width, 3 * width)
    d_w_skip = columns(last_grads, 0, 2 * width).reshape(D // 2, 2, 2, width)
    d_w_skip = jnp.transpose(d_w_skip, (2, 1, 3, 0)).reshape(2, 2 * width, D // 2)
    extra = last_grads[:, :, 2 * width :]
    extra = jnp.where(row == 0, extra[0], extra[1]).astype(F32).T
    vector = (extra[:vector_rows] + extra[vector_rows : 2 * vector_rows]).reshape(-1)
    d_w_mod = extra[2 * vector_rows :]
    d_g_one, d_b_one, d_g_three, d_b_three, d_g_two, d_b_two = vector[: 6 * width].reshape(6, width)
    shared = vector[6 * width : 6 * width + shared_size]
    d_g_query, d_g_key, d_g_cquery, d_g_ckey = shared[: 4 * HD].reshape(4, HD)
    loss = shared[4 * HD] / (count * D)
    skip_sums = vector[6 * width + shared_size : 10 * width + shared_size].reshape(2, 2, width)
    d_g_skip, d_b_skip = skip_sums
    return (
        output,
        d_hidden,
        d_skipped,
        d_w_skip,
        d_g_skip,
        d_b_skip,
        d_w_mod,
        d_g_one,
        d_b_one,
        d_w_qkv,
        d_g_query,
        d_g_key,
        d_w_out,
        d_g_three,
        d_b_three,
        d_w_cquery,
        d_w_ckv,
        d_g_cquery,
        d_g_ckey,
        d_w_cout,
        d_g_two,
        d_b_two,
        d_w_up,
        d_w_down,
        loss,
    )


def solution(mesh):
    side = math.isqrt(mesh.shape["dp"])
    split = Mesh(
        mesh.devices.reshape(side, side, mesh.shape["row"], 2, 2),
        ("dp_0", "dp_1", "row", "col_0", "col_1"),
    )
    in_specs = (
        P(DP, COL_ROW),
        P(DP, COL_ROW),
        P(DP, None, ROW_COL),
        P(DP, ROW_COL),
        P(DP),
        P(DP),
        P(None, DP),
        P(None, COL, "row"),
        P(None, COL_ROW),
        P(None, COL_ROW),
        P(COL, "row"),
        P(ROW_COL),
        P(ROW_COL),
        P("row", COL),
        P(),
        P(),
        P(COL, "row"),
        P(ROW_COL),
        P(ROW_COL),
        P("row", COL),
        P("row", COL),
        P(),
        P(),
        P(COL, "row"),
        P(ROW_COL),
        P(ROW_COL),
        P("row", COL),
        P(COL, "row"),
    )
    out_specs = (
        P(DP, ROW_COL),
        P(DP, COL_ROW),
        P(DP, COL_ROW),
        P(None, COL, "row"),
        P(None, COL_ROW),
        P(None, COL_ROW),
        P(COL, "row"),
        P(ROW_COL),
        P(ROW_COL),
        P("row", COL),
        P(),
        P(),
        P(COL, "row"),
        P(ROW_COL),
        P(ROW_COL),
        P("row", COL),
        P("row", COL),
        P(),
        P(),
        P(COL, "row"),
        P(ROW_COL),
        P(ROW_COL),
        P("row", COL),
        P(COL, "row"),
        P(),
    )
    return jax.shard_map(local, mesh=split, in_specs=in_specs, out_specs=out_specs, check_vma=False)
```

```python
from functools import partial
import math

import jax
import jax.numpy as jnp
from jax import lax
from jax.sharding import Mesh
from jax.sharding import PartitionSpec as P

D = 1408
HEADS = 16
HD = 88
FREQ = 256
TXT = 333
SEQ = 1024
LINE = ("row", "col_0")
CORE = "col_1"
COL = ("col_0", "col_1")
ROW_COL = ("row", "col_0", "col_1")
DP = ("dp_0", "dp_1")
ALL = ("dp_0", "dp_1", "row", "col_0", "col_1")
COL_ROW = ("col_0", "col_1", "row")
CHIPS = 4
HALF = SEQ // 2
PIECE = HALF // CHIPS
BF = jnp.bfloat16
F32 = jnp.float32


epsilon = 1e-06


def mult(left, right):
    return jnp.dot(left, right, preferred_element_type=jnp.float32)


def mult_left(left, right):
    return lax.dot_general(
        left, right, (((0,), (0,)), ((), ())), preferred_element_type=jnp.float32
    )


def mult_right(left, right):
    return lax.dot_general(
        left, right, (((1,), (1,)), ((), ())), preferred_element_type=jnp.float32
    )


def from_chip(value, ahead):
    return lax.ppermute(value, LINE, [(i, (i - ahead) % CHIPS) for i in range(CHIPS)])


def other_core(value):
    return lax.ppermute(value, CORE, [(0, 1), (1, 0)])


def other_row(value):
    return lax.ppermute(value, "row", [(0, 1), (1, 0)])


def gather_tokens(piece):
    return jnp.concatenate([piece] + [from_chip(piece, j) for j in range(1, CHIPS)], axis=0)


def scatter_tokens(partial_sums):
    total = partial_sums[:PIECE]
    for j in range(1, CHIPS):
        sent = partial_sums[j * PIECE : (j + 1) * PIECE].astype(BF)
        total = total + from_chip(sent, CHIPS - j).astype(F32)
    return total


def sum_over_chips(value):
    total = value
    for j in range(1, CHIPS):
        total = total + jnp.roll(from_chip(value, j), j * PIECE, axis=1)
    return total


def turned(value, start):
    twice = jnp.concatenate([value, value], axis=0)
    return lax.dynamic_slice_in_dim(twice, start, value.shape[0], 0)


def norm_forward(values, gain, offset):
    mean = jnp.mean(values, axis=1, keepdims=True)
    spread = jnp.mean(values * values, axis=1, keepdims=True) - mean * mean
    rstd = lax.rsqrt(spread + epsilon)
    scaled = (values - mean) * rstd
    return (scaled * gain + offset, scaled, rstd)


def norm_backward(grad, scaled, rstd, gain):
    weighted = grad * gain
    first = jnp.mean(weighted, axis=1, keepdims=True)
    second = jnp.mean(weighted * scaled, axis=1, keepdims=True)
    back = rstd * (weighted - first - scaled * second)
    return (back, jnp.sum(grad * scaled, axis=0), jnp.sum(grad, axis=0))


def halves_swapped(weight, dim, row, after=None):
    if after is not None:
        row = row + settled_index(after)
    kept = lax.dynamic_slice_in_dim(weight, row * (weight.shape[dim] // 2), weight.shape[dim] // 2, dim)
    sent = lax.dynamic_slice_in_dim(
        weight, (1 - row) * (weight.shape[dim] // 2), weight.shape[dim] // 2, dim
    )
    return (kept, other_row(sent))


def in_row_order(kept, received, dim, row):
    three = jnp.concatenate([received, kept, received], axis=dim)
    return lax.dynamic_slice_in_dim(
        three, (1 - row) * kept.shape[dim], 2 * kept.shape[dim], dim
    )


def settled(value):
    first = jnp.abs(value[(0,) * value.ndim].astype(F32))
    last = jnp.abs(value[(-1,) * value.ndim].astype(F32))
    return jnp.minimum(first + last, 0.0)


def settled_index(value):
    return settled(value).astype(jnp.int32)


def copied_to_each(value, axis):
    length = lax.axis_size(axis)
    return lax.all_to_all(
        jnp.broadcast_to(value[None], (length, *value.shape)), axis, 0, 0, tiled=True
    )


def in_two(value):
    high = lax.reduce_precision(value, exponent_bits=8, mantissa_bits=7)
    return jnp.concatenate([high.astype(BF), (value - high).astype(BF)], axis=0)


def with_other_core(own):
    return jnp.concatenate([own, other_core(own)], axis=1)


def whole_columns(weight, row, after=None):
    kept, received = halves_swapped(weight, 1, row, after)
    return in_row_order(kept, received, 0, row)


def padded(value):
    return jnp.pad(value, ((0, 0), (0, -value.shape[1] % 128)))


def blocks_by_latents(blocks, row):
    half = lax.axis_size(DP) // 2
    kept, sent = [], []
    for block in blocks:
        n = block.shape[1] // 2
        kept.append(padded(lax.dynamic_slice_in_dim(block, row * n, n, 1)))
        sent.append(padded(lax.dynamic_slice_in_dim(block, (1 - row) * n, n, 1)))
    kept = jnp.concatenate(kept, axis=1) if len(kept) > 1 else kept[0]
    sent = jnp.concatenate(sent, axis=1) if len(sent) > 1 else sent[0]
    return jnp.where(lax.axis_index(DP) // half == row, kept, other_row(sent))


def block_of_rows(weight, after):
    half = lax.axis_size(DP) // 2
    rows = weight.shape[0] // half
    place = lax.axis_index(DP) % half + settled_index(after)
    return lax.dynamic_slice_in_dim(weight, place * rows, rows, 0)


def block_of_columns(weight, after):
    half = lax.axis_size(DP) // 2
    columns = weight.shape[1] // half
    place = lax.axis_index(DP) % half + settled_index(after)
    return lax.dynamic_slice_in_dim(weight, place * columns, columns, 1).T


def products(pairs, part, added=None):
    outs = []
    start = 0
    for left, right in pairs:
        n = right.shape[1] // 2
        out = mult_left(left, right[:, part * n : (part + 1) * n])
        short = pairs[0][0].shape[1] - out.shape[0]
        if short:
            count = 2 * max(lax.axis_size(DP) // 2, 1)
            out = out.reshape(count, -1, n)
            out = jnp.pad(out, ((0, 0), (0, short // count), (0, 0))).reshape(-1, n)
        if added is not None:
            out = out + added[:, start : start + n].astype(F32)
        outs.append(out.astype(BF))
        start += n
    return jnp.concatenate(outs, axis=1) if len(outs) > 1 else outs[0]


def weight_grads(pairs, after=None):
    theirs = other_core(products(pairs, 1))
    if after is not None:
        theirs = theirs + settled(after).astype(BF)
    return products(pairs, 0, theirs)


def to_row_half(part):
    count = lax.axis_size(DP)
    half = count // 2
    pairs = []
    for i in range(count):
        for r in range(2):
            stays = i // half == r
            pairs.append((2 * i + r, 2 * i + r if stays else 2 * ((i + half) % count) + 1 - r))
    return lax.ppermute(part, DP + ("row",), pairs)


def scattered_over_latents(grads):
    count = lax.axis_size(DP)
    if count == 1:
        return grads
    blocks = grads.reshape(count, -1, grads.shape[1])
    return to_row_half(lax.psum_scatter(blocks, DP, scatter_dimension=0))


def row_halves(grads, row):
    kept, received = halves_swapped(grads, 0, row)
    first = row == 0
    return (jnp.where(first, kept, received), jnp.where(first, received, kept))


def summed_over_latents(grads, start=0, pairs_of=0, after=()):
    count = lax.axis_size(DP)
    if count == 1:
        return grads
    rows, n = grads.shape
    arrived = lax.all_to_all(grads.reshape(count, rows // count, n), DP, 0, 0, tiled=True)
    part = jnp.sum(arrived.astype(F32), axis=0)
    for value in after:
        part = part + settled(value)
    if pairs_of:
        exact = part[:, start : start + pairs_of] + part[:, start + pairs_of : start + 2 * pairs_of]
        rest = part[:, start + 2 * pairs_of :].astype(BF)
        part = jnp.concatenate([part[:, :start].astype(BF), in_two(exact.T).T, rest], axis=1)
    else:
        part = part.astype(BF)
    return to_row_half(part)


def spread_over_latents(part, row, gather=True):
    count = lax.axis_size(DP)
    if count == 1:
        return jnp.stack(row_halves(part, row))
    rows, n = part.shape
    if gather:
        spread = lax.all_gather(part, DP, axis=0)
    else:
        spread = copied_to_each(part, DP)
    return spread.reshape(2, count // 2 * rows, n)


def head_norm(values, gain):
    mean = jnp.mean(values, axis=-1, keepdims=True)
    spread = jnp.mean(values * values, axis=-1, keepdims=True) - mean * mean
    return (values - mean) * lax.rsqrt(spread + epsilon) * gain


def rotate(values):
    quarter = values.shape[-1] // 4
    return jnp.concatenate(
        [
            -values[..., quarter : 2 * quarter],
            values[..., :quarter],
            -values[..., 3 * quarter :],
            values[..., 2 * quarter : 3 * quarter],
        ],
        axis=-1,
    )


def qk_prep(raw, gain, cosine, sine):
    normal = head_norm(raw, gain)
    return normal * cosine + rotate(normal) * sine


def gelu_tanh(values):
    return jax.nn.gelu(values, approximate=True)


def rope_tables(positions):
    quarter = HD // 4
    freqs = jnp.exp(-math.log(10000.0) * jnp.arange(quarter, dtype=jnp.float32) / quarter)
    rows_angle = positions[0].astype(jnp.float32)[:, None] * freqs[None, :]
    cols_angle = positions[1].astype(jnp.float32)[:, None] * freqs[None, :]
    cosine = jnp.concatenate(
        [jnp.cos(rows_angle), jnp.cos(rows_angle), jnp.cos(cols_angle), jnp.cos(cols_angle)], axis=1
    )
    sine = jnp.concatenate(
        [jnp.sin(rows_angle), jnp.sin(rows_angle), jnp.sin(cols_angle), jnp.sin(cols_angle)], axis=1
    )
    return (cosine, sine)


def time_embed(steps):
    half = FREQ // 2
    freqs = jnp.exp(-math.log(10000.0) * jnp.arange(half, dtype=jnp.float32) / half)
    angles = steps.astype(jnp.float32)[:, None] * freqs[None, :]
    return jnp.concatenate([jnp.cos(angles), jnp.sin(angles)], axis=1)


def attend_forward(query, keys, values):
    scale = HD ** (-0.5)
    length = query.shape[1]
    block = min(512, length)
    outputs = []
    totals = []
    for start in range(0, length, block):
        piece = query[:, start : start + block]
        scores = scale * jnp.einsum(
            "lqhd,lkhd->lhqk", piece, keys, preferred_element_type=jnp.float32
        )
        top = jnp.max(scores, axis=-1, keepdims=True)
        expo = jnp.exp(scores - top)
        summed = jnp.sum(expo, axis=-1, keepdims=True)
        weights = expo / summed
        totals.append(top[..., 0] + jnp.log(summed[..., 0]))
        outputs.append(
            jnp.einsum(
                "lhqk,lkhd->lqhd",
                weights.astype(jnp.bfloat16),
                values,
                preferred_element_type=jnp.float32,
            )
        )
    return (jnp.concatenate(outputs, axis=1), jnp.concatenate(totals, axis=2))


def attend_backward(query, keys, values, totals, grad_out):
    scale = HD ** (-0.5)
    length = query.shape[1]
    block = min(512, length)
    d_keys = jnp.zeros(keys.shape, jnp.float32)
    d_values = jnp.zeros(values.shape, jnp.float32)
    d_query = []
    for start in range(0, length, block):
        piece = query[:, start : start + block]
        grad_piece = grad_out[:, start : start + block]
        scores = scale * jnp.einsum(
            "lqhd,lkhd->lhqk", piece, keys, preferred_element_type=jnp.float32
        )
        weights = jnp.exp(scores - totals[:, :, start : start + block, None])
        d_weights = jnp.einsum(
            "lqhd,lkhd->lhqk", grad_piece, values, preferred_element_type=jnp.float32
        )
        d_scores = weights * (d_weights - jnp.sum(d_weights * weights, axis=-1, keepdims=True))
        d_scores_b = d_scores.astype(jnp.bfloat16)
        d_query.append(
            scale
            * jnp.einsum("lhqk,lkhd->lqhd", d_scores_b, keys, preferred_element_type=jnp.float32)
        )
        d_keys = d_keys + scale * jnp.einsum(
            "lhqk,lqhd->lkhd", d_scores_b, piece, preferred_element_type=jnp.float32
        )
        d_values = d_values + jnp.einsum(
            "lhqk,lqhd->lkhd",
            weights.astype(jnp.bfloat16),
            grad_piece,
            preferred_element_type=jnp.float32,
        )
    return (jnp.concatenate(d_query, axis=1), d_keys, d_values)


def local(
    hidden,
    skipped,
    text,
    teacher,
    valid,
    steps,
    positions,
    w_skip,
    g_skip,
    b_skip,
    w_mod,
    g_one,
    b_one,
    w_qkv,
    g_query,
    g_key,
    w_out,
    g_three,
    b_three,
    w_cquery,
    w_ckv,
    g_cquery,
    g_ckey,
    w_cout,
    g_two,
    b_two,
    w_up,
    w_down,
):
    row = lax.axis_index("row")
    chip = lax.axis_index(LINE)
    core = lax.axis_index(CORE)
    width = hidden.shape[1]
    turn = chip * PIECE
    heads_own = HEADS // (2 * CHIPS)
    heads = 2 * heads_own
    shape_four = (1, HALF, heads, HD)

    def own_tokens(values):
        return turned(lax.dynamic_slice_in_dim(values, core * HALF, HALF, 0), turn)

    def other_tokens(values):
        return turned(lax.dynamic_slice_in_dim(values, (1 - core) * HALF, HALF, 0), turn)

    skip_two = jnp.transpose(w_skip.reshape(2, 2, width, D // 2), (3, 1, 0, 2)).reshape(
        D // 2, 4 * width
    )
    skip_kept, skip_received = halves_swapped(skip_two, 1, row)
    skip_own = in_row_order(skip_kept, skip_received, 0, row)
    skip_other = other_core(skip_own)
    skip_all = jnp.concatenate([skip_own, skip_other], axis=1)
    qkv_all = with_other_core(whole_columns(w_qkv, row, skip_received))
    mask_all = valid.astype(F32)
    if lax.axis_size(DP) == 1:
        count = jnp.sum(mask_all)
        out_all = with_other_core(whole_columns(w_out.T, row))
        cquery_all = with_other_core(whole_columns(w_cquery, row))
        cout_all = with_other_core(whole_columns(w_cout.T, row))
        ckv_all = with_other_core(whole_columns(w_ckv, row))
        up_all = with_other_core(whole_columns(w_up, row))
        down_all = with_other_core(whole_columns(w_down.T, row))
    else:
        ckv_block = block_of_rows(w_ckv, skip_received)
        ckv_rows = ckv_block.shape[0]
        ckv_block = jnp.pad(ckv_block, ((0, D // lax.axis_size(DP) - ckv_rows), (0, 0)))
        four_block = blocks_by_latents(
            [
                block_of_columns(w_out, skip_received),
                block_of_rows(w_cquery, skip_received),
                block_of_columns(w_cout, skip_received),
                ckv_block,
            ],
            row,
        )
        tally = jnp.sum(mask_all)
        parts = jnp.stack([jnp.floor(tally / 32.0), tally - 32.0 * jnp.floor(tally / 32.0)])
        four_block = lax.dynamic_update_slice(four_block, parts.astype(BF)[None], (0, width))
        four_own = lax.all_gather(four_block, DP, axis=0, tiled=True)
        parts = four_own.reshape(lax.axis_size(DP), -1, four_own.shape[1])[:, 0, width : width + 2]
        count = jnp.sum(parts.astype(F32) @ jnp.array([32.0, 1.0], F32))
        two_block = blocks_by_latents(
            [block_of_rows(w_up, four_own), block_of_columns(w_down, four_own)], row
        )
        two_own = lax.all_gather(two_block, DP, axis=0, tiled=True)
        four_other = other_core(four_own)

        def both(start, count):
            return jnp.concatenate(
                [four_own[:, start : start + count], four_other[:, start : start + count]], axis=1
            )

        step = width + (-width) % 128
        out_all = both(0, width)
        cquery_all = both(step, width)
        cout_all = both(2 * step, width)
        ckv_all = both(3 * step, 2 * width).reshape(lax.axis_size(DP), -1, 4 * width)
        ckv_all = ckv_all[:, :ckv_rows].reshape(-1, 4 * width)
        two_other = other_core(two_own)
        hidden_own = two_own.shape[1] // 2
        up_all = jnp.concatenate([two_own[:, :hidden_own], two_other[:, :hidden_own]], axis=1)
        down_all = jnp.concatenate([two_own[:, hidden_own:], two_other[:, hidden_own:]], axis=1)

    freq_here = w_mod.shape[0]
    mask_all = valid.astype(F32)
    emb = time_embed(steps).astype(BF)
    emb_here = lax.dynamic_slice_in_dim(emb, lax.axis_index(COL) * freq_here, freq_here, 1)
    shift_part = mult(emb_here, w_mod)
    vectors = jnp.concatenate(
        [jnp.stack([g_one, b_one, g_three, b_three, g_two, b_two]).reshape(-1), shift_part[0]]
    ) + settled(skip_received)
    gathered = copied_to_each(vectors, ROW_COL)
    gains = jnp.transpose(gathered[:, : 6 * width].reshape(8, 6, width), (1, 0, 2)).reshape(6, D)
    gain_one, offset_one, gain_three, offset_three, gain_two, offset_two = gains
    shift = jnp.sum(gathered[:, 6 * width :].reshape(2, 4, D // 2), axis=1).reshape(D)
    mask = lax.dynamic_slice_in_dim(mask_all, core * HALF + turn, PIECE, 0)

    cosine, sine = rope_tables(own_tokens(positions.T).T)
    prep = partial(qk_prep, cosine=cosine[:, None, :], sine=sine[:, None, :])

    joined = jnp.concatenate([hidden, skipped], axis=1)
    mine = own_tokens(joined)
    theirs = other_core(other_tokens(joined))
    pairs = jnp.concatenate([mine, theirs], axis=1).astype(F32)
    skip_vectors = jnp.stack([g_skip, b_skip]).reshape(2, 2 * width)
    both_vectors = jnp.concatenate([skip_vectors, other_core(skip_vectors)], axis=1)
    skip_sums = sum_over_chips(jnp.stack([jnp.sum(pairs, axis=1), jnp.sum(pairs * pairs, axis=1)]))
    skip_mean = skip_sums[0] / (2 * D)
    skip_rstd = lax.rsqrt(skip_sums[1] / (2 * D) - skip_mean * skip_mean + epsilon)
    skip_scaled = (pairs - skip_mean[:, None]) * skip_rstd[:, None]
    normed = (skip_scaled * both_vectors[0] + both_vectors[1]).astype(BF)
    stream = scatter_tokens(mult_right(normed, skip_all))

    normed_one, scaled_one, rstd_one = norm_forward(stream, gain_one, offset_one)
    text_sent = text[0] + settled(rstd_one).astype(BF)
    wide_text = jnp.transpose(copied_to_each(text_sent, ROW_COL), (1, 0, 2)).reshape(TXT, -1)
    wide_one = gather_tokens((normed_one + shift).astype(BF))
    packed = (mult(wide_one, qkv_all) + settled(wide_text)).reshape(HALF, heads, 3, HD)
    query_raw = packed[:, :, 0]
    key_raw = packed[:, :, 1]
    query = prep(query_raw, g_query).astype(BF).reshape(shape_four)
    keys_here = prep(key_raw, g_key).astype(BF)
    values_here = packed[:, :, 2].astype(BF)

    def swapped_heads(values):
        return jnp.concatenate([values[:, heads_own:], values[:, :heads_own]], axis=1)

    key_values = other_core(swapped_heads(jnp.concatenate([keys_here, values_here], axis=2)))
    keys = jnp.concatenate([keys_here, key_values[..., :HD]], axis=0)[None]
    values = jnp.concatenate([values_here, key_values[..., HD:]], axis=0)[None]
    mixed, self_totals = attend_forward(query, keys, values)
    mixed_here = mixed.reshape(HALF, heads * HD).astype(BF)
    stream_two = stream + scatter_tokens(mult_right(mixed_here, out_all))

    normed_three, scaled_three, rstd_three = norm_forward(stream_two, gain_three, offset_three)
    teacher_blocks = jnp.transpose(
        teacher.reshape(2, CHIPS, PIECE, width) + settled(rstd_three).astype(BF), (1, 0, 2, 3)
    ).reshape(2 * CHIPS, PIECE, width)
    teacher_here = jnp.transpose(
        lax.all_to_all(teacher_blocks, ROW_COL, 0, 0, tiled=True), (1, 0, 2)
    ).reshape(PIECE, D)
    wide_three = gather_tokens(normed_three.astype(BF))
    cquery_raw = mult(wide_three, cquery_all) + settled(teacher_here)
    cquery_raw = cquery_raw.reshape(HALF, heads, HD)
    cquery = prep(cquery_raw, g_cquery).astype(BF).reshape(shape_four)
    ckv = mult(wide_text, ckv_all).reshape(1, TXT, heads, 2, HD)
    ckey_raw = ckv[:, :, :, 0]
    ckeys = head_norm(ckey_raw, g_ckey).astype(BF)
    cvalues = ckv[:, :, :, 1].astype(BF)
    cmixed, cross_totals = attend_forward(cquery, ckeys, cvalues)
    cmixed_here = cmixed.reshape(HALF, heads * HD).astype(BF)
    stream_three = stream_two + scatter_tokens(mult_right(cmixed_here, cout_all))

    normed_two, scaled_two, rstd_two = norm_forward(stream_three, gain_two, offset_two)
    wide_two = gather_tokens(normed_two.astype(BF))
    upper = mult(wide_two, up_all)
    active, gelu_back = jax.vjp(gelu_tanh, upper)
    active_here = active.astype(BF)
    output_here = stream_three + scatter_tokens(mult_right(active_here, down_all))

    diff = output_here - teacher_here.astype(F32)
    sse_local = jnp.sum(mask[:, None] * diff * diff)
    factor = 32.0 * lax.axis_size(DP) / count
    grad_out = factor * mask[:, None] * diff
    output_blocks = jnp.transpose(
        output_here.astype(BF).reshape(PIECE, 2 * CHIPS, width), (1, 0, 2)
    )
    output_back = lax.all_to_all(output_blocks, ROW_COL, 0, 0, tiled=True)
    output = jnp.transpose(
        output_back.reshape(CHIPS, 2, PIECE, width), (1, 0, 2, 3)
    ).reshape(SEQ, width).astype(F32)

    wide_grad = gather_tokens(grad_out.astype(BF))
    d_upper = gelu_back(mult(wide_grad, down_all))[0].astype(BF)
    d_normed_two = scatter_tokens(mult_right(d_upper, up_all))
    two_pairs = [(wide_two, d_upper), (wide_grad, active_here)]
    two_theirs = other_core(products(two_pairs, 1))
    d_normed_two = d_normed_two + (settled(output_back) + settled(two_theirs))
    two_grads = products(two_pairs, 0, two_theirs)
    two_part = scattered_over_latents(two_grads)
    back_two, d_g_two, d_b_two = norm_backward(d_normed_two, scaled_two, rstd_two, gain_two)
    grad_three = grad_out + back_two

    wide_three_grad = gather_tokens(grad_three.astype(BF))
    d_cmixed = mult(wide_three_grad, cout_all) + settled(two_grads)
    d_cmixed = d_cmixed.astype(BF).reshape(shape_four)
    d_cquery, d_ckeys, d_cvalues = attend_backward(cquery, ckeys, cvalues, cross_totals, d_cmixed)
    unused, cquery_back = jax.vjp(prep, cquery_raw, g_cquery)
    d_cquery_raw, d_g_cquery = cquery_back(d_cquery.reshape(HALF, heads, HD))
    d_cquery_here = d_cquery_raw.reshape(HALF, heads * HD).astype(BF)
    d_normed_three = scatter_tokens(mult_right(d_cquery_here, cquery_all))
    unused, ckey_back = jax.vjp(head_norm, ckey_raw, g_ckey)
    d_ckey_raw, d_g_ckey = ckey_back(d_ckeys)
    d_ckv = jnp.stack([d_ckey_raw, d_cvalues], axis=3).reshape(TXT, heads * 2 * HD).astype(BF)
    back_three, d_g_three, d_b_three = norm_backward(
        d_normed_three, scaled_three, rstd_three, gain_three
    )
    grad_two = grad_three + back_three

    three_grads = weight_grads(
        [(wide_three, d_cquery_here), (wide_three_grad, cmixed_here), (wide_text, d_ckv)]
    )

    wide_two_grad = gather_tokens(grad_two.astype(BF))
    d_mixed = mult(wide_two_grad, out_all) + settled(three_grads)
    d_mixed = d_mixed.astype(BF).reshape(shape_four)
    d_query, d_keys, d_values = attend_backward(query, keys, values, self_totals, d_mixed)
    d_both = jnp.concatenate([d_keys[0], d_values[0]], axis=2)
    d_both = d_both[:HALF] + other_core(swapped_heads(d_both[HALF:]).astype(BF)).astype(F32)
    unused, query_back = jax.vjp(prep, query_raw, g_query)
    d_query_raw, d_g_query = query_back(d_query.reshape(HALF, heads, HD))
    unused, key_back = jax.vjp(prep, key_raw, g_key)
    d_key_raw, d_g_key = key_back(d_both[..., :HD])
    d_packed = (
        jnp.stack([d_query_raw, d_key_raw, d_both[..., HD:] + settled(two_part)], axis=2)
        .reshape(HALF, heads * 3 * HD)
        .astype(BF)
    )
    d_inputs_part = mult_right(d_packed, qkv_all)
    late = settled(d_inputs_part).astype(BF)
    three_part = summed_over_latents(three_grads + late)
    d_packed_late = d_packed + late
    d_inputs = scatter_tokens(d_inputs_part)
    d_inputs = d_inputs + settled(three_part)
    back_one, d_g_one, d_b_one = norm_backward(d_inputs, scaled_one, rstd_one, gain_one)
    grad_one = grad_two + back_one

    d_shift_part = jnp.sum(d_inputs, axis=0)
    shared = jnp.concatenate([d_g_query, d_g_key, d_g_cquery, d_g_ckey, sse_local[None]])
    small = jnp.stack(
        [d_g_one, d_b_one, d_g_three, d_b_three, d_g_two, d_b_two, d_shift_part]
        + [jnp.pad(shared, (0, D - shared.shape[0]))]
    )
    piece = jnp.concatenate([grad_one.astype(BF), in_two(small)], axis=0)
    pieces = [piece] + [from_chip(piece, j) for j in range(1, CHIPS)]
    wide_one_grad = jnp.concatenate([p[:PIECE] for p in pieces], axis=0)
    small = sum(p[PIECE:].astype(F32) for p in pieces)
    small = small[:8] + small[8:]
    small = small + other_core(small)
    oq_grads = weight_grads([(wide_two_grad, mixed_here), (wide_one, d_packed_late)], grad_one)
    oq_part = summed_over_latents(oq_grads)
    d_joined = mult(wide_one_grad, skip_all)
    skip_sums = jnp.stack([jnp.sum(d_joined * skip_scaled, axis=0), jnp.sum(d_joined, axis=0)])
    skip_sums = skip_sums[:, : 2 * width] + other_core(skip_sums[:, 2 * width :])
    place = lax.axis_index(ROW_COL)
    shared_size = shared.shape[0]
    vector = jnp.concatenate(
        [
            lax.dynamic_slice_in_dim(small[:6], place * width, width, 1).reshape(-1),
            small[7, :shared_size],
            skip_sums.reshape(-1),
        ]
    )
    vector = jnp.pad(vector, (0, -vector.shape[0] % (D // 2))).reshape(-1, D // 2)
    vector_rows = vector.shape[0]
    latent_shift = lax.dynamic_slice_in_dim(small[6], row * (D // 2), D // 2, 0).astype(BF)
    d_w_mod = mult_left(emb_here, latent_shift[None])
    extra = jnp.concatenate([in_two(vector), d_w_mod.astype(BF)], axis=0).T
    extra = jnp.concatenate([extra, extra], axis=0)
    d_skip = weight_grads([(wide_one_grad, normed)])
    last_sent = jnp.concatenate([d_skip, extra], axis=1)
    def columns(summed, start, count):
        return jnp.concatenate(
            [summed[0][:, start : start + count], summed[1][:, start : start + count]], axis=1
        ).astype(F32)

    n_up = w_up.shape[1] // 2
    two_halves = spread_over_latents(two_part, row)
    d_w_up = columns(two_halves, 0, n_up)
    d_w_down = columns(two_halves, n_up, n_up).T
    skip_part = summed_over_latents(
        last_sent, 2 * width, vector_rows, (d_w_up, d_w_down)
    )
    both_gains = both_vectors[0] + settled(d_skip) + settled(skip_sums)
    weighted = d_joined * both_gains
    back_sums = sum_over_chips(
        jnp.stack([jnp.sum(weighted, axis=1), jnp.sum(weighted * skip_scaled, axis=1)])
    ) / (2 * D)
    back_joined = skip_rstd[:, None] * (
        weighted - back_sums[0][:, None] - skip_scaled * back_sums[1][:, None]
    )
    back_mine = back_joined[:, : 2 * width]
    pinned = settled(skip_part)
    back_theirs = other_core(back_joined[:, 2 * width :] + pinned)
    unturn = (CHIPS - chip) % CHIPS * PIECE
    back_mine = turned(back_mine, unturn)
    back_theirs = turned(back_theirs, unturn)
    back_tokens = lax.dynamic_slice_in_dim(
        jnp.concatenate([back_mine, back_theirs, back_mine], axis=0), core * HALF, SEQ, 0
    )
    d_hidden = back_tokens[:, :width]
    d_skipped = back_tokens[:, width:]

    five_grads = spread_over_latents(jnp.concatenate([oq_part, three_part], axis=1), row)
    d_w_cquery = columns(five_grads, 4 * width, width)
    d_w_cout = columns(five_grads, 5 * width, width).T
    d_w_ckv = columns(five_grads, 6 * width, 2 * width)
    count_blocks = max(lax.axis_size(DP) // 2, 1)
    d_w_ckv = d_w_ckv.reshape(count_blocks, -1, 4 * width)[:, : w_ckv.shape[0] // count_blocks]
    d_w_ckv = d_w_ckv.reshape(-1, 4 * width)
    last_grads = spread_over_latents(skip_part, row, False)
    d_w_out = columns(five_grads, 0, width).T
    d_w_qkv = columns(five_grads, width, 3 * width)
    d_w_skip = columns(last_grads, 0, 2 * width).reshape(D // 2, 2, 2, width)
    d_w_skip = jnp.transpose(d_w_skip, (2, 1, 3, 0)).reshape(2, 2 * width, D // 2)
    extra = last_grads[:, :, 2 * width :]
    extra = jnp.where(row == 0, extra[0], extra[1]).astype(F32).T
    vector = (extra[:vector_rows] + extra[vector_rows : 2 * vector_rows]).reshape(-1)
    d_w_mod = extra[2 * vector_rows :]
    d_g_one, d_b_one, d_g_three, d_b_three, d_g_two, d_b_two = vector[: 6 * width].reshape(6, width)
    shared = vector[6 * width : 6 * width + shared_size]
    d_g_query, d_g_key, d_g_cquery, d_g_ckey = shared[: 4 * HD].reshape(4, HD)
    loss = shared[4 * HD] / (count * D)
    skip_sums = vector[6 * width + shared_size : 10 * width + shared_size].reshape(2, 2, width)
    d_g_skip, d_b_skip = skip_sums
    return (
        output,
        d_hidden,
        d_skipped,
        d_w_skip,
        d_g_skip,
        d_b_skip,
        d_w_mod,
        d_g_one,
        d_b_one,
        d_w_qkv,
        d_g_query,
        d_g_key,
        d_w_out,
        d_g_three,
        d_b_three,
        d_w_cquery,
        d_w_ckv,
        d_g_cquery,
        d_g_ckey,
        d_w_cout,
        d_g_two,
        d_b_two,
        d_w_up,
        d_w_down,
        loss,
    )


def solution(mesh):
    side = math.isqrt(mesh.shape["dp"])
    split = Mesh(
        mesh.devices.reshape(side, side, mesh.shape["row"], 2, 2),
        ("dp_0", "dp_1", "row", "col_0", "col_1"),
    )
    in_specs = (
        P(DP, COL_ROW),
        P(DP, COL_ROW),
        P(DP, None, ROW_COL),
        P(DP, ROW_COL),
        P(DP),
        P(DP),
        P(None, DP),
        P(None, COL, "row"),
        P(None, COL_ROW),
        P(None, COL_ROW),
        P(COL, "row"),
        P(ROW_COL),
        P(ROW_COL),
        P("row", COL),
        P(),
        P(),
        P(COL, "row"),
        P(ROW_COL),
        P(ROW_COL),
        P("row", COL),
        P("row", COL),
        P(),
        P(),
        P(COL, "row"),
        P(ROW_COL),
        P(ROW_COL),
        P("row", COL),
        P(COL, "row"),
    )
    out_specs = (
        P(DP, ROW_COL),
        P(DP, COL_ROW),
        P(DP, COL_ROW),
        P(None, COL, "row"),
        P(None, COL_ROW),
        P(None, COL_ROW),
        P(COL, "row"),
        P(ROW_COL),
        P(ROW_COL),
        P("row", COL),
        P(),
        P(),
        P(COL, "row"),
        P(ROW_COL),
        P(ROW_COL),
        P("row", COL),
        P("row", COL),
        P(),
        P(),
        P(COL, "row"),
        P(ROW_COL),
        P(ROW_COL),
        P("row", COL),
        P(COL, "row"),
        P(),
    )
    return jax.shard_map(local, mesh=split, in_specs=in_specs, out_specs=out_specs, check_vma=False)
```

```python
from functools import partial
import math

import jax
import jax.numpy as jnp
from jax import lax
from jax.sharding import Mesh
from jax.sharding import PartitionSpec as P

D = 1408
HEADS = 16
HD = 88
FREQ = 256
TXT = 333
SEQ = 1024
LINE = ("row", "col_0")
CORE = "col_1"
COL = ("col_0", "col_1")
ROW_COL = ("row", "col_0", "col_1")
DP = ("dp_0", "dp_1")
ALL = ("dp_0", "dp_1", "row", "col_0", "col_1")
COL_ROW = ("col_0", "col_1", "row")
CHIPS = 4
HALF = SEQ // 2
PIECE = HALF // CHIPS
BF = jnp.bfloat16
F32 = jnp.float32


epsilon = 1e-06


def mult(left, right):
    return jnp.dot(left, right, preferred_element_type=jnp.float32)


def mult_left(left, right):
    return lax.dot_general(
        left, right, (((0,), (0,)), ((), ())), preferred_element_type=jnp.float32
    )


def mult_right(left, right):
    return lax.dot_general(
        left, right, (((1,), (1,)), ((), ())), preferred_element_type=jnp.float32
    )


def from_chip(value, ahead):
    return lax.ppermute(value, LINE, [(i, (i - ahead) % CHIPS) for i in range(CHIPS)])


def other_core(value):
    return lax.ppermute(value, CORE, [(0, 1), (1, 0)])


def other_row(value):
    return lax.ppermute(value, "row", [(0, 1), (1, 0)])


def gather_tokens(piece):
    return jnp.concatenate([piece] + [from_chip(piece, j) for j in range(1, CHIPS)], axis=0)


def scatter_tokens(partial_sums):
    total = partial_sums[:PIECE]
    for j in range(1, CHIPS):
        sent = partial_sums[j * PIECE : (j + 1) * PIECE].astype(BF)
        total = total + from_chip(sent, CHIPS - j).astype(F32)
    return total


def sum_over_chips(value):
    total = value
    for j in range(1, CHIPS):
        total = total + jnp.roll(from_chip(value, j), j * PIECE, axis=1)
    return total


def turned(value, start):
    twice = jnp.concatenate([value, value], axis=0)
    return lax.dynamic_slice_in_dim(twice, start, value.shape[0], 0)


def norm_forward(values, gain, offset):
    mean = jnp.mean(values, axis=1, keepdims=True)
    spread = jnp.mean(values * values, axis=1, keepdims=True) - mean * mean
    rstd = lax.rsqrt(spread + epsilon)
    scaled = (values - mean) * rstd
    return (scaled * gain + offset, scaled, rstd)


def norm_backward(grad, scaled, rstd, gain):
    weighted = grad * gain
    first = jnp.mean(weighted, axis=1, keepdims=True)
    second = jnp.mean(weighted * scaled, axis=1, keepdims=True)
    back = rstd * (weighted - first - scaled * second)
    return (back, jnp.sum(grad * scaled, axis=0), jnp.sum(grad, axis=0))


def halves_swapped(weight, dim, row, after=None):
    if after is not None:
        row = row + settled_index(after)
    kept = lax.dynamic_slice_in_dim(weight, row * (weight.shape[dim] // 2), weight.shape[dim] // 2, dim)
    sent = lax.dynamic_slice_in_dim(
        weight, (1 - row) * (weight.shape[dim] // 2), weight.shape[dim] // 2, dim
    )
    return (kept, other_row(sent))


def in_row_order(kept, received, dim, row):
    three = jnp.concatenate([received, kept, received], axis=dim)
    return lax.dynamic_slice_in_dim(
        three, (1 - row) * kept.shape[dim], 2 * kept.shape[dim], dim
    )


def settled(value):
    first = jnp.abs(value[(0,) * value.ndim].astype(F32))
    last = jnp.abs(value[(-1,) * value.ndim].astype(F32))
    return jnp.minimum(first + last, 0.0)


def settled_index(value):
    return settled(value).astype(jnp.int32)


def copied_to_each(value, axis):
    length = lax.axis_size(axis)
    return lax.all_to_all(
        jnp.broadcast_to(value[None], (length, *value.shape)), axis, 0, 0, tiled=True
    )


def in_two(value):
    high = lax.reduce_precision(value, exponent_bits=8, mantissa_bits=7)
    return jnp.concatenate([high.astype(BF), (value - high).astype(BF)], axis=0)


def with_other_core(own):
    return jnp.concatenate([own, other_core(own)], axis=1)


def whole_columns(weight, row, after=None):
    kept, received = halves_swapped(weight, 1, row, after)
    return in_row_order(kept, received, 0, row)


def padded(value):
    return jnp.pad(value, ((0, 0), (0, -value.shape[1] % 128)))


def blocks_by_latents(blocks, row):
    half = lax.axis_size(DP) // 2
    kept, sent = [], []
    for block in blocks:
        n = block.shape[1] // 2
        kept.append(padded(lax.dynamic_slice_in_dim(block, row * n, n, 1)))
        sent.append(padded(lax.dynamic_slice_in_dim(block, (1 - row) * n, n, 1)))
    kept = jnp.concatenate(kept, axis=1) if len(kept) > 1 else kept[0]
    sent = jnp.concatenate(sent, axis=1) if len(sent) > 1 else sent[0]
    return jnp.where(lax.axis_index(DP) // half == row, kept, other_row(sent))


def block_of_rows(weight, after):
    half = lax.axis_size(DP) // 2
    rows = weight.shape[0] // half
    place = lax.axis_index(DP) % half + settled_index(after)
    return lax.dynamic_slice_in_dim(weight, place * rows, rows, 0)


def block_of_columns(weight, after):
    half = lax.axis_size(DP) // 2
    columns = weight.shape[1] // half
    place = lax.axis_index(DP) % half + settled_index(after)
    return lax.dynamic_slice_in_dim(weight, place * columns, columns, 1).T


def products(pairs, part, added=None):
    outs = []
    start = 0
    for left, right in pairs:
        n = right.shape[1] // 2
        out = mult_left(left, right[:, part * n : (part + 1) * n])
        short = pairs[0][0].shape[1] - out.shape[0]
        if short:
            count = 2 * max(lax.axis_size(DP) // 2, 1)
            out = out.reshape(count, -1, n)
            out = jnp.pad(out, ((0, 0), (0, short // count), (0, 0))).reshape(-1, n)
        if added is not None:
            out = out + added[:, start : start + n].astype(F32)
        outs.append(out.astype(BF))
        start += n
    return jnp.concatenate(outs, axis=1) if len(outs) > 1 else outs[0]


def weight_grads(pairs, after=None):
    theirs = other_core(products(pairs, 1))
    if after is not None:
        theirs = theirs + settled(after).astype(BF)
    return products(pairs, 0, theirs)


def to_row_half(part):
    count = lax.axis_size(DP)
    half = count // 2
    pairs = []
    for i in range(count):
        for r in range(2):
            stays = i // half == r
            pairs.append((2 * i + r, 2 * i + r if stays else 2 * ((i + half) % count) + 1 - r))
    return lax.ppermute(part, DP + ("row",), pairs)


def scattered_over_latents(grads):
    count = lax.axis_size(DP)
    if count == 1:
        return grads
    blocks = grads.reshape(count, -1, grads.shape[1])
    return to_row_half(lax.psum_scatter(blocks, DP, scatter_dimension=0))


def row_halves(grads, row):
    kept, received = halves_swapped(grads, 0, row)
    first = row == 0
    return (jnp.where(first, kept, received), jnp.where(first, received, kept))


def summed_over_latents(grads, start=0, pairs_of=0, after=()):
    count = lax.axis_size(DP)
    if count == 1:
        return grads
    rows, n = grads.shape
    arrived = lax.all_to_all(grads.reshape(count, rows // count, n), DP, 0, 0, tiled=True)
    part = jnp.sum(arrived.astype(F32), axis=0)
    for value in after:
        part = part + settled(value)
    if pairs_of:
        exact = part[:, start : start + pairs_of] + part[:, start + pairs_of : start + 2 * pairs_of]
        rest = part[:, start + 2 * pairs_of :].astype(BF)
        part = jnp.concatenate([part[:, :start].astype(BF), in_two(exact.T).T, rest], axis=1)
    else:
        part = part.astype(BF)
    return to_row_half(part)


def spread_over_latents(part, row, gather=True):
    count = lax.axis_size(DP)
    if count == 1:
        return jnp.stack(row_halves(part, row))
    rows, n = part.shape
    if gather:
        spread = lax.all_gather(part, DP, axis=0)
    else:
        spread = copied_to_each(part, DP)
    return spread.reshape(2, count // 2 * rows, n)


def head_norm(values, gain):
    mean = jnp.mean(values, axis=-1, keepdims=True)
    spread = jnp.mean(values * values, axis=-1, keepdims=True) - mean * mean
    return (values - mean) * lax.rsqrt(spread + epsilon) * gain


def rotate(values):
    quarter = values.shape[-1] // 4
    return jnp.concatenate(
        [
            -values[..., quarter : 2 * quarter],
            values[..., :quarter],
            -values[..., 3 * quarter :],
            values[..., 2 * quarter : 3 * quarter],
        ],
        axis=-1,
    )


def qk_prep(raw, gain, cosine, sine):
    normal = head_norm(raw, gain)
    return normal * cosine + rotate(normal) * sine


def gelu_tanh(values):
    return jax.nn.gelu(values, approximate=True)


def rope_tables(positions):
    quarter = HD // 4
    freqs = jnp.exp(-math.log(10000.0) * jnp.arange(quarter, dtype=jnp.float32) / quarter)
    rows_angle = positions[0].astype(jnp.float32)[:, None] * freqs[None, :]
    cols_angle = positions[1].astype(jnp.float32)[:, None] * freqs[None, :]
    cosine = jnp.concatenate(
        [jnp.cos(rows_angle), jnp.cos(rows_angle), jnp.cos(cols_angle), jnp.cos(cols_angle)], axis=1
    )
    sine = jnp.concatenate(
        [jnp.sin(rows_angle), jnp.sin(rows_angle), jnp.sin(cols_angle), jnp.sin(cols_angle)], axis=1
    )
    return (cosine, sine)


def time_embed(steps):
    half = FREQ // 2
    freqs = jnp.exp(-math.log(10000.0) * jnp.arange(half, dtype=jnp.float32) / half)
    angles = steps.astype(jnp.float32)[:, None] * freqs[None, :]
    return jnp.concatenate([jnp.cos(angles), jnp.sin(angles)], axis=1)


def attend_forward(query, keys, values):
    scale = HD ** (-0.5)
    length = query.shape[1]
    block = min(512, length)
    outputs = []
    totals = []
    for start in range(0, length, block):
        piece = query[:, start : start + block]
        scores = scale * jnp.einsum(
            "lqhd,lkhd->lhqk", piece, keys, preferred_element_type=jnp.float32
        )
        top = jnp.max(scores, axis=-1, keepdims=True)
        expo = jnp.exp(scores - top)
        summed = jnp.sum(expo, axis=-1, keepdims=True)
        weights = expo / summed
        totals.append(top[..., 0] + jnp.log(summed[..., 0]))
        outputs.append(
            jnp.einsum(
                "lhqk,lkhd->lqhd",
                weights.astype(jnp.bfloat16),
                values,
                preferred_element_type=jnp.float32,
            )
        )
    return (jnp.concatenate(outputs, axis=1), jnp.concatenate(totals, axis=2))


def attend_backward(query, keys, values, totals, grad_out):
    scale = HD ** (-0.5)
    length = query.shape[1]
    block = min(512, length)
    d_keys = jnp.zeros(keys.shape, jnp.float32)
    d_values = jnp.zeros(values.shape, jnp.float32)
    d_query = []
    for start in range(0, length, block):
        piece = query[:, start : start + block]
        grad_piece = grad_out[:, start : start + block]
        scores = scale * jnp.einsum(
            "lqhd,lkhd->lhqk", piece, keys, preferred_element_type=jnp.float32
        )
        weights = jnp.exp(scores - totals[:, :, start : start + block, None])
        d_weights = jnp.einsum(
            "lqhd,lkhd->lhqk", grad_piece, values, preferred_element_type=jnp.float32
        )
        d_scores = weights * (d_weights - jnp.sum(d_weights * weights, axis=-1, keepdims=True))
        d_scores_b = d_scores.astype(jnp.bfloat16)
        d_query.append(
            scale
            * jnp.einsum("lhqk,lkhd->lqhd", d_scores_b, keys, preferred_element_type=jnp.float32)
        )
        d_keys = d_keys + scale * jnp.einsum(
            "lhqk,lqhd->lkhd", d_scores_b, piece, preferred_element_type=jnp.float32
        )
        d_values = d_values + jnp.einsum(
            "lhqk,lqhd->lkhd",
            weights.astype(jnp.bfloat16),
            grad_piece,
            preferred_element_type=jnp.float32,
        )
    return (jnp.concatenate(d_query, axis=1), d_keys, d_values)


def local(
    hidden,
    skipped,
    text,
    teacher,
    valid,
    steps,
    positions,
    w_skip,
    g_skip,
    b_skip,
    w_mod,
    g_one,
    b_one,
    w_qkv,
    g_query,
    g_key,
    w_out,
    g_three,
    b_three,
    w_cquery,
    w_ckv,
    g_cquery,
    g_ckey,
    w_cout,
    g_two,
    b_two,
    w_up,
    w_down,
):
    row = lax.axis_index("row")
    chip = lax.axis_index(LINE)
    core = lax.axis_index(CORE)
    width = hidden.shape[1]
    turn = chip * PIECE
    heads_own = HEADS // (2 * CHIPS)
    heads = 2 * heads_own
    shape_four = (1, HALF, heads, HD)

    def own_tokens(values):
        return turned(lax.dynamic_slice_in_dim(values, core * HALF, HALF, 0), turn)

    def other_tokens(values):
        return turned(lax.dynamic_slice_in_dim(values, (1 - core) * HALF, HALF, 0), turn)

    skip_two = jnp.transpose(w_skip.reshape(2, 2, width, D // 2), (3, 1, 0, 2)).reshape(
        D // 2, 4 * width
    )
    skip_kept, skip_received = halves_swapped(skip_two, 1, row)
    skip_own = in_row_order(skip_kept, skip_received, 0, row)
    skip_other = other_core(skip_own)
    skip_all = jnp.concatenate([skip_own, skip_other], axis=1)
    qkv_all = with_other_core(whole_columns(w_qkv, row, skip_received))
    mask_all = valid.astype(F32)
    if lax.axis_size(DP) == 1:
        count = jnp.sum(mask_all)
        out_all = with_other_core(whole_columns(w_out.T, row))
        cquery_all = with_other_core(whole_columns(w_cquery, row))
        cout_all = with_other_core(whole_columns(w_cout.T, row))
        ckv_all = with_other_core(whole_columns(w_ckv, row))
        up_all = with_other_core(whole_columns(w_up, row))
        down_all = with_other_core(whole_columns(w_down.T, row))
    else:
        ckv_block = block_of_rows(w_ckv, skip_received)
        ckv_rows = ckv_block.shape[0]
        ckv_block = jnp.pad(ckv_block, ((0, D // lax.axis_size(DP) - ckv_rows), (0, 0)))
        four_block = blocks_by_latents(
            [
                block_of_columns(w_out, skip_received),
                block_of_rows(w_cquery, skip_received),
                block_of_columns(w_cout, skip_received),
                ckv_block,
            ],
            row,
        )
        tally = jnp.sum(mask_all)
        parts = jnp.stack([jnp.floor(tally / 32.0), tally - 32.0 * jnp.floor(tally / 32.0)])
        four_block = lax.dynamic_update_slice(four_block, parts.astype(BF)[None], (0, width))
        four_own = lax.all_gather(four_block, DP, axis=0, tiled=True)
        parts = four_own.reshape(lax.axis_size(DP), -1, four_own.shape[1])[:, 0, width : width + 2]
        count = jnp.sum(parts.astype(F32) @ jnp.array([32.0, 1.0], F32))
        two_block = blocks_by_latents(
            [block_of_rows(w_up, four_own), block_of_columns(w_down, four_own)], row
        )
        two_own = lax.all_gather(two_block, DP, axis=0, tiled=True)
        four_other = other_core(four_own)

        def both(start, count):
            return jnp.concatenate(
                [four_own[:, start : start + count], four_other[:, start : start + count]], axis=1
            )

        step = width + (-width) % 128
        out_all = both(0, width)
        cquery_all = both(step, width)
        cout_all = both(2 * step, width)
        ckv_all = both(3 * step, 2 * width).reshape(lax.axis_size(DP), -1, 4 * width)
        ckv_all = ckv_all[:, :ckv_rows].reshape(-1, 4 * width)
        two_other = other_core(two_own)
        hidden_own = two_own.shape[1] // 2
        up_all = jnp.concatenate([two_own[:, :hidden_own], two_other[:, :hidden_own]], axis=1)
        down_all = jnp.concatenate([two_own[:, hidden_own:], two_other[:, hidden_own:]], axis=1)

    freq_here = w_mod.shape[0]
    mask_all = valid.astype(F32)
    emb = time_embed(steps).astype(BF)
    emb_here = lax.dynamic_slice_in_dim(emb, lax.axis_index(COL) * freq_here, freq_here, 1)
    shift_part = mult(emb_here, w_mod)
    vectors = jnp.concatenate(
        [jnp.stack([g_one, b_one, g_three, b_three, g_two, b_two]).reshape(-1), shift_part[0]]
    ) + settled(skip_received)
    gathered = copied_to_each(vectors, ROW_COL)
    gains = jnp.transpose(gathered[:, : 6 * width].reshape(8, 6, width), (1, 0, 2)).reshape(6, D)
    gain_one, offset_one, gain_three, offset_three, gain_two, offset_two = gains
    shift = jnp.sum(gathered[:, 6 * width :].reshape(2, 4, D // 2), axis=1).reshape(D)
    mask = lax.dynamic_slice_in_dim(mask_all, core * HALF + turn, PIECE, 0)

    cosine, sine = rope_tables(own_tokens(positions.T).T)
    prep = partial(qk_prep, cosine=cosine[:, None, :], sine=sine[:, None, :])

    joined = jnp.concatenate([hidden, skipped], axis=1)
    mine = own_tokens(joined)
    theirs = other_core(other_tokens(joined))
    pairs = jnp.concatenate([mine, theirs], axis=1).astype(F32)
    skip_vectors = jnp.stack([g_skip, b_skip]).reshape(2, 2 * width)
    both_vectors = jnp.concatenate([skip_vectors, other_core(skip_vectors)], axis=1)
    skip_sums = sum_over_chips(jnp.stack([jnp.sum(pairs, axis=1), jnp.sum(pairs * pairs, axis=1)]))
    skip_mean = skip_sums[0] / (2 * D)
    skip_rstd = lax.rsqrt(skip_sums[1] / (2 * D) - skip_mean * skip_mean + epsilon)
    skip_scaled = (pairs - skip_mean[:, None]) * skip_rstd[:, None]
    normed = (skip_scaled * both_vectors[0] + both_vectors[1]).astype(BF)
    stream = scatter_tokens(mult_right(normed, skip_all))

    normed_one, scaled_one, rstd_one = norm_forward(stream, gain_one, offset_one)
    text_sent = text[0] + settled(rstd_one).astype(BF)
    wide_text = jnp.transpose(copied_to_each(text_sent, ROW_COL), (1, 0, 2)).reshape(TXT, -1)
    wide_one = gather_tokens((normed_one + shift).astype(BF))
    packed = (mult(wide_one, qkv_all) + settled(wide_text)).reshape(HALF, heads, 3, HD)
    query_raw = packed[:, :, 0]
    key_raw = packed[:, :, 1]
    query = prep(query_raw, g_query).astype(BF).reshape(shape_four)
    keys_here = prep(key_raw, g_key).astype(BF)
    values_here = packed[:, :, 2].astype(BF)

    def swapped_heads(values):
        return jnp.concatenate([values[:, heads_own:], values[:, :heads_own]], axis=1)

    key_values = other_core(swapped_heads(jnp.concatenate([keys_here, values_here], axis=2)))
    keys = jnp.concatenate([keys_here, key_values[..., :HD]], axis=0)[None]
    values = jnp.concatenate([values_here, key_values[..., HD:]], axis=0)[None]
    mixed, self_totals = attend_forward(query, keys, values)
    mixed_here = mixed.reshape(HALF, heads * HD).astype(BF)
    stream_two = stream + scatter_tokens(mult_right(mixed_here, out_all))

    normed_three, scaled_three, rstd_three = norm_forward(stream_two, gain_three, offset_three)
    teacher_blocks = jnp.transpose(
        teacher.reshape(2, CHIPS, PIECE, width) + settled(rstd_three).astype(BF), (1, 0, 2, 3)
    ).reshape(2 * CHIPS, PIECE, width)
    teacher_here = jnp.transpose(
        lax.all_to_all(teacher_blocks, ROW_COL, 0, 0, tiled=True), (1, 0, 2)
    ).reshape(PIECE, D)
    wide_three = gather_tokens(normed_three.astype(BF))
    cquery_raw = mult(wide_three, cquery_all) + settled(teacher_here)
    cquery_raw = cquery_raw.reshape(HALF, heads, HD)
    cquery = prep(cquery_raw, g_cquery).astype(BF).reshape(shape_four)
    ckv = mult(wide_text, ckv_all).reshape(1, TXT, heads, 2, HD)
    ckey_raw = ckv[:, :, :, 0]
    ckeys = head_norm(ckey_raw, g_ckey).astype(BF)
    cvalues = ckv[:, :, :, 1].astype(BF)
    cmixed, cross_totals = attend_forward(cquery, ckeys, cvalues)
    cmixed_here = cmixed.reshape(HALF, heads * HD).astype(BF)
    stream_three = stream_two + scatter_tokens(mult_right(cmixed_here, cout_all))

    normed_two, scaled_two, rstd_two = norm_forward(stream_three, gain_two, offset_two)
    wide_two = gather_tokens(normed_two.astype(BF))
    upper = mult(wide_two, up_all)
    active, gelu_back = jax.vjp(gelu_tanh, upper)
    active_here = active.astype(BF)
    output_here = stream_three + scatter_tokens(mult_right(active_here, down_all))

    diff = output_here - teacher_here.astype(F32)
    sse_local = jnp.sum(mask[:, None] * diff * diff)
    factor = 32.0 * lax.axis_size(DP) / count
    grad_out = factor * mask[:, None] * diff
    output_blocks = jnp.transpose(
        output_here.astype(BF).reshape(PIECE, 2 * CHIPS, width), (1, 0, 2)
    )
    output_back = lax.all_to_all(output_blocks, ROW_COL, 0, 0, tiled=True)
    output = jnp.transpose(
        output_back.reshape(CHIPS, 2, PIECE, width), (1, 0, 2, 3)
    ).reshape(SEQ, width).astype(F32)

    wide_grad = gather_tokens(grad_out.astype(BF))
    d_upper = gelu_back(mult(wide_grad, down_all))[0].astype(BF)
    d_normed_two = scatter_tokens(mult_right(d_upper, up_all))
    two_pairs = [(wide_two, d_upper), (wide_grad, active_here)]
    two_theirs = other_core(products(two_pairs, 1))
    d_normed_two = d_normed_two + (settled(output_back) + settled(two_theirs))
    two_grads = products(two_pairs, 0, two_theirs)
    back_two, d_g_two, d_b_two = norm_backward(d_normed_two, scaled_two, rstd_two, gain_two)
    grad_three = grad_out + back_two

    wide_three_grad = gather_tokens(grad_three.astype(BF))
    d_cmixed = mult(wide_three_grad, cout_all) + settled(two_grads)
    d_cmixed = d_cmixed.astype(BF).reshape(shape_four)
    d_cquery, d_ckeys, d_cvalues = attend_backward(cquery, ckeys, cvalues, cross_totals, d_cmixed)
    unused, cquery_back = jax.vjp(prep, cquery_raw, g_cquery)
    d_cquery_raw, d_g_cquery = cquery_back(d_cquery.reshape(HALF, heads, HD))
    d_cquery_here = d_cquery_raw.reshape(HALF, heads * HD).astype(BF)
    d_normed_three = scatter_tokens(mult_right(d_cquery_here, cquery_all))
    unused, ckey_back = jax.vjp(head_norm, ckey_raw, g_ckey)
    d_ckey_raw, d_g_ckey = ckey_back(d_ckeys)
    d_ckv = jnp.stack([d_ckey_raw, d_cvalues], axis=3).reshape(TXT, heads * 2 * HD).astype(BF)
    back_three, d_g_three, d_b_three = norm_backward(
        d_normed_three, scaled_three, rstd_three, gain_three
    )
    grad_two = grad_three + back_three

    three_grads = weight_grads(
        [(wide_three, d_cquery_here), (wide_three_grad, cmixed_here), (wide_text, d_ckv)]
    )

    most_part = scattered_over_latents(jnp.concatenate([two_grads, three_grads], axis=1))

    wide_two_grad = gather_tokens(grad_two.astype(BF))
    d_mixed = mult(wide_two_grad, out_all) + settled(three_grads)
    d_mixed = d_mixed.astype(BF).reshape(shape_four)
    d_query, d_keys, d_values = attend_backward(query, keys, values, self_totals, d_mixed)
    d_both = jnp.concatenate([d_keys[0], d_values[0]], axis=2)
    d_both = d_both[:HALF] + other_core(swapped_heads(d_both[HALF:]).astype(BF)).astype(F32)
    unused, query_back = jax.vjp(prep, query_raw, g_query)
    d_query_raw, d_g_query = query_back(d_query.reshape(HALF, heads, HD))
    unused, key_back = jax.vjp(prep, key_raw, g_key)
    d_key_raw, d_g_key = key_back(d_both[..., :HD])
    d_packed = (
        jnp.stack([d_query_raw, d_key_raw, d_both[..., HD:]], axis=2)
        .reshape(HALF, heads * 3 * HD)
        .astype(BF)
    )
    d_inputs = scatter_tokens(mult_right(d_packed, qkv_all))
    back_one, d_g_one, d_b_one = norm_backward(d_inputs, scaled_one, rstd_one, gain_one)
    grad_one = grad_two + back_one

    d_shift_part = jnp.sum(d_inputs, axis=0)
    shared = jnp.concatenate([d_g_query, d_g_key, d_g_cquery, d_g_ckey, sse_local[None]])
    small = jnp.stack(
        [d_g_one, d_b_one, d_g_three, d_b_three, d_g_two, d_b_two, d_shift_part]
        + [jnp.pad(shared, (0, D - shared.shape[0]))]
    )
    piece = jnp.concatenate([grad_one.astype(BF), in_two(small)], axis=0)
    pieces = [piece] + [from_chip(piece, j) for j in range(1, CHIPS)]
    wide_one_grad = jnp.concatenate([p[:PIECE] for p in pieces], axis=0)
    small = sum(p[PIECE:].astype(F32) for p in pieces)
    small = small[:8] + small[8:]
    small = small + other_core(small)
    oq_grads = weight_grads([(wide_two_grad, mixed_here), (wide_one, d_packed)], grad_one)
    oq_part = summed_over_latents(oq_grads)
    d_joined = mult(wide_one_grad, skip_all) + settled(most_part)
    skip_sums = jnp.stack([jnp.sum(d_joined * skip_scaled, axis=0), jnp.sum(d_joined, axis=0)])
    skip_sums = skip_sums[:, : 2 * width] + other_core(skip_sums[:, 2 * width :])
    place = lax.axis_index(ROW_COL)
    shared_size = shared.shape[0]
    vector = jnp.concatenate(
        [
            lax.dynamic_slice_in_dim(small[:6], place * width, width, 1).reshape(-1),
            small[7, :shared_size],
            skip_sums.reshape(-1),
        ]
    )
    vector = jnp.pad(vector, (0, -vector.shape[0] % (D // 2))).reshape(-1, D // 2)
    vector_rows = vector.shape[0]
    latent_shift = lax.dynamic_slice_in_dim(small[6], row * (D // 2), D // 2, 0).astype(BF)
    d_w_mod = mult_left(emb_here, latent_shift[None])
    extra = jnp.concatenate([in_two(vector), d_w_mod.astype(BF)], axis=0).T
    extra = jnp.concatenate([extra, extra], axis=0)
    d_skip = weight_grads([(wide_one_grad, normed)])
    last_sent = jnp.concatenate([d_skip, extra], axis=1)
    n_up = w_up.shape[1] // 2
    most_halves = spread_over_latents(most_part, row)
    skip_part = summed_over_latents(
        last_sent, 2 * width, vector_rows
    )
    both_gains = both_vectors[0] + settled(d_skip) + settled(skip_sums)
    weighted = d_joined * both_gains
    back_sums = sum_over_chips(
        jnp.stack([jnp.sum(weighted, axis=1), jnp.sum(weighted * skip_scaled, axis=1)])
    ) / (2 * D)
    back_joined = skip_rstd[:, None] * (
        weighted - back_sums[0][:, None] - skip_scaled * back_sums[1][:, None]
    )
    back_mine = back_joined[:, : 2 * width]
    pinned = settled(skip_part)
    back_theirs = other_core(back_joined[:, 2 * width :] + pinned)
    unturn = (CHIPS - chip) % CHIPS * PIECE
    back_mine = turned(back_mine, unturn)
    back_theirs = turned(back_theirs, unturn)
    back_tokens = lax.dynamic_slice_in_dim(
        jnp.concatenate([back_mine, back_theirs, back_mine], axis=0), core * HALF, SEQ, 0
    )
    d_hidden = back_tokens[:, :width]
    d_skipped = back_tokens[:, width:]

    def columns(summed, start, count):
        return jnp.concatenate(
            [summed[0][:, start : start + count], summed[1][:, start : start + count]], axis=1
        ).astype(F32)

    d_w_up = columns(most_halves, 0, n_up)
    d_w_down = columns(most_halves, n_up, n_up).T
    d_w_cquery = columns(most_halves, 2 * n_up, width)
    d_w_cout = columns(most_halves, 2 * n_up + width, width).T
    d_w_ckv = columns(most_halves, 2 * n_up + 2 * width, 2 * width)
    count_blocks = max(lax.axis_size(DP) // 2, 1)
    d_w_ckv = d_w_ckv.reshape(count_blocks, -1, 4 * width)[:, : w_ckv.shape[0] // count_blocks]
    d_w_ckv = d_w_ckv.reshape(-1, 4 * width)
    last_grads = spread_over_latents(jnp.concatenate([oq_part, skip_part], axis=1), row, False)
    d_w_out = columns(last_grads, 0, width).T
    d_w_qkv = columns(last_grads, width, 3 * width)
    d_w_skip = columns(last_grads, 4 * width, 2 * width).reshape(D // 2, 2, 2, width)
    d_w_skip = jnp.transpose(d_w_skip, (2, 1, 3, 0)).reshape(2, 2 * width, D // 2)
    extra = last_grads[:, :, 6 * width :]
    extra = jnp.where(row == 0, extra[0], extra[1]).astype(F32).T
    vector = (extra[:vector_rows] + extra[vector_rows : 2 * vector_rows]).reshape(-1)
    d_w_mod = extra[2 * vector_rows :]
    d_g_one, d_b_one, d_g_three, d_b_three, d_g_two, d_b_two = vector[: 6 * width].reshape(6, width)
    shared = vector[6 * width : 6 * width + shared_size]
    d_g_query, d_g_key, d_g_cquery, d_g_ckey = shared[: 4 * HD].reshape(4, HD)
    loss = shared[4 * HD] / (count * D)
    skip_sums = vector[6 * width + shared_size : 10 * width + shared_size].reshape(2, 2, width)
    d_g_skip, d_b_skip = skip_sums
    return (
        output,
        d_hidden,
        d_skipped,
        d_w_skip,
        d_g_skip,
        d_b_skip,
        d_w_mod,
        d_g_one,
        d_b_one,
        d_w_qkv,
        d_g_query,
        d_g_key,
        d_w_out,
        d_g_three,
        d_b_three,
        d_w_cquery,
        d_w_ckv,
        d_g_cquery,
        d_g_ckey,
        d_w_cout,
        d_g_two,
        d_b_two,
        d_w_up,
        d_w_down,
        loss,
    )


def solution(mesh):
    side = math.isqrt(mesh.shape["dp"])
    split = Mesh(
        mesh.devices.reshape(side, side, mesh.shape["row"], 2, 2),
        ("dp_0", "dp_1", "row", "col_0", "col_1"),
    )
    in_specs = (
        P(DP, COL_ROW),
        P(DP, COL_ROW),
        P(DP, None, ROW_COL),
        P(DP, ROW_COL),
        P(DP),
        P(DP),
        P(None, DP),
        P(None, COL, "row"),
        P(None, COL_ROW),
        P(None, COL_ROW),
        P(COL, "row"),
        P(ROW_COL),
        P(ROW_COL),
        P("row", COL),
        P(),
        P(),
        P(COL, "row"),
        P(ROW_COL),
        P(ROW_COL),
        P("row", COL),
        P("row", COL),
        P(),
        P(),
        P(COL, "row"),
        P(ROW_COL),
        P(ROW_COL),
        P("row", COL),
        P(COL, "row"),
    )
    out_specs = (
        P(DP, ROW_COL),
        P(DP, COL_ROW),
        P(DP, COL_ROW),
        P(None, COL, "row"),
        P(None, COL_ROW),
        P(None, COL_ROW),
        P(COL, "row"),
        P(ROW_COL),
        P(ROW_COL),
        P("row", COL),
        P(),
        P(),
        P(COL, "row"),
        P(ROW_COL),
        P(ROW_COL),
        P("row", COL),
        P("row", COL),
        P(),
        P(),
        P(COL, "row"),
        P(ROW_COL),
        P(ROW_COL),
        P("row", COL),
        P(COL, "row"),
        P(),
    )
    return jax.shard_map(local, mesh=split, in_specs=in_specs, out_specs=out_specs, check_vma=False)
```

```python
from functools import partial
import math

import jax
import jax.numpy as jnp
from jax import lax
from jax.sharding import Mesh
from jax.sharding import PartitionSpec as P

D = 1408
HEADS = 16
HD = 88
FREQ = 256
TXT = 333
SEQ = 1024
LINE = ("row", "col_0")
CORE = "col_1"
COL = ("col_0", "col_1")
ROW_COL = ("row", "col_0", "col_1")
DP = ("dp_0", "dp_1")
ALL = ("dp_0", "dp_1", "row", "col_0", "col_1")
COL_ROW = ("col_0", "col_1", "row")
CHIPS = 4
HALF = SEQ // 2
PIECE = HALF // CHIPS
BF = jnp.bfloat16
F32 = jnp.float32


epsilon = 1e-06


def mult(left, right):
    return jnp.dot(left, right, preferred_element_type=jnp.float32)


def mult_left(left, right):
    return lax.dot_general(
        left, right, (((0,), (0,)), ((), ())), preferred_element_type=jnp.float32
    )


def mult_right(left, right):
    return lax.dot_general(
        left, right, (((1,), (1,)), ((), ())), preferred_element_type=jnp.float32
    )


def from_chip(value, ahead):
    return lax.ppermute(value, LINE, [(i, (i - ahead) % CHIPS) for i in range(CHIPS)])


def other_core(value):
    return lax.ppermute(value, CORE, [(0, 1), (1, 0)])


def other_row(value):
    return lax.ppermute(value, "row", [(0, 1), (1, 0)])


def gather_tokens(piece):
    return jnp.concatenate([piece] + [from_chip(piece, j) for j in range(1, CHIPS)], axis=0)


def scatter_tokens(partial_sums):
    total = partial_sums[:PIECE]
    for j in range(1, CHIPS):
        sent = partial_sums[j * PIECE : (j + 1) * PIECE].astype(BF)
        total = total + from_chip(sent, CHIPS - j).astype(F32)
    return total


def sum_over_chips(value):
    total = value
    for j in range(1, CHIPS):
        total = total + jnp.roll(from_chip(value, j), j * PIECE, axis=1)
    return total


def turned(value, start):
    twice = jnp.concatenate([value, value], axis=0)
    return lax.dynamic_slice_in_dim(twice, start, value.shape[0], 0)


def norm_forward(values, gain, offset):
    mean = jnp.mean(values, axis=1, keepdims=True)
    spread = jnp.mean(values * values, axis=1, keepdims=True) - mean * mean
    rstd = lax.rsqrt(spread + epsilon)
    scaled = (values - mean) * rstd
    return (scaled * gain + offset, scaled, rstd)


def norm_backward(grad, scaled, rstd, gain):
    weighted = grad * gain
    first = jnp.mean(weighted, axis=1, keepdims=True)
    second = jnp.mean(weighted * scaled, axis=1, keepdims=True)
    back = rstd * (weighted - first - scaled * second)
    return (back, jnp.sum(grad * scaled, axis=0), jnp.sum(grad, axis=0))


def halves_swapped(weight, dim, row, after=None):
    if after is not None:
        row = row + settled_index(after)
    kept = lax.dynamic_slice_in_dim(weight, row * (weight.shape[dim] // 2), weight.shape[dim] // 2, dim)
    sent = lax.dynamic_slice_in_dim(
        weight, (1 - row) * (weight.shape[dim] // 2), weight.shape[dim] // 2, dim
    )
    return (kept, other_row(sent))


def in_row_order(kept, received, dim, row):
    three = jnp.concatenate([received, kept, received], axis=dim)
    return lax.dynamic_slice_in_dim(
        three, (1 - row) * kept.shape[dim], 2 * kept.shape[dim], dim
    )


def settled(value):
    first = jnp.abs(value[(0,) * value.ndim].astype(F32))
    last = jnp.abs(value[(-1,) * value.ndim].astype(F32))
    return jnp.minimum(first + last, 0.0)


def settled_index(value):
    return settled(value).astype(jnp.int32)


def copied_to_each(value, axis):
    length = lax.axis_size(axis)
    return lax.all_to_all(
        jnp.broadcast_to(value[None], (length, *value.shape)), axis, 0, 0, tiled=True
    )


def in_two(value):
    high = lax.reduce_precision(value, exponent_bits=8, mantissa_bits=7)
    return jnp.concatenate([high.astype(BF), (value - high).astype(BF)], axis=0)


def with_other_core(own):
    return jnp.concatenate([own, other_core(own)], axis=1)


def whole_columns(weight, row, after=None):
    kept, received = halves_swapped(weight, 1, row, after)
    return in_row_order(kept, received, 0, row)


def padded(value):
    return jnp.pad(value, ((0, 0), (0, -value.shape[1] % 128)))


def blocks_by_latents(blocks, row):
    half = lax.axis_size(DP) // 2
    kept, sent = [], []
    for block in blocks:
        n = block.shape[1] // 2
        kept.append(padded(lax.dynamic_slice_in_dim(block, row * n, n, 1)))
        sent.append(padded(lax.dynamic_slice_in_dim(block, (1 - row) * n, n, 1)))
    kept = jnp.concatenate(kept, axis=1) if len(kept) > 1 else kept[0]
    sent = jnp.concatenate(sent, axis=1) if len(sent) > 1 else sent[0]
    return jnp.where(lax.axis_index(DP) // half == row, kept, other_row(sent))


def block_of_rows(weight, after):
    half = lax.axis_size(DP) // 2
    rows = weight.shape[0] // half
    place = lax.axis_index(DP) % half + settled_index(after)
    return lax.dynamic_slice_in_dim(weight, place * rows, rows, 0)


def block_of_columns(weight, after):
    half = lax.axis_size(DP) // 2
    columns = weight.shape[1] // half
    place = lax.axis_index(DP) % half + settled_index(after)
    return lax.dynamic_slice_in_dim(weight, place * columns, columns, 1).T


def products(pairs, part, added=None):
    outs = []
    start = 0
    for left, right in pairs:
        n = right.shape[1] // 2
        out = mult_left(left, right[:, part * n : (part + 1) * n])
        short = pairs[0][0].shape[1] - out.shape[0]
        if short:
            count = 2 * max(lax.axis_size(DP) // 2, 1)
            out = out.reshape(count, -1, n)
            out = jnp.pad(out, ((0, 0), (0, short // count), (0, 0))).reshape(-1, n)
        if added is not None:
            out = out + added[:, start : start + n].astype(F32)
        outs.append(out.astype(BF))
        start += n
    return jnp.concatenate(outs, axis=1) if len(outs) > 1 else outs[0]


def weight_grads(pairs, after=None):
    theirs = other_core(products(pairs, 1))
    if after is not None:
        theirs = theirs + settled(after).astype(BF)
    return products(pairs, 0, theirs)


def to_row_half(part):
    count = lax.axis_size(DP)
    half = count // 2
    pairs = []
    for i in range(count):
        for r in range(2):
            stays = i // half == r
            pairs.append((2 * i + r, 2 * i + r if stays else 2 * ((i + half) % count) + 1 - r))
    return lax.ppermute(part, DP + ("row",), pairs)


def scattered_over_latents(grads):
    count = lax.axis_size(DP)
    if count == 1:
        return grads
    blocks = grads.reshape(count, -1, grads.shape[1])
    return to_row_half(lax.psum_scatter(blocks, DP, scatter_dimension=0))


def row_halves(grads, row):
    kept, received = halves_swapped(grads, 0, row)
    first = row == 0
    return (jnp.where(first, kept, received), jnp.where(first, received, kept))


def summed_over_latents(grads, start=0, pairs_of=0, after=()):
    count = lax.axis_size(DP)
    if count == 1:
        return grads
    rows, n = grads.shape
    arrived = lax.all_to_all(grads.reshape(count, rows // count, n), DP, 0, 0, tiled=True)
    part = jnp.sum(arrived.astype(F32), axis=0)
    for value in after:
        part = part + settled(value)
    if pairs_of:
        exact = part[:, start : start + pairs_of] + part[:, start + pairs_of : start + 2 * pairs_of]
        rest = part[:, start + 2 * pairs_of :].astype(BF)
        part = jnp.concatenate([part[:, :start].astype(BF), in_two(exact.T).T, rest], axis=1)
    else:
        part = part.astype(BF)
    return to_row_half(part)


def spread_over_latents(part, row, gather=True):
    count = lax.axis_size(DP)
    if count == 1:
        return jnp.stack(row_halves(part, row))
    rows, n = part.shape
    if gather:
        spread = lax.all_gather(part, DP, axis=0)
    else:
        spread = copied_to_each(part, DP)
    return spread.reshape(2, count // 2 * rows, n)


def head_norm(values, gain):
    mean = jnp.mean(values, axis=-1, keepdims=True)
    spread = jnp.mean(values * values, axis=-1, keepdims=True) - mean * mean
    return (values - mean) * lax.rsqrt(spread + epsilon) * gain


def rotate(values):
    quarter = values.shape[-1] // 4
    return jnp.concatenate(
        [
            -values[..., quarter : 2 * quarter],
            values[..., :quarter],
            -values[..., 3 * quarter :],
            values[..., 2 * quarter : 3 * quarter],
        ],
        axis=-1,
    )


def qk_prep(raw, gain, cosine, sine):
    normal = head_norm(raw, gain)
    return normal * cosine + rotate(normal) * sine


def gelu_tanh(values):
    return jax.nn.gelu(values, approximate=True)


def rope_tables(positions):
    quarter = HD // 4
    freqs = jnp.exp(-math.log(10000.0) * jnp.arange(quarter, dtype=jnp.float32) / quarter)
    rows_angle = positions[0].astype(jnp.float32)[:, None] * freqs[None, :]
    cols_angle = positions[1].astype(jnp.float32)[:, None] * freqs[None, :]
    cosine = jnp.concatenate(
        [jnp.cos(rows_angle), jnp.cos(rows_angle), jnp.cos(cols_angle), jnp.cos(cols_angle)], axis=1
    )
    sine = jnp.concatenate(
        [jnp.sin(rows_angle), jnp.sin(rows_angle), jnp.sin(cols_angle), jnp.sin(cols_angle)], axis=1
    )
    return (cosine, sine)


def time_embed(steps):
    half = FREQ // 2
    freqs = jnp.exp(-math.log(10000.0) * jnp.arange(half, dtype=jnp.float32) / half)
    angles = steps.astype(jnp.float32)[:, None] * freqs[None, :]
    return jnp.concatenate([jnp.cos(angles), jnp.sin(angles)], axis=1)


def attend_forward(query, keys, values):
    scale = HD ** (-0.5)
    length = query.shape[1]
    block = min(512, length)
    outputs = []
    totals = []
    for start in range(0, length, block):
        piece = query[:, start : start + block]
        scores = scale * jnp.einsum(
            "lqhd,lkhd->lhqk", piece, keys, preferred_element_type=jnp.float32
        )
        top = jnp.max(scores, axis=-1, keepdims=True)
        expo = jnp.exp(scores - top)
        summed = jnp.sum(expo, axis=-1, keepdims=True)
        weights = expo / summed
        totals.append(top[..., 0] + jnp.log(summed[..., 0]))
        outputs.append(
            jnp.einsum(
                "lhqk,lkhd->lqhd",
                weights.astype(jnp.bfloat16),
                values,
                preferred_element_type=jnp.float32,
            )
        )
    return (jnp.concatenate(outputs, axis=1), jnp.concatenate(totals, axis=2))


def attend_backward(query, keys, values, totals, grad_out):
    scale = HD ** (-0.5)
    length = query.shape[1]
    block = min(512, length)
    d_keys = jnp.zeros(keys.shape, jnp.float32)
    d_values = jnp.zeros(values.shape, jnp.float32)
    d_query = []
    for start in range(0, length, block):
        piece = query[:, start : start + block]
        grad_piece = grad_out[:, start : start + block]
        scores = scale * jnp.einsum(
            "lqhd,lkhd->lhqk", piece, keys, preferred_element_type=jnp.float32
        )
        weights = jnp.exp(scores - totals[:, :, start : start + block, None])
        d_weights = jnp.einsum(
            "lqhd,lkhd->lhqk", grad_piece, values, preferred_element_type=jnp.float32
        )
        d_scores = weights * (d_weights - jnp.sum(d_weights * weights, axis=-1, keepdims=True))
        d_scores_b = d_scores.astype(jnp.bfloat16)
        d_query.append(
            scale
            * jnp.einsum("lhqk,lkhd->lqhd", d_scores_b, keys, preferred_element_type=jnp.float32)
        )
        d_keys = d_keys + scale * jnp.einsum(
            "lhqk,lqhd->lkhd", d_scores_b, piece, preferred_element_type=jnp.float32
        )
        d_values = d_values + jnp.einsum(
            "lhqk,lqhd->lkhd",
            weights.astype(jnp.bfloat16),
            grad_piece,
            preferred_element_type=jnp.float32,
        )
    return (jnp.concatenate(d_query, axis=1), d_keys, d_values)


def local(
    hidden,
    skipped,
    text,
    teacher,
    valid,
    steps,
    positions,
    w_skip,
    g_skip,
    b_skip,
    w_mod,
    g_one,
    b_one,
    w_qkv,
    g_query,
    g_key,
    w_out,
    g_three,
    b_three,
    w_cquery,
    w_ckv,
    g_cquery,
    g_ckey,
    w_cout,
    g_two,
    b_two,
    w_up,
    w_down,
):
    row = lax.axis_index("row")
    chip = lax.axis_index(LINE)
    core = lax.axis_index(CORE)
    width = hidden.shape[1]
    turn = chip * PIECE
    heads_own = HEADS // (2 * CHIPS)
    heads = 2 * heads_own
    shape_four = (1, HALF, heads, HD)

    def own_tokens(values):
        return turned(lax.dynamic_slice_in_dim(values, core * HALF, HALF, 0), turn)

    def other_tokens(values):
        return turned(lax.dynamic_slice_in_dim(values, (1 - core) * HALF, HALF, 0), turn)

    skip_two = jnp.transpose(w_skip.reshape(2, 2, width, D // 2), (3, 1, 0, 2)).reshape(
        D // 2, 4 * width
    )
    skip_kept, skip_received = halves_swapped(skip_two, 1, row)
    skip_own = in_row_order(skip_kept, skip_received, 0, row)
    skip_other = other_core(skip_own)
    skip_all = jnp.concatenate([skip_own, skip_other], axis=1)
    qkv_all = with_other_core(whole_columns(w_qkv, row, skip_received))
    mask_all = valid.astype(F32)
    if lax.axis_size(DP) == 1:
        count = jnp.sum(mask_all)
        out_all = with_other_core(whole_columns(w_out.T, row))
        cquery_all = with_other_core(whole_columns(w_cquery, row))
        cout_all = with_other_core(whole_columns(w_cout.T, row))
        ckv_all = with_other_core(whole_columns(w_ckv, row))
        up_all = with_other_core(whole_columns(w_up, row))
        down_all = with_other_core(whole_columns(w_down.T, row))
    else:
        ckv_block = block_of_rows(w_ckv, skip_received)
        ckv_rows = ckv_block.shape[0]
        ckv_block = jnp.pad(ckv_block, ((0, D // lax.axis_size(DP) - ckv_rows), (0, 0)))
        four_block = blocks_by_latents(
            [
                block_of_columns(w_out, skip_received),
                block_of_rows(w_cquery, skip_received),
                block_of_columns(w_cout, skip_received),
                ckv_block,
            ],
            row,
        )
        tally = jnp.sum(mask_all)
        parts = jnp.stack([jnp.floor(tally / 32.0), tally - 32.0 * jnp.floor(tally / 32.0)])
        four_block = lax.dynamic_update_slice(four_block, parts.astype(BF)[None], (0, width))
        four_own = lax.all_gather(four_block, DP, axis=0, tiled=True)
        parts = four_own.reshape(lax.axis_size(DP), -1, four_own.shape[1])[:, 0, width : width + 2]
        count = jnp.sum(parts.astype(F32) @ jnp.array([32.0, 1.0], F32))
        two_block = blocks_by_latents(
            [block_of_rows(w_up, four_own), block_of_columns(w_down, four_own)], row
        )
        two_own = lax.all_gather(two_block, DP, axis=0, tiled=True)
        four_other = other_core(four_own)

        def both(start, count):
            return jnp.concatenate(
                [four_own[:, start : start + count], four_other[:, start : start + count]], axis=1
            )

        step = width + (-width) % 128
        out_all = both(0, width)
        cquery_all = both(step, width)
        cout_all = both(2 * step, width)
        ckv_all = both(3 * step, 2 * width).reshape(lax.axis_size(DP), -1, 4 * width)
        ckv_all = ckv_all[:, :ckv_rows].reshape(-1, 4 * width)
        two_other = other_core(two_own)
        hidden_own = two_own.shape[1] // 2
        up_all = jnp.concatenate([two_own[:, :hidden_own], two_other[:, :hidden_own]], axis=1)
        down_all = jnp.concatenate([two_own[:, hidden_own:], two_other[:, hidden_own:]], axis=1)

    freq_here = w_mod.shape[0]
    mask_all = valid.astype(F32)
    emb = time_embed(steps).astype(BF)
    emb_here = lax.dynamic_slice_in_dim(emb, lax.axis_index(COL) * freq_here, freq_here, 1)
    shift_part = mult(emb_here, w_mod)
    vectors = jnp.concatenate(
        [jnp.stack([g_one, b_one, g_three, b_three, g_two, b_two]).reshape(-1), shift_part[0]]
    ) + settled(skip_received)
    gathered = copied_to_each(vectors, ROW_COL)
    gains = jnp.transpose(gathered[:, : 6 * width].reshape(8, 6, width), (1, 0, 2)).reshape(6, D)
    gain_one, offset_one, gain_three, offset_three, gain_two, offset_two = gains
    shift = jnp.sum(gathered[:, 6 * width :].reshape(2, 4, D // 2), axis=1).reshape(D)
    mask = lax.dynamic_slice_in_dim(mask_all, core * HALF + turn, PIECE, 0)

    cosine, sine = rope_tables(own_tokens(positions.T).T)
    prep = partial(qk_prep, cosine=cosine[:, None, :], sine=sine[:, None, :])

    joined = jnp.concatenate([hidden, skipped], axis=1)
    mine = own_tokens(joined)
    theirs = other_core(other_tokens(joined))
    pairs = jnp.concatenate([mine, theirs], axis=1).astype(F32)
    skip_vectors = jnp.stack([g_skip, b_skip]).reshape(2, 2 * width)
    both_vectors = jnp.concatenate([skip_vectors, other_core(skip_vectors)], axis=1)
    skip_sums = sum_over_chips(jnp.stack([jnp.sum(pairs, axis=1), jnp.sum(pairs * pairs, axis=1)]))
    skip_mean = skip_sums[0] / (2 * D)
    skip_rstd = lax.rsqrt(skip_sums[1] / (2 * D) - skip_mean * skip_mean + epsilon)
    skip_scaled = (pairs - skip_mean[:, None]) * skip_rstd[:, None]
    normed = (skip_scaled * both_vectors[0] + both_vectors[1]).astype(BF)
    stream = scatter_tokens(mult_right(normed, skip_all))

    normed_one, scaled_one, rstd_one = norm_forward(stream, gain_one, offset_one)
    text_sent = text[0] + settled(rstd_one).astype(BF)
    wide_text = jnp.transpose(copied_to_each(text_sent, ROW_COL), (1, 0, 2)).reshape(TXT, -1)
    wide_one = gather_tokens((normed_one + shift).astype(BF))
    packed = (mult(wide_one, qkv_all) + settled(wide_text)).reshape(HALF, heads, 3, HD)
    query_raw = packed[:, :, 0]
    key_raw = packed[:, :, 1]
    query = prep(query_raw, g_query).astype(BF).reshape(shape_four)
    keys_here = prep(key_raw, g_key).astype(BF)
    values_here = packed[:, :, 2].astype(BF)

    def swapped_heads(values):
        return jnp.concatenate([values[:, heads_own:], values[:, :heads_own]], axis=1)

    key_values = other_core(swapped_heads(jnp.concatenate([keys_here, values_here], axis=2)))
    keys = jnp.concatenate([keys_here, key_values[..., :HD]], axis=0)[None]
    values = jnp.concatenate([values_here, key_values[..., HD:]], axis=0)[None]
    mixed, self_totals = attend_forward(query, keys, values)
    mixed_here = mixed.reshape(HALF, heads * HD).astype(BF)
    stream_two = stream + scatter_tokens(mult_right(mixed_here, out_all))

    normed_three, scaled_three, rstd_three = norm_forward(stream_two, gain_three, offset_three)
    teacher_blocks = jnp.transpose(
        teacher.reshape(2, CHIPS, PIECE, width) + settled(rstd_three).astype(BF), (1, 0, 2, 3)
    ).reshape(2 * CHIPS, PIECE, width)
    teacher_here = jnp.transpose(
        lax.all_to_all(teacher_blocks, ROW_COL, 0, 0, tiled=True), (1, 0, 2)
    ).reshape(PIECE, D)
    wide_three = gather_tokens(normed_three.astype(BF))
    cquery_raw = mult(wide_three, cquery_all) + settled(teacher_here)
    cquery_raw = cquery_raw.reshape(HALF, heads, HD)
    cquery = prep(cquery_raw, g_cquery).astype(BF).reshape(shape_four)
    ckv = mult(wide_text, ckv_all).reshape(1, TXT, heads, 2, HD)
    ckey_raw = ckv[:, :, :, 0]
    ckeys = head_norm(ckey_raw, g_ckey).astype(BF)
    cvalues = ckv[:, :, :, 1].astype(BF)
    cmixed, cross_totals = attend_forward(cquery, ckeys, cvalues)
    cmixed_here = cmixed.reshape(HALF, heads * HD).astype(BF)
    stream_three = stream_two + scatter_tokens(mult_right(cmixed_here, cout_all))

    normed_two, scaled_two, rstd_two = norm_forward(stream_three, gain_two, offset_two)
    wide_two = gather_tokens(normed_two.astype(BF))
    upper = mult(wide_two, up_all)
    active, gelu_back = jax.vjp(gelu_tanh, upper)
    active_here = active.astype(BF)
    output_here = stream_three + scatter_tokens(mult_right(active_here, down_all))

    diff = output_here - teacher_here.astype(F32)
    sse_local = jnp.sum(mask[:, None] * diff * diff)
    factor = 32.0 * lax.axis_size(DP) / count
    grad_out = factor * mask[:, None] * diff
    output_blocks = jnp.transpose(
        output_here.astype(BF).reshape(PIECE, 2 * CHIPS, width), (1, 0, 2)
    )
    output_back = lax.all_to_all(output_blocks, ROW_COL, 0, 0, tiled=True)
    output = jnp.transpose(
        output_back.reshape(CHIPS, 2, PIECE, width), (1, 0, 2, 3)
    ).reshape(SEQ, width).astype(F32)

    wide_grad = gather_tokens(grad_out.astype(BF))
    d_upper = gelu_back(mult(wide_grad, down_all))[0].astype(BF)
    d_normed_two = scatter_tokens(mult_right(d_upper, up_all))
    two_pairs = [(wide_two, d_upper), (wide_grad, active_here)]
    two_theirs = other_core(products(two_pairs, 1))
    d_normed_two = d_normed_two + (settled(output_back) + settled(two_theirs))
    two_grads = products(two_pairs, 0, two_theirs)
    two_part = scattered_over_latents(two_grads)
    back_two, d_g_two, d_b_two = norm_backward(d_normed_two, scaled_two, rstd_two, gain_two)
    grad_three = grad_out + back_two

    wide_three_grad = gather_tokens(grad_three.astype(BF))
    d_cmixed = mult(wide_three_grad, cout_all) + settled(two_grads)
    d_cmixed = d_cmixed.astype(BF).reshape(shape_four)
    d_cquery, d_ckeys, d_cvalues = attend_backward(cquery, ckeys, cvalues, cross_totals, d_cmixed)
    unused, cquery_back = jax.vjp(prep, cquery_raw, g_cquery)
    d_cquery_raw, d_g_cquery = cquery_back(d_cquery.reshape(HALF, heads, HD))
    d_cquery_here = d_cquery_raw.reshape(HALF, heads * HD).astype(BF)
    d_normed_three = scatter_tokens(mult_right(d_cquery_here, cquery_all))
    unused, ckey_back = jax.vjp(head_norm, ckey_raw, g_ckey)
    d_ckey_raw, d_g_ckey = ckey_back(d_ckeys)
    d_ckv = jnp.stack([d_ckey_raw, d_cvalues], axis=3).reshape(TXT, heads * 2 * HD).astype(BF)
    back_three, d_g_three, d_b_three = norm_backward(
        d_normed_three, scaled_three, rstd_three, gain_three
    )
    grad_two = grad_three + back_three

    three_grads = weight_grads(
        [(wide_three, d_cquery_here), (wide_three_grad, cmixed_here), (wide_text, d_ckv)]
    )

    wide_two_grad = gather_tokens(grad_two.astype(BF))
    d_mixed = mult(wide_two_grad, out_all) + settled(three_grads)
    d_mixed = d_mixed.astype(BF).reshape(shape_four)
    d_query, d_keys, d_values = attend_backward(query, keys, values, self_totals, d_mixed)
    d_both = jnp.concatenate([d_keys[0], d_values[0]], axis=2)
    d_both = d_both[:HALF] + other_core(swapped_heads(d_both[HALF:]).astype(BF)).astype(F32)
    unused, query_back = jax.vjp(prep, query_raw, g_query)
    d_query_raw, d_g_query = query_back(d_query.reshape(HALF, heads, HD))
    unused, key_back = jax.vjp(prep, key_raw, g_key)
    d_key_raw, d_g_key = key_back(d_both[..., :HD])
    d_packed = (
        jnp.stack([d_query_raw, d_key_raw, d_both[..., HD:] + settled(two_part)], axis=2)
        .reshape(HALF, heads * 3 * HD)
        .astype(BF)
    )
    d_inputs = scatter_tokens(mult_right(d_packed, qkv_all))
    back_one, d_g_one, d_b_one = norm_backward(d_inputs, scaled_one, rstd_one, gain_one)
    grad_one = grad_two + back_one

    d_shift_part = jnp.sum(d_inputs, axis=0)
    shared = jnp.concatenate([d_g_query, d_g_key, d_g_cquery, d_g_ckey, sse_local[None]])
    small = jnp.stack(
        [d_g_one, d_b_one, d_g_three, d_b_three, d_g_two, d_b_two, d_shift_part]
        + [jnp.pad(shared, (0, D - shared.shape[0]))]
    )
    piece = jnp.concatenate([grad_one.astype(BF), in_two(small)], axis=0)
    pieces = [piece] + [from_chip(piece, j) for j in range(1, CHIPS)]
    wide_one_grad = jnp.concatenate([p[:PIECE] for p in pieces], axis=0)
    small = sum(p[PIECE:].astype(F32) for p in pieces)
    small = small[:8] + small[8:]
    small = small + other_core(small)
    oq_grads = weight_grads([(wide_two_grad, mixed_here), (wide_one, d_packed)], grad_one)
    five_part = summed_over_latents(jnp.concatenate([oq_grads, three_grads], axis=1))
    d_joined = mult(wide_one_grad, skip_all)
    skip_sums = jnp.stack([jnp.sum(d_joined * skip_scaled, axis=0), jnp.sum(d_joined, axis=0)])
    skip_sums = skip_sums[:, : 2 * width] + other_core(skip_sums[:, 2 * width :])
    place = lax.axis_index(ROW_COL)
    shared_size = shared.shape[0]
    vector = jnp.concatenate(
        [
            lax.dynamic_slice_in_dim(small[:6], place * width, width, 1).reshape(-1),
            small[7, :shared_size],
            skip_sums.reshape(-1),
        ]
    )
    vector = jnp.pad(vector, (0, -vector.shape[0] % (D // 2))).reshape(-1, D // 2)
    vector_rows = vector.shape[0]
    latent_shift = lax.dynamic_slice_in_dim(small[6], row * (D // 2), D // 2, 0).astype(BF)
    d_w_mod = mult_left(emb_here, latent_shift[None])
    extra = jnp.concatenate([in_two(vector), d_w_mod.astype(BF)], axis=0).T
    extra = jnp.concatenate([extra, extra], axis=0)
    d_skip = weight_grads([(wide_one_grad, normed)])
    last_sent = jnp.concatenate([d_skip, extra], axis=1)
    n_up = w_up.shape[1] // 2
    two_halves = spread_over_latents(two_part, row)
    skip_part = summed_over_latents(
        last_sent, 2 * width, vector_rows
    )
    both_gains = both_vectors[0] + settled(d_skip) + settled(skip_sums)
    weighted = d_joined * both_gains
    back_sums = sum_over_chips(
        jnp.stack([jnp.sum(weighted, axis=1), jnp.sum(weighted * skip_scaled, axis=1)])
    ) / (2 * D)
    back_joined = skip_rstd[:, None] * (
        weighted - back_sums[0][:, None] - skip_scaled * back_sums[1][:, None]
    )
    back_mine = back_joined[:, : 2 * width]
    pinned = settled(skip_part) + settled(two_halves)
    back_theirs = other_core(back_joined[:, 2 * width :] + pinned)
    unturn = (CHIPS - chip) % CHIPS * PIECE
    back_mine = turned(back_mine, unturn)
    back_theirs = turned(back_theirs, unturn)
    back_tokens = lax.dynamic_slice_in_dim(
        jnp.concatenate([back_mine, back_theirs, back_mine], axis=0), core * HALF, SEQ, 0
    )
    d_hidden = back_tokens[:, :width]
    d_skipped = back_tokens[:, width:]

    def columns(summed, start, count):
        return jnp.concatenate(
            [summed[0][:, start : start + count], summed[1][:, start : start + count]], axis=1
        ).astype(F32)

    d_w_up = columns(two_halves, 0, n_up)
    d_w_down = columns(two_halves, n_up, n_up).T
    five_grads = spread_over_latents(five_part, row)
    d_w_cquery = columns(five_grads, 4 * width, width)
    d_w_cout = columns(five_grads, 5 * width, width).T
    d_w_ckv = columns(five_grads, 6 * width, 2 * width)
    count_blocks = max(lax.axis_size(DP) // 2, 1)
    d_w_ckv = d_w_ckv.reshape(count_blocks, -1, 4 * width)[:, : w_ckv.shape[0] // count_blocks]
    d_w_ckv = d_w_ckv.reshape(-1, 4 * width)
    last_grads = spread_over_latents(skip_part, row, False)
    d_w_out = columns(five_grads, 0, width).T
    d_w_qkv = columns(five_grads, width, 3 * width)
    d_w_skip = columns(last_grads, 0, 2 * width).reshape(D // 2, 2, 2, width)
    d_w_skip = jnp.transpose(d_w_skip, (2, 1, 3, 0)).reshape(2, 2 * width, D // 2)
    extra = last_grads[:, :, 2 * width :]
    extra = jnp.where(row == 0, extra[0], extra[1]).astype(F32).T
    vector = (extra[:vector_rows] + extra[vector_rows : 2 * vector_rows]).reshape(-1)
    d_w_mod = extra[2 * vector_rows :]
    d_g_one, d_b_one, d_g_three, d_b_three, d_g_two, d_b_two = vector[: 6 * width].reshape(6, width)
    shared = vector[6 * width : 6 * width + shared_size]
    d_g_query, d_g_key, d_g_cquery, d_g_ckey = shared[: 4 * HD].reshape(4, HD)
    loss = shared[4 * HD] / (count * D)
    skip_sums = vector[6 * width + shared_size : 10 * width + shared_size].reshape(2, 2, width)
    d_g_skip, d_b_skip = skip_sums
    return (
        output,
        d_hidden,
        d_skipped,
        d_w_skip,
        d_g_skip,
        d_b_skip,
        d_w_mod,
        d_g_one,
        d_b_one,
        d_w_qkv,
        d_g_query,
        d_g_key,
        d_w_out,
        d_g_three,
        d_b_three,
        d_w_cquery,
        d_w_ckv,
        d_g_cquery,
        d_g_ckey,
        d_w_cout,
        d_g_two,
        d_b_two,
        d_w_up,
        d_w_down,
        loss,
    )


def solution(mesh):
    side = math.isqrt(mesh.shape["dp"])
    split = Mesh(
        mesh.devices.reshape(side, side, mesh.shape["row"], 2, 2),
        ("dp_0", "dp_1", "row", "col_0", "col_1"),
    )
    in_specs = (
        P(DP, COL_ROW),
        P(DP, COL_ROW),
        P(DP, None, ROW_COL),
        P(DP, ROW_COL),
        P(DP),
        P(DP),
        P(None, DP),
        P(None, COL, "row"),
        P(None, COL_ROW),
        P(None, COL_ROW),
        P(COL, "row"),
        P(ROW_COL),
        P(ROW_COL),
        P("row", COL),
        P(),
        P(),
        P(COL, "row"),
        P(ROW_COL),
        P(ROW_COL),
        P("row", COL),
        P("row", COL),
        P(),
        P(),
        P(COL, "row"),
        P(ROW_COL),
        P(ROW_COL),
        P("row", COL),
        P(COL, "row"),
    )
    out_specs = (
        P(DP, ROW_COL),
        P(DP, COL_ROW),
        P(DP, COL_ROW),
        P(None, COL, "row"),
        P(None, COL_ROW),
        P(None, COL_ROW),
        P(COL, "row"),
        P(ROW_COL),
        P(ROW_COL),
        P("row", COL),
        P(),
        P(),
        P(COL, "row"),
        P(ROW_COL),
        P(ROW_COL),
        P("row", COL),
        P("row", COL),
        P(),
        P(),
        P(COL, "row"),
        P(ROW_COL),
        P(ROW_COL),
        P("row", COL),
        P(COL, "row"),
        P(),
    )
    return jax.shard_map(local, mesh=split, in_specs=in_specs, out_specs=out_specs, check_vma=False)
```
